32 devices in a mesh: seq: 2 (over x), tm: 16 (over z, y, core).
Axes of the slice: x: 2, y: 2, z: 4, core: 2. Of those that a mesh axis runs over, the one named last changes fastest.
Arguments:
- layer_input: bfloat16 [2, 4096, 1024], P('seq', 'tm'), may hold values from -6 to 6
- routes: int32 [2, 4096, 8, 2], P('seq', 'tm'), may hold values from 0 to 4, all different within a row
- memory_lengths: int32 [2, 16], P('seq', 'tm'), may hold values from 0 to 256, as said below
- norm_gains: bfloat16 [2, 1024], replicated, may hold values from 0.5 to 1.5
- w_query: bfloat16 [1024, 448], replicated, may hold values from -0.25 to 0.25
- w_key: bfloat16 [1024, 448], replicated, may hold values from -0.25 to 0.25
- w_value: bfloat16 [1024, 2240], replicated, may hold values from -0.1875 to 0.1875
- w_router: bfloat16 [1024, 40], replicated, may hold values from -0.125 to 0.125
- w_output: bfloat16 [2240, 1024], replicated, may hold values from -3.5 to 3.5
- w_up: bfloat16 [1024, 4096], replicated, may hold values from -0.1875 to 0.1875
- w_down: bfloat16 [4096, 1024], replicated, may hold values from -0.09375 to 0.09375
- output_cot: bfloat16 [2, 4096, 1024], P('seq', 'tm'), may hold values from -6 to 6
Outputs:
- layer_output: bfloat16 [2, 4096, 1024], P('seq', 'tm')
- input_grad: float32 [2, 4096, 1024], P('seq', 'tm')
- gains_grad: float32 [2, 1024], P(None, ('seq', 'tm'))
- query_weight_grad: float32 [1024, 448], P(('seq', 'tm'))
- key_weight_grad: float32 [1024, 448], P(('seq', 'tm'))
- value_weight_grad: float32 [1024, 2240], P(('seq', 'tm'))
- router_weight_grad: float32 [1024, 40], P(('seq', 'tm'))
- output_weight_grad: float32 [2240, 1024], P(None, ('seq', 'tm'))
- up_weight_grad: float32 [1024, 4096], P(('seq', 'tm'))
- down_weight_grad: float32 [4096, 1024], P(None, ('seq', 'tm'))
The draws below stay inside these ranges and needn't reach their ends.
Inputs may be any that keep to these rules, and one draw needn't show every extreme that they name: `routes`: each token names two different experts for each head's value branch and output branch. `memory_lengths`: the first segment of each sequence has 0; each sequence has a segment with exactly 256; all other segments have 1 to 256.
All inputs are finite; a program needn't handle non-finite values.
Results may differ from the reference program's by a relative error of at most 0.012.
The reference program's roundings to bfloat16 on the way count: a program that leaves them out, or rounds other values in their place, can miss the bound.
Values may be sent and summed in bfloat16 or wider, within the bound.
A program may use at most 256 MiB of HBM per device.

```python
import jax
import jax.numpy as jnp
from jax import lax

D = 1024
H = 4
DH = 112
E = 5
FF = 4096
SEG = 256
SEQUENCES = 2
SEGMENTS = 16
SEQ_LEN = 4096


def draw_memory_lengths(key, part):
    key = jax.random.fold_in(key, 7)
    first_key, second_key = jax.random.split(key)
    lengths = jax.random.randint(first_key, (SEQUENCES, SEGMENTS), 1, SEG + 1)
    chosen = jax.random.randint(second_key, (SEQUENCES, 1), 1, SEGMENTS)
    position = jnp.arange(SEGMENTS)[None, :]
    lengths = jnp.where(position == chosen, SEG, lengths)
    lengths = jnp.where(position == 0, 0, lengths)
    return lengths.astype(jnp.int32)


def with_spikes(array, own_key, source, target, parts, factor):
    owner, partner = [(jnp.arange(array.shape[axis_at]) // (array.shape[axis_at] // parts)).reshape([-1 if axis == axis_at else 1 for axis in range(array.ndim)]) for axis_at in (source, target)]
    chosen = jax.random.permutation(own_key, parts)[partner]
    strong = (owner == chosen) | (owner == (partner + parts // 2) % parts)
    return jnp.where(strong, factor * array, array)


def block_levels(key, dims, cuts, smallest, largest):
    def one(dim, parts):
        heights = jax.random.uniform(jax.random.fold_in(jax.random.fold_in(key, 6), dim), (parts,), jnp.float32, smallest / len(cuts), largest / len(cuts))
        return jnp.repeat(jnp.exp(heights), dims[dim] // parts).reshape((-1,) + (1,) * (len(dims) - dim - 1))

    gain = one(*cuts[0])
    for cut in cuts[1:]:
        gain = gain * one(*cut)
    return gain


def different_ones(rng, rows, number_of, top, lift):
    order = jax.random.permutation(jax.random.fold_in(rng, 1), number_of)
    favour = order
    for power in range(3):
        favour = favour * favour // number_of
    favour = favour * lift // number_of
    lots = jax.random.randint(jax.random.fold_in(rng, 2), (rows, number_of), 0, 4096) + favour
    sure = jax.random.permutation(jax.random.fold_in(rng, 3), rows)[jnp.arange(number_of) % rows]
    lots = jnp.where(jnp.arange(rows)[:, None] == sure[None, :], 1 << 14, lots)
    priority = lots * number_of + jnp.arange(number_of)
    return lax.top_k(priority.astype(jnp.int32), top)[1].astype(jnp.int32)


def centred(rng, extent, scale, most, pieces=(), kind=jnp.bfloat16):
    entries = scale * jax.random.normal(rng, extent, jnp.float32)
    if pieces:
        entries = entries * block_levels(rng, extent, pieces, -0.22, 0.18)
    return jnp.clip(entries, -most, most).astype(kind)


def noise_with(rng, extent, width, most, shards, heavy, kind=jnp.bfloat16):
    drawn = width * jax.random.normal(rng, extent, jnp.float32)
    if shards:
        drawn = drawn * block_levels(rng, extent, shards, -0.22, 0.18)
    return jnp.clip(with_spikes(drawn, jax.random.fold_in(rng, 3), *heavy), -most, most).astype(kind)


def setup_inputs(seed: int = 0) -> dict:
    key_list = jax.random.split(jax.random.key(seed), 13)
    return {
        "layer_input": noise_with(key_list[0], (SEQUENCES, SEQ_LEN, D), 1.0, 6.0, ((0, 2), (1, 16)), (1, 2, 16, 2.0)),
        "routes": different_ones(key_list[1], SEQUENCES * SEQ_LEN * (2 * H), E, 2, 0).reshape((SEQUENCES, SEQ_LEN, 2 * H, 2)),
        "memory_lengths": draw_memory_lengths(jax.random.fold_in(key_list[12], 71), 0),
        "norm_gains": jnp.clip(1.0 + 0.1 * jax.random.normal(key_list[3], (2, D), jnp.float32), 0.5, 1.5).astype(jnp.bfloat16),
        "w_query": centred(key_list[4], (D, H * DH), (D // 2) ** -0.5, 0.25),
        "w_key": centred(key_list[5], (D, H * DH), (D // 2) ** -0.5, 0.25),
        "w_value": centred(key_list[6], (D, H * E * DH), D ** -0.5, 0.1875),
        "w_router": centred(key_list[7], (D, 2 * H * E), (2 * D) ** -0.5, 0.125),
        "w_output": centred(key_list[8], (H * E * DH, D), (max(1, 2 * H * DH // SEG)) ** -0.5, 3.5),
        "w_up": centred(key_list[9], (D, FF), D ** -0.5, 0.1875),
        "w_down": centred(key_list[10], (FF, D), FF ** -0.5, 0.09375),
        "output_cot": noise_with(key_list[11], (SEQUENCES, SEQ_LEN, D), 1.0, 6.0, ((0, 2), (1, 16)), (1, 2, 16, 2.0)),
    }


@jax.custom_vjp
def low(v):
    return lax.optimization_barrier(v.astype(jnp.bfloat16)).astype(jnp.float32)

@jax.custom_vjp
def low_back(v):
    return v

def low_keep(v):
    return (low(v), None)

def low_pass(kept, grad):
    return (grad,)

def back_keep(v):
    return (v, None)

def back_low(kept, grad):
    return (low(grad),)
low.defvjp(low_keep, low_pass)
low_back.defvjp(back_keep, back_low)
epsilon = 1e-05
highest = lax.Precision.HIGHEST

def normalize(values, gain_vec):
    centre = values - lax.optimization_barrier(jnp.mean(values, axis=-1, keepdims=True))
    spread = lax.optimization_barrier(jnp.mean(centre * centre, axis=-1, keepdims=True))
    return centre * lax.rsqrt(spread + epsilon) * gain_vec

def matmul(left_op, right_op):
    return jnp.dot(left_op, right_op, precision=highest, preferred_element_type=jnp.float32)

def one_hot_routes(route_ids):
    return lax.optimization_barrier(jnp.sum((route_ids[..., None] == jnp.arange(E, dtype=jnp.int32)).astype(jnp.float32), axis=-2))

def gate_values(normed, route_ids, w_router):
    logits = low_back(matmul(normed, w_router)).reshape(SEG, 2 * H, E)
    return jax.nn.sigmoid(logits) * one_hot_routes(route_ids)

def expert_values(normed, gate_vals, w_value):
    projected = low_back(matmul(normed, w_value)).reshape(SEG, H, E, DH)
    return low_back(low(lax.optimization_barrier(jnp.sum(gate_vals[:, :H, :, None] * projected, axis=2))))

def segment(params, own_rows, memory_rows, own_routes, memory_routes, memory_length):
    norm_gains, w_query, w_key, w_value, w_router, w_output, w_up, w_down = params
    own_normed = low(normalize(own_rows, norm_gains[0]))
    mem_normed = low(normalize(memory_rows, norm_gains[0]))
    queries = low_back(low(matmul(own_normed, w_query))).reshape(SEG, H, DH)
    own_keys = low_back(low(matmul(own_normed, w_key))).reshape(SEG, H, DH)
    mem_keys = low_back(low(matmul(mem_normed, w_key))).reshape(SEG, H, DH)
    own_gates = gate_values(own_normed, own_routes, w_router)
    mem_gates = gate_values(mem_normed, memory_routes, w_router)
    own_vals = expert_values(own_normed, own_gates, w_value)
    mem_vals = expert_values(mem_normed, mem_gates, w_value)
    key_rows = jnp.concatenate([mem_keys, own_keys], axis=0)
    value_rows = jnp.concatenate([mem_vals, own_vals], axis=0)
    scores = low_back(jnp.einsum('qhd,khd->hqk', queries, key_rows, precision=highest) * DH ** (-0.5))
    query_pos = jnp.arange(SEG, dtype=jnp.int32)[:, None]
    key_pos = jnp.arange(2 * SEG, dtype=jnp.int32)[None, :]
    allowed = jnp.where(key_pos < SEG, key_pos >= SEG - memory_length, key_pos - SEG <= query_pos)
    weights = jax.nn.softmax(jnp.where(allowed[None], scores, -1e+30), axis=-1)
    attended = low_back(low(jnp.einsum('hqk,khd->qhd', low(weights), value_rows, precision=highest)))
    mixed_in = low(attended[:, :, None, :] * own_gates[:, H:, :, None]).reshape(SEG, H * E * DH)
    branch = low_back(matmul(mixed_in, w_output))
    middle = own_rows + branch
    hidden_normed = low(normalize(middle, norm_gains[1]))
    pre_act = low_back(matmul(hidden_normed, w_up))
    activated = low(jax.nn.gelu(pre_act, approximate=False))
    return middle + low_back(matmul(activated, w_down))

def reference(layer_input, routes, memory_lengths, norm_gains, w_query, w_key, w_value, w_router, w_output, w_up, w_down, output_cot):
    params = tuple((tensor.astype(jnp.float32) for tensor in (norm_gains, w_query, w_key, w_value, w_router, w_output, w_up, w_down)))
    seq_rows = layer_input.astype(jnp.float32).reshape(SEQUENCES, SEGMENTS, SEG, D)
    earlier = jnp.concatenate([jnp.zeros((SEQUENCES, 1, SEG, D), jnp.float32), seq_rows[:, :-1]], axis=1)
    earlier = earlier.reshape(SEQUENCES * SEGMENTS, SEG, D)
    route_segs = routes.reshape(SEQUENCES, SEGMENTS, SEG, 2 * H, 2)
    route_prev = jnp.concatenate([jnp.zeros((SEQUENCES, 1, SEG, 2 * H, 2), jnp.int32), route_segs[:, :-1]], axis=1)
    route_prev = route_prev.reshape(SEQUENCES * SEGMENTS, SEG, 2 * H, 2)
    own_routes = route_segs.reshape(SEQUENCES * SEGMENTS, SEG, 2 * H, 2)
    lengths = memory_lengths.reshape(SEQUENCES * SEGMENTS)
    own_segs = seq_rows.reshape(SEQUENCES * SEGMENTS, SEG, D)

    def forward(weight_set, rows_all):

        def one_segment(segment_items):
            return segment(weight_set, segment_items[0], segment_items[1], segment_items[2], segment_items[3], segment_items[4])
        return lax.map(jax.checkpoint(one_segment), (rows_all, earlier, own_routes, route_prev, lengths))
    result, pullback = jax.vjp(forward, params, own_segs)
    cotangent = output_cot.astype(jnp.float32).reshape(SEQUENCES * SEGMENTS, SEG, D)
    weight_grads, input_grad = pullback(cotangent)
    layer_output = result.reshape(SEQUENCES, SEQ_LEN, D).astype(jnp.bfloat16)
    input_grad = input_grad.reshape(SEQUENCES, SEQ_LEN, D)
    return (layer_output, input_grad, weight_grads[0], weight_grads[1], weight_grads[2], weight_grads[3], weight_grads[4], weight_grads[5], weight_grads[6], weight_grads[7])
```

```python
import functools

import jax
import jax.numpy as jnp
from jax import lax
from jax.experimental import pallas as pl
from jax.experimental.pallas import tpu as pltpu
from jax.sharding import PartitionSpec as P

H = 4
DH = 112
E = 5


epsilon = 1e-05


def passed_along(value, axis, steps):
    count = lax.axis_size(axis)
    initial, last = (max(0, -steps), min(count, count - steps))
    return lax.ppermute(value, axis, [(source, source + steps) for source in range(initial, last)])


def normalize(values, gain_vec):
    centre = values - jnp.mean(values, axis=-1, keepdims=True)
    spread = jnp.mean(centre * centre, axis=-1, keepdims=True)
    return centre * lax.rsqrt(spread + epsilon) * gain_vec


def exact_gelu(arg_in):
    return jax.nn.gelu(arg_in, approximate=False)


def matmul(left_op, right_op):
    return jnp.dot(left_op, right_op, preferred_element_type=jnp.float32)


def times_tr(left_op, right_op):
    return lax.dot_general(
        left_op, right_op, (((1,), (1,)), ((), ())), preferred_element_type=jnp.float32
    )


def tr_times(left_op, right_op):
    return lax.dot_general(
        left_op, right_op, (((0,), (0,)), ((), ())), preferred_element_type=jnp.float32
    )


def one_hot_routes(route_ids):
    return jnp.sum(
        (route_ids[..., None] == jnp.arange(E, dtype=jnp.int32)).astype(jnp.float32), axis=-2
    )


def attention_mask(memory_length, seg_len):
    query_pos = jnp.arange(seg_len, dtype=jnp.int32)[:, None]
    key_pos = jnp.arange(2 * seg_len, dtype=jnp.int32)[None, :]
    return jnp.where(
        key_pos < seg_len, key_pos >= seg_len - memory_length, key_pos - seg_len <= query_pos
    )


MESH_ID = pl.DeviceIdType.MESH
NS = 12
TILE = 128
AB_T = 7
C_T = 2
PER = AB_T + C_T
AB_W = AB_T * TILE
C_W = C_T * TILE
FLAT = NS * PER * TILE


def place():
    s = lax.axis_index("seq")
    t = lax.axis_index("tm")
    return s, t, t // 4, (t // 2) % 2, t % 2


def store_tile(p_ab, p_c, tile, value):
    piece = tile // PER
    slot = tile % PER

    def first():
        cols = pl.ds(pl.multiple_of(slot * TILE, TILE), TILE)
        p_ab[piece, :, :, :, :, :, cols] = value.reshape(2, 4, 2, 2, 16, TILE).astype(jnp.bfloat16)

    def second():
        cols = pl.ds(pl.multiple_of((slot - AB_T) * TILE, TILE), TILE)
        p_c[piece, :, :, :, :, cols] = value.reshape(2, 4, 2, 32, TILE).astype(jnp.bfloat16)

    if isinstance(tile, int):
        first() if slot < AB_T else second()
    else:
        pl.when(slot < AB_T)(first)
        pl.when(slot >= AB_T)(second)


class Exchange:
    def __init__(self, p_ab, p_c, bufs, sems, out):
        self.p_ab, self.p_c, self.out = p_ab, p_c, out
        (self.xa, self.yb, self.ya, self.xb, self.zu, self.zd, self.zuc, self.zdc, self.xc, self.yc) = bufs
        self.ssem, self.rsem = sems
        self.s, self.t, self.z, self.y, self.c = place()
        s, t = self.s, self.t
        self.to_x = {"seq": 1 - s, "tm": t}
        self.to_y = {"seq": s, "tm": t + 2 - 4 * self.y}
        self.to_up = {"seq": s, "tm": t + 4}
        self.to_down = {"seq": s, "tm": t - 4}

    def copy(self, kind, piece, src, dst, dev):
        return pltpu.make_async_remote_copy(
            src_ref=src, dst_ref=dst, send_sem=self.ssem.at[kind, piece],
            recv_sem=self.rsem.at[kind, piece], device_id=dev, device_id_type=MESH_ID)

    def c_xa(self, p):
        return self.copy(0, p, self.p_ab.at[p, 1 - self.s, :, :, 0], self.xa.at[p], self.to_x)

    def c_yb(self, p):
        return self.copy(1, p, self.p_ab.at[p, :, :, 1 - self.y, 1], self.yb.at[p], self.to_y)

    def c_ya(self, p):
        return self.copy(2, p, self.p_ab.at[p, self.s, :, 1 - self.y, 0], self.ya.at[p], self.to_y)

    def c_xb(self, p):
        return self.copy(3, p, self.p_ab.at[p, 1 - self.s, :, self.y, 1], self.xb.at[p], self.to_x)

    def c_xc(self, p):
        return self.copy(4, p, self.p_c.at[p, 1 - self.s, self.z], self.xc.at[p], self.to_x)

    def c_yc(self, p):
        return self.copy(5, p, self.p_c.at[p, self.s, self.z, 1 - self.y], self.yc.at[p], self.to_y)

    def c_up(self, p, z):
        return self.copy(6, p, self.p_ab.at[p, self.s, z + 1:4, self.y], self.zu.at[p, z:3], self.to_up)

    def c_down(self, p, z):
        return self.copy(7, p, self.p_ab.at[p, self.s, 0:z, self.y], self.zd.at[p, 0:z], self.to_down)

    def c_upc(self, p, z):
        return self.copy(8, p, self.p_c.at[p, :, z + 1:4], self.zuc.at[p, :, z:3], self.to_up)

    def c_downc(self, p, z):
        return self.copy(9, p, self.p_c.at[p, :, 0:z], self.zdc.at[p, :, 0:z], self.to_down)

    def z_step(self, p, k, is_c):
        up, down = (self.c_upc, self.c_downc) if is_c else (self.c_up, self.c_down)

        def add(u, src, at):
            if is_c:
                def body(i, _):
                    a, b = i // 2, i % 2
                    self.p_c[p, a, u, b] = self.p_c[p, a, u, b] + src[p, a, at, b]
                    return 0
                lax.fori_loop(0, 4, body, 0)
            else:
                for h in range(2):
                    self.p_ab[p, self.s, u, self.y, h] = self.p_ab[p, self.s, u, self.y, h] + src[p, at, h]

        @pl.when(self.z == k - 1)
        def _():
            z = k - 1
            if z > 0:
                up(p, z - 1).wait_recv()
                for u in range(z + 1, 4):
                    add(u, self.zuc if is_c else self.zu, u - 1)
            if z < 3:
                up(p, z).start()

        @pl.when(self.z == 4 - k)
        def _():
            z = 4 - k
            if z < 3:
                down(p, z + 1).wait_recv()
                for u in range(0, z):
                    add(u, self.zdc if is_c else self.zd, u)
            if z > 0:
                down(p, z).start()

    def step1(self, p):
        self.c_xa(p).start()
        self.c_yb(p).start()
        self.z_step(p, 1, True)

    def step2(self, p):
        self.c_xa(p).wait_recv()

        def body(i, _):
            a, b = i // 2, i % 2
            self.p_ab[p, self.s, a, b, 0] = self.p_ab[p, self.s, a, b, 0] + self.xa[p, a, b]
            return 0
        lax.fori_loop(0, 8, body, 0)
        self.c_ya(p).start()
        self.c_yb(p).wait_recv()

        def body(i, _):
            a, b = i // 4, i % 4
            self.p_ab[p, a, b, self.y, 1] = self.p_ab[p, a, b, self.y, 1] + self.yb[p, a, b]
            return 0
        lax.fori_loop(0, 8, body, 0)
        self.c_xb(p).start()
        self.z_step(p, 2, True)

    def step3(self, p):
        self.c_ya(p).wait_recv()
        self.c_xb(p).wait_recv()

        def body(b, _):
            self.p_ab[p, self.s, b, self.y, 0] = self.p_ab[p, self.s, b, self.y, 0] + self.ya[p, b]
            self.p_ab[p, self.s, b, self.y, 1] = self.p_ab[p, self.s, b, self.y, 1] + self.xb[p, b]
            return 0
        lax.fori_loop(0, 4, body, 0)
        self.z_step(p, 1, False)
        self.z_step(p, 3, True)

    def step4(self, p):
        self.z_step(p, 2, False)
        self.z_step(p, 4, True)
        z = self.z

        @pl.when(z > 0)
        def _():
            def body(i, _):
                a, b = i // 2, i % 2
                self.p_c[p, a, z, b] = self.p_c[p, a, z, b] + self.zuc[p, a, z - 1, b]
                return 0
            lax.fori_loop(0, 4, body, 0)

        @pl.when(z < 3)
        def _():
            def body(i, _):
                a, b = i // 2, i % 2
                self.p_c[p, a, z, b] = self.p_c[p, a, z, b] + self.zdc[p, a, z, b]
                return 0
            lax.fori_loop(0, 4, body, 0)
        self.c_xc(p).start()

    def step5(self, p):
        self.z_step(p, 3, False)
        self.c_xc(p).wait_recv()
        for b in range(2):
            self.p_c[p, self.s, self.z, b] = self.p_c[p, self.s, self.z, b] + self.xc[p, b]
        self.c_yc(p).start()

    def step6(self, p):
        self.z_step(p, 4, False)
        z = self.z
        base = p * (PER * TILE)
        cols = pl.ds(pl.multiple_of(base, TILE), AB_W)
        colc = pl.ds(pl.multiple_of(base + AB_W, TILE), C_W)
        for h in range(2):
            rows = slice(16 * h, 16 * h + 16)
            mine = self.p_ab[p, self.s, z, self.y, h].astype(jnp.float32)

            @pl.when(z == 0)
            def _():
                self.out[rows, cols] = mine + self.zd[p, 0, h].astype(jnp.float32)

            @pl.when(z == 3)
            def _():
                self.out[rows, cols] = mine + self.zu[p, 2, h].astype(jnp.float32)

            @pl.when((z > 0) & (z < 3))
            def _():
                self.out[rows, cols] = (mine + self.zu[p, z - 1, h].astype(jnp.float32)) + self.zd[p, z, h].astype(jnp.float32)
        self.c_yc(p).wait_recv()
        self.out[:, colc] = self.p_c[p, self.s, z, self.y].astype(jnp.float32) + self.yc[p].astype(jnp.float32)

    def tick(self, t):
        steps = (self.step1, self.step2, self.step3, self.step4, self.step5, self.step6)
        for k, step in enumerate(steps):
            p = t - k
            if isinstance(t, int):
                if 0 <= p < NS:
                    step(p)
            else:
                @pl.when((p >= 0) & (p < NS))
                def _(step=step, p=p):
                    step(p)

    def finish(self):
        def body(p, _):
            self.c_xa(p).wait_send()
            self.c_yb(p).wait_send()
            self.c_ya(p).wait_send()
            self.c_xb(p).wait_send()
            self.c_xc(p).wait_send()
            self.c_yc(p).wait_send()
            for z in range(4):
                @pl.when(self.z == z)
                def _(z=z):
                    if z < 3:
                        self.c_up(p, z).wait_send()
                        self.c_upc(p, z).wait_send()
                    if z > 0:
                        self.c_down(p, z).wait_send()
                        self.c_downc(p, z).wait_send()
            return 0
        lax.fori_loop(0, NS, body, 0)


EXCHANGE_SCRATCH = [
    pltpu.VMEM((NS, 2, 4, 2, 2, 16, AB_W), jnp.bfloat16),
    pltpu.VMEM((NS, 2, 4, 2, 32, C_W), jnp.bfloat16),
    pltpu.VMEM((NS, 4, 2, 16, AB_W), jnp.bfloat16),
    pltpu.VMEM((NS, 2, 4, 16, AB_W), jnp.bfloat16),
    pltpu.VMEM((NS, 4, 16, AB_W), jnp.bfloat16),
    pltpu.VMEM((NS, 4, 16, AB_W), jnp.bfloat16),
    pltpu.VMEM((NS, 3, 2, 16, AB_W), jnp.bfloat16),
    pltpu.VMEM((NS, 3, 2, 16, AB_W), jnp.bfloat16),
    pltpu.VMEM((NS, 2, 3, 2, 32, C_W), jnp.bfloat16),
    pltpu.VMEM((NS, 2, 3, 2, 32, C_W), jnp.bfloat16),
    pltpu.VMEM((NS, 2, 32, C_W), jnp.bfloat16),
    pltpu.VMEM((NS, 32, C_W), jnp.bfloat16),
    pltpu.SemaphoreType.DMA((10, NS)),
    pltpu.SemaphoreType.DMA((10, NS)),
]


def greet():
    s, t, z, y, c = place()
    bar = pltpu.get_barrier_semaphore()

    def tell(dev):
        pl.semaphore_signal(bar, inc=1, device_id=dev, device_id_type=MESH_ID)
    tell({"seq": 1 - s, "tm": t})
    tell({"seq": s, "tm": t + 2 - 4 * y})
    tell({"seq": s, "tm": t + 1 - 2 * c})

    @pl.when(z < 3)
    def _():
        tell({"seq": s, "tm": t + 4})

    @pl.when(z > 0)
    def _():
        tell({"seq": s, "tm": t - 4})
    pl.semaphore_wait(bar, 3 + jnp.where(z < 3, 1, 0) + jnp.where(z > 0, 1, 0))


def grads_kernel(a0, a1, a2, a3, a4, a5, g_d, g_u, g_o, g_p, out,
                 at_full, at_oth, o_d, o_u, o_o, o_p, sib_s, sib_r, p_ab, p_c, *rest):
    bufs, sems = rest[:10], rest[10:]
    s, t, z, y, c = place()
    greet()
    sib = {"seq": s, "tm": t + 1 - 2 * c}
    ex = Exchange(p_ab, p_c, bufs, sems, out)
    copies = []

    def to_sibling(src, dst):
        k = len(copies)
        cp = pltpu.make_async_remote_copy(
            src_ref=src, dst_ref=dst, send_sem=sib_s.at[k], recv_sem=sib_r.at[k],
            device_id=sib, device_id_type=MESH_ID)
        cp.start()
        copies.append(cp)

    for i, a in enumerate((a0, a1, a2, a3, a4, a5)):
        at_full[i] = jnp.transpose(a[...]).reshape(16, 2, 32, 256)
        to_sibling(at_full.at[i, :, 1 - c], at_oth.at[i])
    for g, o in ((g_d, o_d), (g_u, o_u), (g_o, o_o), (g_p, o_p)):
        to_sibling(g, o)
    for cp in copies:
        cp.wait_recv()

    def product(i, g, o, cols):
        own = at_full[i, :, c].reshape(512, 256)
        oth = at_oth[i].reshape(512, 256)
        return (jnp.dot(own, g[:, cols], preferred_element_type=jnp.float32)
                + jnp.dot(oth, o[:, cols], preferred_element_type=jnp.float32))

    def pair(i, g, o, block, tile):
        acc = product(i, g, o, pl.ds(pl.multiple_of(block * 256, 256), 256))
        store_tile(p_ab, p_c, tile, acc[:, :128])
        store_tile(p_ab, p_c, tile + 1, acc[:, 128:])

    def ff(b, _):
        f = 8 * (b // 2) + 2 * (b % 2)
        pair(0, g_d, o_d, b, f)
        pair(1, g_u, o_u, b, f + 4)
        return 0
    lax.fori_loop(0, 16, ff, 0)

    def op(b, _):
        pair(2, g_o, o_o, b, 64 + 2 * b)
        return 0
    lax.fori_loop(0, 9, op, 0)

    def pp(b, _):
        pair(3, g_p, o_p, b, 82 + 2 * b)
        return 0
    lax.fori_loop(0, 12, pp, 0)
    last = product(3, g_p, o_p, slice(24 * 128, 25 * 128))
    lane = lax.broadcasted_iota(jnp.int32, (256, 128), 1)
    for i, at in ((4, 104), (5, 105)):
        ones = jnp.where(lane == at, 1.0, 0.0).astype(jnp.bfloat16)
        last += jnp.dot(at_full[i, :, c].reshape(512, 256), ones, preferred_element_type=jnp.float32)
        last += jnp.dot(at_oth[i].reshape(512, 256), ones, preferred_element_type=jnp.float32)
    store_tile(p_ab, p_c, 106, last)
    store_tile(p_ab, p_c, 107, jnp.zeros((512, 128), jnp.float32))

    def run(t, _):
        ex.tick(t)
        return 0
    lax.fori_loop(0, NS + 5, run, 0)
    ex.finish()
    for cp in copies:
        cp.wait_send()


def summed_grads(acts, g_d, g_u, g_o, g_p):
    n = 10
    return pl.pallas_call(
        grads_kernel,
        out_shape=jax.ShapeDtypeStruct((32, FLAT), jnp.float32),
        in_specs=[pl.BlockSpec(memory_space=pltpu.VMEM)] * 10,
        out_specs=pl.BlockSpec(memory_space=pltpu.VMEM),
        scratch_shapes=[
            pltpu.VMEM((6, 16, 2, 32, 256), jnp.bfloat16),
            pltpu.VMEM((6, 16, 32, 256), jnp.bfloat16),
            pltpu.VMEM(g_d.shape, jnp.bfloat16),
            pltpu.VMEM(g_u.shape, jnp.bfloat16),
            pltpu.VMEM(g_o.shape, jnp.bfloat16),
            pltpu.VMEM(g_p.shape, jnp.bfloat16),
            pltpu.SemaphoreType.DMA((n,)),
            pltpu.SemaphoreType.DMA((n,)),
        ] + EXCHANGE_SCRATCH,
        compiler_params=pltpu.CompilerParams(
            collective_id=0, has_side_effects=True, vmem_limit_bytes=62 << 20),
        name="grads",
    )(*acts, g_d, g_u, g_o, g_p)


def per_device(
    kernel_path,
    layer_input,
    routes,
    memory_lengths,
    norm_gains,
    w_query,
    w_key,
    w_value,
    w_router,
    w_output,
    w_up,
    w_down,
    output_cot,
):
    seg_len = layer_input.shape[1]
    own_rows = layer_input[0].astype(jnp.float32)
    memory_length = memory_lengths[0, 0]
    gains_f = norm_gains.astype(jnp.float32)
    first_gain = gains_f[0]
    second_gain = gains_f[1]
    scale_factor = DH ** (-0.5)
    allowed = attention_mask(memory_length, seg_len)
    onehot = one_hot_routes(routes[0])
    unit_normed = normalize(own_rows, jnp.ones_like(first_gain))
    own_normed = (unit_normed * first_gain).astype(jnp.bfloat16)

    def projections():
        queries = matmul(own_normed, w_query).astype(jnp.bfloat16)
        key_own = matmul(own_normed, w_key).astype(jnp.bfloat16)
        logits = matmul(own_normed, w_router).reshape(seg_len, 2 * H, E)
        gate_sig = jax.nn.sigmoid(logits)
        gate_vals = gate_sig * onehot
        projected = matmul(own_normed, w_value).reshape(seg_len, H, E, DH)
        value_own = (
            jnp.sum(gate_vals[:, :H, :, None] * projected, axis=2)
            .reshape(seg_len, H * DH)
            .astype(jnp.bfloat16)
        )
        return (queries, key_own, gate_sig, gate_vals, projected, value_own)

    queries, key_own, gate_sig, gate_vals, projected, value_own = projections()
    key_mem, value_mem = passed_along((key_own, value_own), "tm", 1)
    key_rows = jnp.concatenate([key_mem, key_own], axis=0)
    value_rows = jnp.concatenate([value_mem, value_own], axis=0)
    head_outs = []
    log_norms = []
    for head_idx in range(H):
        columns = slice(head_idx * DH, (head_idx + 1) * DH)
        scores = (
            jnp.einsum(
                "qd,kd->qk",
                queries[:, columns],
                key_rows[:, columns],
                preferred_element_type=jnp.float32,
            )
            * scale_factor
        )
        scores = jnp.where(allowed, scores, -1e30)
        peak = jnp.max(scores, axis=-1, keepdims=True)
        exp_scores = jnp.exp(scores - peak)
        total = jnp.sum(exp_scores, axis=-1, keepdims=True)
        weights = (exp_scores / total).astype(jnp.bfloat16)
        head_outs.append(matmul(weights, value_rows[:, columns]))
        log_norms.append(peak + jnp.log(total))
    attended = jnp.concatenate(head_outs, axis=1).astype(jnp.bfloat16)
    out_gates = gate_vals[:, H:]
    attended_f = attended.astype(jnp.float32).reshape(seg_len, H, 1, DH)
    mixed_in = (attended_f * out_gates[..., None]).reshape(seg_len, H * E * DH).astype(jnp.bfloat16)
    middle = own_rows + matmul(mixed_in, w_output)
    hidden_normed = normalize(middle, second_gain).astype(jnp.bfloat16)
    pre_act = matmul(hidden_normed, w_up)
    activated = exact_gelu(pre_act).astype(jnp.bfloat16)
    layer_out = middle + matmul(activated, w_down)
    output_block = layer_out.astype(jnp.bfloat16)[None]
    down_cot = output_cot[0]
    out_cot = down_cot.astype(jnp.float32)
    grad_down = tr_times(activated, down_cot)
    grad_act = times_tr(down_cot, w_down)
    unused_gelu, gelu_pull = jax.vjp(exact_gelu, pre_act)
    up_cot = gelu_pull(grad_act)[0].astype(jnp.bfloat16)
    grad_up = tr_times(hidden_normed, up_cot)
    normed_second_cot = times_tr(up_cot, w_up)
    unused_norm, second_pull = jax.vjp(normalize, middle, second_gain)
    middle_part, grad_second = second_pull(normed_second_cot)
    middle_cot = out_cot + middle_part
    branch_cot = middle_cot.astype(jnp.bfloat16)
    grad_output = tr_times(mixed_in, branch_cot)
    mixed_cot = times_tr(branch_cot, w_output).reshape(seg_len, H, E, DH)
    out_gate_cot = jnp.sum(mixed_cot * attended_f, axis=-1)
    attended_cot = (
        jnp.sum(mixed_cot * out_gates[..., None], axis=2)
        .reshape(seg_len, H * DH)
        .astype(jnp.bfloat16)
    )
    queries, key_own, gate_sig, gate_vals, projected, value_own = projections()
    key_back, value_back = passed_along((key_own, value_own), "tm", 1)
    key_rows = jnp.concatenate([key_back, key_own], axis=0)
    value_rows = jnp.concatenate([value_back, value_own], axis=0)
    query_grads = []
    key_grads = []
    value_grads = []
    for head_idx in range(H):
        columns = slice(head_idx * DH, (head_idx + 1) * DH)
        scores = (
            jnp.einsum(
                "qd,kd->qk",
                queries[:, columns],
                key_rows[:, columns],
                preferred_element_type=jnp.float32,
            )
            * scale_factor
        )
        scores = jnp.where(allowed, scores, -1e30)
        probs = jnp.exp(scores - log_norms[head_idx])
        weights = probs.astype(jnp.bfloat16)
        cot_head = attended_cot[:, columns]
        value_grads.append(tr_times(weights, cot_head))
        prob_cot = times_tr(cot_head, value_rows[:, columns])
        score_cot = (probs * (prob_cot - jnp.sum(probs * prob_cot, axis=-1, keepdims=True))).astype(
            jnp.bfloat16
        )
        query_grads.append(matmul(score_cot, key_rows[:, columns]) * scale_factor)
        key_grads.append(tr_times(score_cot, queries[:, columns]) * scale_factor)
    query_cot = jnp.concatenate(query_grads, axis=1).astype(jnp.bfloat16)
    key_cot_all = jnp.concatenate(key_grads, axis=1)
    value_cot_all = jnp.concatenate(value_grads, axis=1)
    key_mem_cot = key_cot_all[:seg_len].astype(jnp.bfloat16)
    key_own_cot = key_cot_all[seg_len:].astype(jnp.bfloat16)
    value_mem_cot = value_cot_all[:seg_len].astype(jnp.bfloat16)
    value_own_cot = value_cot_all[seg_len:].astype(jnp.bfloat16)
    key_next, value_next = passed_along((key_mem_cot, value_mem_cot), "tm", -1)
    own_vcot = value_own_cot.astype(jnp.float32).reshape(seg_len, H, 1, DH)
    next_vcot = value_next.astype(jnp.float32).reshape(seg_len, H, 1, DH)
    val_gates = gate_vals[:, :H, :, None]
    proj_own_cot = (val_gates * own_vcot).reshape(seg_len, H * E * DH).astype(jnp.bfloat16)
    proj_next_cot = (val_gates * next_vcot).reshape(seg_len, H * E * DH).astype(jnp.bfloat16)
    gate_own_cot = jnp.concatenate([jnp.sum(own_vcot * projected, axis=-1), out_gate_cot], axis=1)
    gate_next_cot = jnp.concatenate(
        [jnp.sum(next_vcot * projected, axis=-1), jnp.zeros_like(out_gate_cot)], axis=1
    )
    slope = gate_sig * (1.0 - gate_sig) * onehot
    logit_own_cot = (gate_own_cot * slope).reshape(seg_len, 2 * H * E).astype(jnp.bfloat16)
    logit_next_cot = (gate_next_cot * slope).reshape(seg_len, 2 * H * E).astype(jnp.bfloat16)
    twice_normed = jnp.concatenate([own_normed, own_normed], axis=0)
    key_both = jnp.concatenate([key_own_cot, key_next], axis=0)
    proj_both = jnp.concatenate([proj_own_cot, proj_next_cot], axis=0)
    logit_both = jnp.concatenate([logit_own_cot, logit_next_cot], axis=0)
    grad_query = tr_times(own_normed, query_cot)
    grad_key = tr_times(twice_normed, key_both)
    grad_value = tr_times(twice_normed, proj_both)
    grad_router = tr_times(twice_normed, logit_both)
    normed_both = (
        times_tr(key_both, w_key) + times_tr(proj_both, w_value) + times_tr(logit_both, w_router)
    )
    own_normed_cot = normed_both[:seg_len] + times_tr(query_cot, w_query)
    next_normed_cot = normed_both[seg_len:]
    grad_first = jnp.sum((own_normed_cot + next_normed_cot) * unit_normed, axis=0)
    unused_first, first_pull = jax.vjp(normalize, own_rows, first_gain)
    input_part = first_pull(own_normed_cot)[0]
    input_cot = middle_cot + input_part
    grad_gains = jnp.stack([grad_first, grad_second], axis=0)
    if kernel_path:
        middle_unit = normalize(middle, jnp.ones_like(second_gain))
        bf = jnp.bfloat16
        acts = (down_cot, hidden_normed, branch_cot, own_normed,
                ((own_normed_cot + next_normed_cot) * unit_normed).astype(bf),
                (normed_second_cot * middle_unit).astype(bf))
        g_o = jnp.pad(mixed_in, ((0, 0), (0, 64)))
        add = lambda a, b: (a.astype(jnp.float32) + b.astype(jnp.float32)).astype(bf)
        g_p = jnp.concatenate([query_cot, add(key_own_cot, key_next), add(proj_own_cot, proj_next_cot),
                               add(logit_own_cot, logit_next_cot), jnp.zeros((seg_len, 24), bf)], axis=1)
        flat = summed_grads(acts, activated, up_cot, g_o, g_p)
        ff = flat[:, :8192].reshape(32, 8, 2, 512)
        o = flat[:, 64 * 128:64 * 128 + 2240]
        p = flat[:, 82 * 128:]
        return (output_block, input_cot[None], p[:, 3176 + 0:3178].T, p[:, :448], p[:, 448:896],
                p[:, 896:3136], p[:, 3136:3176], o.T, ff[:, :, 1].reshape(32, 4096), ff[:, :, 0].reshape(32, 4096).T)
    row_query, row_key, row_value, row_router, row_up = (
        lax.psum_scatter(grad_query, ("seq", "tm"), scatter_dimension=0, tiled=True),
        lax.psum_scatter(grad_key, ("seq", "tm"), scatter_dimension=0, tiled=True),
        lax.psum_scatter(grad_value, ("seq", "tm"), scatter_dimension=0, tiled=True),
        lax.psum_scatter(grad_router, ("seq", "tm"), scatter_dimension=0, tiled=True),
        lax.psum_scatter(grad_up, ("seq", "tm"), scatter_dimension=0, tiled=True),
    )
    col_gains, col_output, col_down = (
        lax.psum_scatter(grad_gains, ("seq", "tm"), scatter_dimension=1, tiled=True),
        lax.psum_scatter(grad_output, ("seq", "tm"), scatter_dimension=1, tiled=True),
        lax.psum_scatter(grad_down, ("seq", "tm"), scatter_dimension=1, tiled=True),
    )
    return (
        output_block,
        input_cot[None],
        col_gains,
        row_query,
        row_key,
        row_value,
        row_router,
        col_output,
        row_up,
        col_down,
    )


def solution(mesh):
    placed = (
        P("seq", "tm", None),
        P("seq", "tm", None, None),
        P("seq", "tm"),
        P(),
        P(),
        P(),
        P(),
        P(),
        P(),
        P(),
        P(),
        P("seq", "tm", None),
    )
    kernel_path = mesh.shape["seq"] == 2 and mesh.shape["tm"] == 16
    return jax.shard_map(
        functools.partial(per_device, kernel_path),
        mesh=mesh,
        in_specs=placed,
        out_specs=(
            P("seq", "tm", None),
            P("seq", "tm", None),
            P(None, ("seq", "tm")),
            P(("seq", "tm"), None),
            P(("seq", "tm"), None),
            P(("seq", "tm"), None),
            P(("seq", "tm"), None),
            P(None, ("seq", "tm")),
            P(("seq", "tm"), None),
            P(None, ("seq", "tm")),
        ),
        check_vma=False,
    )
```

```python
import types

import jax
import jax.numpy as jnp
import ml_dtypes
import numpy as np
from jax import lax
from jax.experimental import pallas as pl
from jax.experimental.pallas import tpu as pltpu
from jax.sharding import PartitionSpec as P

H = 4
DH = 112
E = 5


epsilon = 1e-05


def passed_along(value, axis, steps):
    count = lax.axis_size(axis)
    initial, last = (max(0, -steps), min(count, count - steps))
    return lax.ppermute(value, axis, [(source, source + steps) for source in range(initial, last)])


def normalize(values, gain_vec):
    centre = values - jnp.mean(values, axis=-1, keepdims=True)
    spread = jnp.mean(centre * centre, axis=-1, keepdims=True)
    return centre * lax.rsqrt(spread + epsilon) * gain_vec


def exact_gelu(arg_in):
    return jax.nn.gelu(arg_in, approximate=False)


def matmul(left_op, right_op):
    return jnp.dot(left_op, right_op, preferred_element_type=jnp.float32)


def times_tr(left_op, right_op):
    return lax.dot_general(
        left_op, right_op, (((1,), (1,)), ((), ())), preferred_element_type=jnp.float32
    )


def tr_times(left_op, right_op):
    return lax.dot_general(
        left_op, right_op, (((0,), (0,)), ((), ())), preferred_element_type=jnp.float32
    )


def one_hot_routes(route_ids):
    return jnp.sum(
        (route_ids[..., None] == jnp.arange(E, dtype=jnp.int32)).astype(jnp.float32), axis=-2
    )


def attention_mask(memory_length, seg_len):
    query_pos = jnp.arange(seg_len, dtype=jnp.int32)[:, None]
    key_pos = jnp.arange(2 * seg_len, dtype=jnp.int32)[None, :]
    return jnp.where(
        key_pos < seg_len, key_pos >= seg_len - memory_length, key_pos - seg_len <= query_pos
    )


def per_device(
    layer_input,
    routes,
    memory_lengths,
    norm_gains,
    w_query,
    w_key,
    w_value,
    w_router,
    w_output,
    w_up,
    w_down,
    output_cot,
):
    seg_len = layer_input.shape[1]
    own_rows = layer_input[0].astype(jnp.float32)
    memory_length = memory_lengths[0, 0]
    gains_f = norm_gains.astype(jnp.float32)
    first_gain = gains_f[0]
    second_gain = gains_f[1]
    scale_factor = DH ** (-0.5)
    allowed = attention_mask(memory_length, seg_len)
    onehot = one_hot_routes(routes[0])
    unit_normed = normalize(own_rows, jnp.ones_like(first_gain))
    own_normed = (unit_normed * first_gain).astype(jnp.bfloat16)

    def projections():
        queries = matmul(own_normed, w_query).astype(jnp.bfloat16)
        key_own = matmul(own_normed, w_key).astype(jnp.bfloat16)
        logits = matmul(own_normed, w_router).reshape(seg_len, 2 * H, E)
        gate_sig = jax.nn.sigmoid(logits)
        gate_vals = gate_sig * onehot
        projected = matmul(own_normed, w_value).reshape(seg_len, H, E, DH)
        value_own = (
            jnp.sum(gate_vals[:, :H, :, None] * projected, axis=2)
            .reshape(seg_len, H * DH)
            .astype(jnp.bfloat16)
        )
        return (queries, key_own, gate_sig, gate_vals, projected, value_own)

    queries, key_own, gate_sig, gate_vals, projected, value_own = projections()
    key_mem, value_mem = passed_along((key_own, value_own), "tm", 1)
    key_rows = jnp.concatenate([key_mem, key_own], axis=0)
    value_rows = jnp.concatenate([value_mem, value_own], axis=0)
    head_outs = []
    log_norms = []
    for head_idx in range(H):
        columns = slice(head_idx * DH, (head_idx + 1) * DH)
        scores = (
            jnp.einsum(
                "qd,kd->qk",
                queries[:, columns],
                key_rows[:, columns],
                preferred_element_type=jnp.float32,
            )
            * scale_factor
        )
        scores = jnp.where(allowed, scores, -1e30)
        peak = jnp.max(scores, axis=-1, keepdims=True)
        exp_scores = jnp.exp(scores - peak)
        total = jnp.sum(exp_scores, axis=-1, keepdims=True)
        weights = (exp_scores / total).astype(jnp.bfloat16)
        head_outs.append(matmul(weights, value_rows[:, columns]))
        log_norms.append(peak + jnp.log(total))
    attended = jnp.concatenate(head_outs, axis=1).astype(jnp.bfloat16)
    out_gates = gate_vals[:, H:]
    attended_f = attended.astype(jnp.float32).reshape(seg_len, H, 1, DH)
    mixed_in = (attended_f * out_gates[..., None]).reshape(seg_len, H * E * DH).astype(jnp.bfloat16)
    middle = own_rows + matmul(mixed_in, w_output)
    hidden_normed = normalize(middle, second_gain).astype(jnp.bfloat16)
    pre_act = matmul(hidden_normed, w_up)
    activated = exact_gelu(pre_act).astype(jnp.bfloat16)
    layer_out = middle + matmul(activated, w_down)
    output_block = layer_out.astype(jnp.bfloat16)[None]
    down_cot = output_cot[0]
    out_cot = down_cot.astype(jnp.float32)
    grad_down = tr_times(activated, down_cot)
    grad_act = times_tr(down_cot, w_down)
    unused_gelu, gelu_pull = jax.vjp(exact_gelu, pre_act)
    up_cot = gelu_pull(grad_act)[0].astype(jnp.bfloat16)
    grad_up = tr_times(hidden_normed, up_cot)
    normed_second_cot = times_tr(up_cot, w_up)
    unused_norm, second_pull = jax.vjp(normalize, middle, second_gain)
    middle_part, grad_second = second_pull(normed_second_cot)
    middle_cot = out_cot + middle_part
    branch_cot = middle_cot.astype(jnp.bfloat16)
    grad_output = tr_times(mixed_in, branch_cot)
    mixed_cot = times_tr(branch_cot, w_output).reshape(seg_len, H, E, DH)
    out_gate_cot = jnp.sum(mixed_cot * attended_f, axis=-1)
    attended_cot = (
        jnp.sum(mixed_cot * out_gates[..., None], axis=2)
        .reshape(seg_len, H * DH)
        .astype(jnp.bfloat16)
    )
    queries, key_own, gate_sig, gate_vals, projected, value_own = projections()
    key_back, value_back = passed_along((key_own, value_own), "tm", 1)
    key_rows = jnp.concatenate([key_back, key_own], axis=0)
    value_rows = jnp.concatenate([value_back, value_own], axis=0)
    query_grads = []
    key_grads = []
    value_grads = []
    for head_idx in range(H):
        columns = slice(head_idx * DH, (head_idx + 1) * DH)
        scores = (
            jnp.einsum(
                "qd,kd->qk",
                queries[:, columns],
                key_rows[:, columns],
                preferred_element_type=jnp.float32,
            )
            * scale_factor
        )
        scores = jnp.where(allowed, scores, -1e30)
        probs = jnp.exp(scores - log_norms[head_idx])
        weights = probs.astype(jnp.bfloat16)
        cot_head = attended_cot[:, columns]
        value_grads.append(tr_times(weights, cot_head))
        prob_cot = times_tr(cot_head, value_rows[:, columns])
        score_cot = (probs * (prob_cot - jnp.sum(probs * prob_cot, axis=-1, keepdims=True))).astype(
            jnp.bfloat16
        )
        query_grads.append(matmul(score_cot, key_rows[:, columns]) * scale_factor)
        key_grads.append(tr_times(score_cot, queries[:, columns]) * scale_factor)
    query_cot = jnp.concatenate(query_grads, axis=1).astype(jnp.bfloat16)
    key_cot_all = jnp.concatenate(key_grads, axis=1)
    value_cot_all = jnp.concatenate(value_grads, axis=1)
    key_mem_cot = key_cot_all[:seg_len].astype(jnp.bfloat16)
    key_own_cot = key_cot_all[seg_len:].astype(jnp.bfloat16)
    value_mem_cot = value_cot_all[:seg_len].astype(jnp.bfloat16)
    value_own_cot = value_cot_all[seg_len:].astype(jnp.bfloat16)
    key_next, value_next = passed_along((key_mem_cot, value_mem_cot), "tm", -1)
    own_vcot = value_own_cot.astype(jnp.float32).reshape(seg_len, H, 1, DH)
    next_vcot = value_next.astype(jnp.float32).reshape(seg_len, H, 1, DH)
    val_gates = gate_vals[:, :H, :, None]
    proj_own_cot = (val_gates * own_vcot).reshape(seg_len, H * E * DH).astype(jnp.bfloat16)
    proj_next_cot = (val_gates * next_vcot).reshape(seg_len, H * E * DH).astype(jnp.bfloat16)
    gate_own_cot = jnp.concatenate([jnp.sum(own_vcot * projected, axis=-1), out_gate_cot], axis=1)
    gate_next_cot = jnp.concatenate(
        [jnp.sum(next_vcot * projected, axis=-1), jnp.zeros_like(out_gate_cot)], axis=1
    )
    slope = gate_sig * (1.0 - gate_sig) * onehot
    logit_own_cot = (gate_own_cot * slope).reshape(seg_len, 2 * H * E).astype(jnp.bfloat16)
    logit_next_cot = (gate_next_cot * slope).reshape(seg_len, 2 * H * E).astype(jnp.bfloat16)
    twice_normed = jnp.concatenate([own_normed, own_normed], axis=0)
    key_both = jnp.concatenate([key_own_cot, key_next], axis=0)
    proj_both = jnp.concatenate([proj_own_cot, proj_next_cot], axis=0)
    logit_both = jnp.concatenate([logit_own_cot, logit_next_cot], axis=0)
    grad_query = tr_times(own_normed, query_cot)
    grad_key = tr_times(twice_normed, key_both)
    grad_value = tr_times(twice_normed, proj_both)
    grad_router = tr_times(twice_normed, logit_both)
    normed_both = (
        times_tr(key_both, w_key) + times_tr(proj_both, w_value) + times_tr(logit_both, w_router)
    )
    own_normed_cot = normed_both[:seg_len] + times_tr(query_cot, w_query)
    next_normed_cot = normed_both[seg_len:]
    grad_first = jnp.sum((own_normed_cot + next_normed_cot) * unit_normed, axis=0)
    unused_first, first_pull = jax.vjp(normalize, own_rows, first_gain)
    input_part = first_pull(own_normed_cot)[0]
    input_cot = middle_cot + input_part
    grad_gains = jnp.stack([grad_first, grad_second], axis=0)
    row_query, row_key, row_value, row_router, row_up = (
        lax.psum_scatter(grad_query, ("seq", "tm"), scatter_dimension=0, tiled=True),
        lax.psum_scatter(grad_key, ("seq", "tm"), scatter_dimension=0, tiled=True),
        lax.psum_scatter(grad_value, ("seq", "tm"), scatter_dimension=0, tiled=True),
        lax.psum_scatter(grad_router, ("seq", "tm"), scatter_dimension=0, tiled=True),
        lax.psum_scatter(grad_up, ("seq", "tm"), scatter_dimension=0, tiled=True),
    )
    col_gains, col_output, col_down = (
        lax.psum_scatter(grad_gains, ("seq", "tm"), scatter_dimension=1, tiled=True),
        lax.psum_scatter(grad_output, ("seq", "tm"), scatter_dimension=1, tiled=True),
        lax.psum_scatter(grad_down, ("seq", "tm"), scatter_dimension=1, tiled=True),
    )
    return (
        output_block,
        input_cot[None],
        col_gains,
        row_query,
        row_key,
        row_value,
        row_router,
        col_output,
        row_up,
        col_down,
    )


VMEM_LIMIT = 64 << 20

MESH_ID = pl.DeviceIdType.MESH
NS = 12
TILE = 128
AB_T = 7
C_T = 2
PER = AB_T + C_T
AB_W = AB_T * TILE
C_W = C_T * TILE
FLAT = NS * PER * TILE
NR = 4
NZ = 6
FIRST = slice(0, AB_W)
LAST = slice(AB_W, AB_W + C_W)
HALF = (slice(0, 16), slice(16, 32))


def rem(a, n):
    return a % n if isinstance(a, int) else lax.rem(a, n)


def place():
    s = lax.axis_index("seq")
    t = lax.axis_index("tm")
    return s, t, t // 4, (t // 2) % 2, t % 2


def store_tile(parts, tile, value):
    piece = tile // PER
    slot = tile - piece * PER
    at = slot * TILE
    cols = slice(at, at + TILE) if isinstance(at, int) else pl.ds(pl.multiple_of(at, TILE), TILE)
    parts[piece, :, :, :, :, cols] = value.reshape(2, 4, 2, 32, TILE).astype(jnp.bfloat16)


class Exchange:
    def __init__(self, parts, bufs, sems, stage, out_sem, out):
        self.parts, self.out = parts, out
        self.stage, self.out_sem = stage, out_sem
        (self.xa, self.yb, self.ya, self.xb, self.zu, self.zd, self.zuc, self.zdc, self.xc, self.yc) = bufs
        self.ssem, self.rsem = sems
        self.s, self.t, self.z, self.y, self.c = place()
        s, t = self.s, self.t
        self.to_x = {"seq": 1 - s, "tm": t}
        self.to_y = {"seq": s, "tm": t + 2 - 4 * self.y}
        self.to_up = {"seq": s, "tm": t + 4}
        self.to_down = {"seq": s, "tm": t - 4}

    def copy(self, kind, piece, src, dst, dev):
        return pltpu.make_async_remote_copy(
            src_ref=src, dst_ref=dst, send_sem=self.ssem.at[kind, piece],
            recv_sem=self.rsem.at[kind, piece], device_id=dev, device_id_type=MESH_ID)

    def c_xa(self, p):
        return self.copy(0, p, self.parts.at[p, 1 - self.s, :, :, HALF[0], FIRST], self.xa.at[rem(p, NR)], self.to_x)

    def c_yb(self, p):
        return self.copy(1, p, self.parts.at[p, :, :, 1 - self.y, HALF[1], FIRST], self.yb.at[rem(p, NR)], self.to_y)

    def c_ya(self, p):
        return self.copy(2, p, self.parts.at[p, self.s, :, 1 - self.y, HALF[0], FIRST], self.ya.at[rem(p, NR)], self.to_y)

    def c_xb(self, p):
        return self.copy(3, p, self.parts.at[p, 1 - self.s, :, self.y, HALF[1], FIRST], self.xb.at[rem(p, NR)], self.to_x)

    def c_xc(self, p):
        return self.copy(4, p, self.parts.at[p, 1 - self.s, self.z, :, :, LAST], self.xc.at[rem(p, NR)], self.to_x)

    def c_yc(self, p):
        return self.copy(5, p, self.parts.at[p, self.s, self.z, 1 - self.y, :, LAST], self.yc.at[rem(p, NR)], self.to_y)

    def c_up(self, p, z):
        return self.copy(6, p, self.parts.at[p, self.s, z + 1:4, self.y, :, FIRST], self.zu.at[rem(p, NZ), z:3], self.to_up)

    def c_down(self, p, z):
        return self.copy(7, p, self.parts.at[p, self.s, 0:z, self.y, :, FIRST], self.zd.at[rem(p, NZ), 0:z], self.to_down)

    def c_upc(self, p, z):
        return self.copy(8, p, self.parts.at[p, :, z + 1:4, :, :, LAST], self.zuc.at[rem(p, NZ), :, z:3], self.to_up)

    def c_downc(self, p, z):
        return self.copy(9, p, self.parts.at[p, :, 0:z, :, :, LAST], self.zdc.at[rem(p, NZ), :, 0:z], self.to_down)

    def z_step(self, p, k, is_c):
        up, down = (self.c_upc, self.c_downc) if is_c else (self.c_up, self.c_down)

        def add(u, src, at):
            if is_c:
                def body(i, _):
                    a, b = i // 2, i % 2
                    self.parts[p, a, u, b, :, LAST] = self.parts[p, a, u, b, :, LAST] + src[rem(p, NZ), a, at, b]
                    return 0
                lax.fori_loop(0, 4, body, 0)
            else:
                self.parts[p, self.s, u, self.y, :, FIRST] = self.parts[p, self.s, u, self.y, :, FIRST] + src[rem(p, NZ), at]

        @pl.when(self.z == k - 1)
        def _():
            z = k - 1
            if z > 0:
                up(p, z - 1).wait_recv()
                for u in range(z + 1, 4):
                    add(u, self.zuc if is_c else self.zu, u - 1)
            if z < 3:
                up(p, z).start()

        @pl.when(self.z == 4 - k)
        def _():
            z = 4 - k
            if z < 3:
                down(p, z + 1).wait_recv()
                for u in range(0, z):
                    add(u, self.zdc if is_c else self.zd, u)
            if z > 0:
                down(p, z).start()

    def step1_ab(self, p):
        self.c_xa(p).start()
        self.c_yb(p).start()

    def step1(self, p):
        if isinstance(p, int):
            if p > 0:
                self.step1_ab(p)
        else:
            pl.when(p > 0)(lambda: self.step1_ab(p))
        self.z_step(p, 1, True)

    def step2(self, p):
        self.c_xa(p).wait_recv()

        def body(i, _):
            a, b = i // 2, i % 2
            self.parts[p, self.s, a, b, HALF[0], FIRST] = self.parts[p, self.s, a, b, HALF[0], FIRST] + self.xa[rem(p, NR), a, b]
            return 0
        lax.fori_loop(0, 8, body, 0)
        self.c_ya(p).start()
        self.c_yb(p).wait_recv()

        def body(i, _):
            a, b = i // 4, i % 4
            self.parts[p, a, b, self.y, HALF[1], FIRST] = self.parts[p, a, b, self.y, HALF[1], FIRST] + self.yb[rem(p, NR), a, b]
            return 0
        lax.fori_loop(0, 8, body, 0)
        self.c_xb(p).start()
        self.z_step(p, 2, True)

    def step3(self, p):
        self.c_ya(p).wait_recv()
        self.c_xb(p).wait_recv()

        def body(b, _):
            self.parts[p, self.s, b, self.y, HALF[0], FIRST] = self.parts[p, self.s, b, self.y, HALF[0], FIRST] + self.ya[rem(p, NR), b]
            self.parts[p, self.s, b, self.y, HALF[1], FIRST] = self.parts[p, self.s, b, self.y, HALF[1], FIRST] + self.xb[rem(p, NR), b]
            return 0
        lax.fori_loop(0, 4, body, 0)
        self.z_step(p, 1, False)
        self.z_step(p, 3, True)

    def step4(self, p):
        self.z_step(p, 2, False)
        self.z_step(p, 4, True)
        z = self.z

        @pl.when(z > 0)
        def _():
            def body(i, _):
                a, b = i // 2, i % 2
                self.parts[p, a, z, b, :, LAST] = self.parts[p, a, z, b, :, LAST] + self.zuc[rem(p, NZ), a, z - 1, b]
                return 0
            lax.fori_loop(0, 4, body, 0)

        @pl.when(z < 3)
        def _():
            def body(i, _):
                a, b = i // 2, i % 2
                self.parts[p, a, z, b, :, LAST] = self.parts[p, a, z, b, :, LAST] + self.zdc[rem(p, NZ), a, z, b]
                return 0
            lax.fori_loop(0, 4, body, 0)
        self.c_xc(p).start()

    def step5(self, p):
        self.z_step(p, 3, False)
        self.c_xc(p).wait_recv()
        for b in range(2):
            self.parts[p, self.s, self.z, b, :, LAST] = self.parts[p, self.s, self.z, b, :, LAST] + self.xc[rem(p, NR), b]
        self.c_yc(p).start()

    def step6(self, p):
        self.z_step(p, 4, False)
        z = self.z
        k = p % 2

        @pl.when(p >= 2)
        def _():
            self.c_out(p - 2).wait()
        cols, colc = slice(0, AB_W), slice(AB_W, AB_W + C_W)
        mine = self.parts[p, self.s, z, self.y, :, FIRST].astype(jnp.float32)

        @pl.when(z == 0)
        def _():
            self.stage[k, :, cols] = mine + self.zd[rem(p, NZ), 0].astype(jnp.float32)

        @pl.when(z == 3)
        def _():
            self.stage[k, :, cols] = mine + self.zu[rem(p, NZ), 2].astype(jnp.float32)

        @pl.when((z > 0) & (z < 3))
        def _():
            self.stage[k, :, cols] = (mine + self.zu[rem(p, NZ), z - 1].astype(jnp.float32)) + self.zd[rem(p, NZ), z].astype(jnp.float32)
        self.c_yc(p).wait_recv()
        self.stage[k, :, colc] = self.parts[p, self.s, z, self.y, :, LAST].astype(jnp.float32) + self.yc[rem(p, NR)].astype(jnp.float32)
        self.c_out(p).start()

    def c_out(self, p):
        cols = pl.ds(pl.multiple_of(p * (PER * TILE), TILE), PER * TILE)
        return pltpu.make_async_copy(self.stage.at[p % 2], self.out.at[:, cols], self.out_sem.at[p % 2])

    def tick(self, t):
        steps = (self.step1, self.step2, self.step3, self.step4, self.step5, self.step6)
        for k, step in enumerate(steps):
            p = t - k
            if isinstance(t, int):
                if 0 <= p < NS:
                    step(p)
            else:
                @pl.when((p >= 0) & (p < NS))
                def _(step=step, p=p):
                    step(p)

    def finish(self):
        self.c_out(NS - 2).wait()
        self.c_out(NS - 1).wait()

        def body(p, _):
            self.c_xa(p).wait_send()
            self.c_yb(p).wait_send()
            self.c_ya(p).wait_send()
            self.c_xb(p).wait_send()
            self.c_xc(p).wait_send()
            self.c_yc(p).wait_send()
            for z in range(4):
                @pl.when(self.z == z)
                def _(z=z):
                    if z < 3:
                        self.c_up(p, z).wait_send()
                        self.c_upc(p, z).wait_send()
                    if z > 0:
                        self.c_down(p, z).wait_send()
                        self.c_downc(p, z).wait_send()
            return 0
        lax.fori_loop(0, NS, body, 0)


P_SCRATCH = [pltpu.VMEM((NS, 2, 4, 2, 32, PER * TILE), jnp.bfloat16)]
RECV_SCRATCH = [
    pltpu.VMEM((NR, 4, 2, 16, AB_W), jnp.bfloat16),
    pltpu.VMEM((NR, 2, 4, 16, AB_W), jnp.bfloat16),
    pltpu.VMEM((NR, 4, 16, AB_W), jnp.bfloat16),
    pltpu.VMEM((NR, 4, 16, AB_W), jnp.bfloat16),
    pltpu.VMEM((NZ, 3, 32, AB_W), jnp.bfloat16),
    pltpu.VMEM((NZ, 3, 32, AB_W), jnp.bfloat16),
    pltpu.VMEM((NZ, 2, 3, 2, 32, C_W), jnp.bfloat16),
    pltpu.VMEM((NZ, 2, 3, 2, 32, C_W), jnp.bfloat16),
    pltpu.VMEM((NR, 2, 32, C_W), jnp.bfloat16),
    pltpu.VMEM((NR, 32, C_W), jnp.bfloat16),
]


def greet():
    s, t, z, y, c = place()
    bar = pltpu.get_barrier_semaphore()

    def tell(dev):
        pl.semaphore_signal(bar, inc=1, device_id=dev, device_id_type=MESH_ID)
    tell({"seq": 1 - s, "tm": t})
    tell({"seq": s, "tm": t + 2 - 4 * y})
    tell({"seq": s, "tm": t + 1 - 2 * c})

    @pl.when(z < 3)
    def _():
        tell({"seq": s, "tm": t + 4})

    @pl.when(z > 0)
    def _():
        tell({"seq": s, "tm": t - 4})
    far = jnp.where(c == 1, t + 1, t - 1)
    has_far = (far >= 0) & (far < 16)

    @pl.when(has_far)
    def _():
        tell({"seq": s, "tm": far})
    return bar, 3 + jnp.where(has_far, 1, 0) + jnp.where(z < 3, 1, 0) + jnp.where(z > 0, 1, 0)


D = 1024
FF = 4096
SEG = 256
HD = H * DH
WIDE = H * E * DH
FFB = 512
NFF = FF // FFB
NG = 4
WB = 512
LOGIT = 64
OWN_SIB = 24
F32 = jnp.float32
BF = jnp.bfloat16


def dot(a, b):
    return jnp.dot(a, b, preferred_element_type=F32)


def dot_nt(a, b):
    return lax.dot_general(a, b, (((1,), (1,)), ((), ())), preferred_element_type=F32)


def dot_tn(a, b):
    return lax.dot_general(a, b, (((0,), (0,)), ((), ())), preferred_element_type=F32)


def halves(v):
    top = v.astype(BF)
    return top, (v - top.astype(F32)).astype(BF)


def unit_rows(v):
    centre = v - jnp.mean(v, axis=-1, keepdims=True)
    spread = jnp.mean(centre * centre, axis=-1, keepdims=True)
    inv = lax.rsqrt(spread + epsilon)
    return centre * inv, inv


def norm_back(unit, inv, cot):
    return inv * (cot - jnp.mean(cot, axis=-1, keepdims=True)
                  - unit * jnp.mean(cot * unit, axis=-1, keepdims=True))


def for_rows(step, body):
    def inner(i, _):
        body(pl.ds(pl.multiple_of(i * step, step), step))
        return 0
    lax.fori_loop(0, SEG // step, inner, 0)


def for_wide(body):
    whole = WIDE // WB

    def inner(i, _):
        body(pl.ds(pl.multiple_of(i * WB, WB), WB), i * WB)
        return 0
    lax.fori_loop(0, whole, inner, 0)
    body(slice(whole * WB, WIDE), whole * WB)


NAMES = (
    "x", "oc", "gains", "rt", "rf", "spread", "hot", "wq", "wk", "wr", "wrp", "wu", "wd", "sel", "exv", "exo",
    "xn", "hn", "mid", "lo", "nsc", "q", "k", "v", "sig", "att", "acc", "g_o", "g_p",
    "act", "uc", "bc", "kc", "vc", "kn", "vn", "ob", "gg", "ogc", "qc",
    "at", "full",
    "ld", "ld2", "kv_s", "kv_r", "sib_s", "sib_r", "st", "stage", "out_sem", "ssem", "rsem",
)


def layer_scratch():
    dma = pltpu.SemaphoreType.DMA
    v = pltpu.VMEM
    return [
        v((SEG, D), BF), v((SEG, D), BF), v((2, D), BF), v((2 * H, 2, SEG), jnp.int32), v((128, SEG), BF),
        v((128, 256), BF), v((SEG, 128), F32),
        v((HD, D), BF), v((HD, D), BF), v((2 * H * E, D), BF), v((128, D), BF),
        v((2, D, FFB), BF), v((2, FFB, D), BF), v((WIDE, 512), BF), v((256, 2304), BF), v((256, 2304), BF),
        v((SEG, D), BF), v((SEG, D), BF), v((SEG, D), F32), v((SEG, D), F32), v((SEG, D), F32),
        v((SEG, HD), BF), v((2 * SEG, HD), BF), v((2 * SEG, HD), BF), v((SEG, 128), F32),
        v((SEG, HD), BF), v((2 * SEG, HD), F32), v((2 * SEG, 2304), BF), v((2 * SEG, 3328), BF),
        v((NG, 2 * SEG, FFB), BF), v((NG, 2 * SEG, FFB), BF), v((SEG, D), BF),
        v((2 * SEG, HD), BF), v((2 * SEG, HD), BF), v((SEG, HD), BF), v((SEG, HD), BF), v((SEG, D), BF), v((SEG, 256), BF), v((SEG, 128), F32), v((SEG, HD), F32),
        v((6, 16, 32, 2 * SEG), BF), v((2, 16, 2, 32, SEG), BF),
        dma((16,)), dma((4,)), dma((4,)), dma((4,)), dma((OWN_SIB,)), dma((OWN_SIB,)), dma((2,)),
        v((2, 32, PER * TILE), F32), dma((2,)), dma((10, NS)), dma((10, NS)),
    ]


def layer_kernel(x_h, rt_h, len_s, gains_h, wq_h, wk_h, wv_h, wr_h, wo_h, wu_h, wd_h, oc_h,
                 sel_h, exv_h, exo_h, spread_h, lo_h, ig_h, flat_h, *scratch):
    m = types.SimpleNamespace(**dict(zip(NAMES, scratch[:len(NAMES)])))
    recv = scratch[len(NAMES):]
    s, t, z, y, c = place()
    last_t = lax.axis_size("tm") - 1
    sib = {"seq": s, "tm": t + 1 - 2 * c}
    scale = DH ** -0.5
    own = slice(SEG, 2 * SEG)
    mem = slice(0, SEG)

    bar, peers = greet()

    def load(i, src, dst):
        cp = pltpu.make_async_copy(src, dst, m.ld.at[i])
        cp.start()
        return cp

    def sibling(i, src, dst):
        return pltpu.make_async_remote_copy(
            src_ref=src, dst_ref=dst, send_sem=m.sib_s.at[i], recv_sem=m.sib_r.at[i],
            device_id=sib, device_id_type=MESH_ID)

    def at_copy(i, slot):
        return sibling(i, m.full.at[slot, :, 1 - c], m.at.at[i, :, :, SEG:])

    def turn(i, slot, value):
        m.full[slot] = jnp.transpose(value).reshape(16, 2, 32, SEG)
        m.at[i, :, :, :SEG] = m.full[slot, :, c]
        at_copy(i, slot).start()

    def go_copy():
        return sibling(6, m.g_o.at[mem], m.g_o.at[own])

    def gp_copy():
        return sibling(7, m.g_p.at[mem], m.g_p.at[own])

    def ff_copies(j):
        g = rem(j, NG)
        return (sibling(8 + 2 * j, m.act.at[g, mem], m.act.at[g, own]),
                sibling(9 + 2 * j, m.uc.at[g, mem], m.uc.at[g, own]))

    def ff_loads(j):
        cols = pl.ds(pl.multiple_of(j * FFB, FFB), FFB)
        return (pltpu.make_async_copy(wu_h.at[:, cols], m.wu.at[j % 2], m.ld2.at[j % 2]),
                pltpu.make_async_copy(wd_h.at[cols, :], m.wd.at[j % 2], m.ld2.at[2 + j % 2]))

    def along(i, src, dst, by):
        return pltpu.make_async_remote_copy(
            src_ref=src, dst_ref=dst, send_sem=m.kv_s.at[i], recv_sem=m.kv_r.at[i],
            device_id={"seq": s, "tm": t + by}, device_id_type=MESH_ID)

    def k_copy():
        return along(0, m.k.at[own], m.k.at[mem], 1)

    def v_copy():
        return along(1, m.v.at[own], m.v.at[mem], 1)

    def kc_copy():
        return along(2, m.kc.at[mem], m.kn, -1)

    def vc_copy():
        return along(3, m.vc.at[mem], m.vn, -1)

    def head_lanes(rows, h):
        lane = lax.broadcasted_iota(jnp.int32, (rows, HD), 1)
        return (lane >= h * DH) & (lane < (h + 1) * DH)

    def head_only(v, h):
        return jnp.where(head_lanes(v.shape[0], h), v, jnp.zeros_like(v))

    def gates_wide(table, cols):
        return dot(m.gg[...], table[:, cols])

    def weights_of(h):
        scores = dot_nt(head_only(m.q[...], h), m.k[...]) * scale
        length = len_s[0, 0]
        row = lax.broadcasted_iota(jnp.int32, (SEG, 2 * SEG), 0)
        col = lax.broadcasted_iota(jnp.int32, (SEG, 2 * SEG), 1)
        allowed = ((col < SEG) & (col >= SEG - length)) | ((col >= SEG) & (col - SEG <= row))
        scores = jnp.where(allowed, scores, -1e30)
        e = jnp.exp(scores - jnp.max(scores, axis=-1, keepdims=True))
        return e / jnp.sum(e, axis=-1, keepdims=True)

    l_x = load(0, x_h, m.x)
    l_g = load(1, gains_h, m.gains)
    l_k = load(2, wk_h, m.wk)
    l_r = load(3, wr_h, m.wr)
    l_rt = load(4, rt_h, m.rt)
    l_sp = load(12, spread_h, m.spread)

    def forward(wv, wo):
        l_v = load(5, wv_h, wv)
        l_ev = load(6, exv_h, m.exv)
        l_sel = load(7, sel_h, m.sel)
        l_x.wait()
        l_g.wait()

        def norm1(rows):
            unit, _ = unit_rows(m.x[rows, :].astype(F32))
            m.xn[rows, :] = (unit * m.gains[0:1, :].astype(F32)).astype(BF)
        for_rows(32, norm1)
        l_k.wait()
        m.k[own, :] = dot_nt(m.xn[...], m.wk[...]).astype(BF)
        l_q = load(8, wq_h, m.wq)
        l_oc = load(9, oc_h, m.oc)
        l_eo = load(10, exo_h, m.exo)
        l_wo = load(11, wo_h, wo)
        for j in range(2):
            for cp in ff_loads(j):
                cp.start()
        pl.semaphore_wait(bar, peers)

        @pl.when(t < last_t)
        def _():
            k_copy().start()
        l_r.wait()
        m.wrp[...] = jnp.zeros((128, D), BF)
        m.wrp[LOGIT:LOGIT + 2 * H * E, :] = m.wr[...]
        sig = jax.nn.sigmoid(dot_nt(m.xn[...], m.wrp[...]))
        l_rt.wait()
        l_sp.wait()
        m.rf[...] = jnp.zeros((128, SEG), BF)
        for i in range(2):
            m.rf[16 * i:16 * i + 2 * H, :] = m.rt[:, i, :].astype(F32).astype(BF)
        named = dot_tn(m.rf[...], m.spread[...])
        expert = m.spread[127:128, :128].astype(F32)
        hit = (named[:, :128] == expert) | (named[:, 128:] == expert)
        m.hot[...] = jnp.where(hit, 1.0, 0.0)
        m.sig[...] = sig
        top, low = halves(sig * m.hot[...])
        m.gg[:, :128] = top
        m.gg[:, 128:] = low
        l_v.wait()
        l_ev.wait()
        l_sel.wait()
        m.acc[mem, :] = jnp.zeros((SEG, HD), F32)

        def values(cols, _):
            top, low = halves(dot_nt(m.xn[...], wv[cols, :]) * gates_wide(m.exv, cols))
            m.acc[mem, :] += dot(top, m.sel[cols, :HD]) + dot(low, m.sel[cols, :HD])
        for_wide(values)
        m.v[own, :] = m.acc[mem, :].astype(BF)

        @pl.when(t < last_t)
        def _():
            v_copy().start()
        l_q.wait()
        m.q[...] = dot_nt(m.xn[...], m.wq[...]).astype(BF)
        l_oc.wait()
        turn(0, 0, m.oc[...])
        turn(3, 1, m.xn[...])

        @pl.when(t > 0)
        def _():
            k_copy().wait_recv()
            v_copy().wait_recv()

        @pl.when(t == 0)
        def _():
            m.k[mem, :] = jnp.zeros((SEG, HD), BF)
            m.v[mem, :] = jnp.zeros((SEG, HD), BF)
        m.acc[mem, :] = jnp.zeros((SEG, HD), F32)

        def attend(h, _):
            m.acc[mem, :] += dot(weights_of(h).astype(BF), head_only(m.v[...], h))
            return 0
        lax.fori_loop(0, H, attend, 0)
        m.att[...] = m.acc[mem, :].astype(BF)
        m.g_o[mem, 2176:2304] = jnp.zeros((SEG, 128), BF)
        l_eo.wait()

        def mixing(cols, _):
            m.g_o[mem, cols] = (gates_wide(m.exo, cols) * dot_nt(m.att[...], m.sel[cols, :HD])).astype(BF)
        for_wide(mixing)
        go_copy().start()
        l_wo.wait()
        m.mid[...] = m.x[...].astype(F32) + dot(m.g_o[mem, :WIDE], wo[...])

        def norm2(rows):
            unit, _ = unit_rows(m.mid[rows, :])
            m.hn[rows, :] = (unit * m.gains[1:2, :].astype(F32)).astype(BF)
        for_rows(32, norm2)
        at_copy(0, 0).wait_send()
        turn(1, 0, m.hn[...])

    pl.run_scoped(forward, pltpu.VMEM((WIDE, D), BF), pltpu.VMEM((WIDE, D), BF))

    def backward(parts):
        ex = Exchange(parts, recv, (m.ssem, m.rsem), m.stage, m.out_sem, flat_h)

        def product(i, g):
            return dot(m.at[i].reshape(512, 2 * SEG), g)

        def tiles(i, g, tile):
            acc = product(i, g)
            for k in range(acc.shape[1] // TILE):
                store_tile(parts, tile + k, acc[:, k * TILE:(k + 1) * TILE])

        def two(i):
            return pl.ds(pl.multiple_of(i * 2 * TILE, 2 * TILE), 2 * TILE)

        m.lo[...] = m.mid[...]
        m.nsc[...] = jnp.zeros((SEG, D), F32)
        at_copy(0, 0).wait_recv()
        at_copy(1, 0).wait_recv()

        def block(j, _):
            b = rem(j, 2)
            g = rem(j, NG)
            for cp in ff_loads(j):
                cp.wait()
            pre = dot(m.hn[...], m.wu[b])
            cdf = 0.5 * (1.0 + lax.erf(pre * 0.7071067811865476))
            pdf = jnp.exp(-0.5 * pre * pre) * 0.3989422804014327
            up = dot_nt(m.oc[...], m.wd[b])

            @pl.when(j >= NG)
            def _():
                for cp in ff_copies(j - NG):
                    cp.wait_send()
            m.act[g, mem] = (pre * cdf).astype(BF)
            m.uc[g, mem] = (up * (cdf + pre * pdf)).astype(BF)
            for cp in ff_copies(j):
                cp.start()

            @pl.when(j > 1)
            def _():
                weights_grad(j - 1)
            m.lo[...] += dot(m.act[g, mem], m.wd[b])
            m.nsc[...] += dot_nt(m.uc[g, mem], m.wu[b])

            @pl.when(j + 2 < NFF)
            def _():
                for cp in ff_loads(j + 2):
                    cp.start()

            @pl.when(j == 0)
            def _():
                weights_grad(0)
                ex.step1_ab(0)

            @pl.when((lax.rem(j, 2) == 0) & (j > 0))
            def _():
                ex.tick(j // 2 - 1)
            return 0

        def weights_grad(j):
            for cp in ff_copies(j):
                cp.wait_recv()
            tiles(0, m.act[rem(j, NG)], 8 * j)
            tiles(1, m.uc[rem(j, NG)], 8 * j + 4)
        lax.fori_loop(0, NFF, block, 0)
        weights_grad(NFF - 1)
        ex.tick(3)
        for j in range(NFF - NG, NFF):
            for cp in ff_copies(j):
                cp.wait_send()
        m.ob[...] = m.lo[...].astype(BF)
        l_lo = pltpu.make_async_copy(m.ob, lo_h, m.st.at[0])
        l_lo.start()

        def norm2_back(rows):
            unit, inv = unit_rows(m.mid[rows, :])
            cot = m.nsc[rows, :]
            mcot = m.oc[rows, :].astype(F32) + norm_back(unit, inv, cot * m.gains[1:2, :].astype(F32))
            m.lo[rows, :] = mcot
            m.bc[rows, :] = mcot.astype(BF)
            m.hn[rows, :] = (cot * unit).astype(BF)
        for_rows(32, norm2_back)
        at_copy(3, 1).wait_send()
        turn(2, 1, m.bc[...])
        at_copy(1, 0).wait_send()
        turn(5, 0, m.hn[...])
        go_copy().wait_recv()
        at_copy(2, 1).wait_recv()

        def out_grad(i, _):
            tiles(2, m.g_o[:, two(i)], 64 + 2 * i)
            return 0
        lax.fori_loop(0, 9, out_grad, 0)
        ex.tick(4)

        def through_output(wo):
            load(11, wo_h, wo).wait()
            m.acc[mem, :] = jnp.zeros((SEG, HD), F32)
            m.ogc[...] = jnp.zeros((SEG, 128), F32)

            def mixed(cols, _):
                cot = dot_nt(m.bc[...], wo[cols, :])
                seen = (cot * dot_nt(m.att[...], m.sel[cols, :HD])).astype(BF)
                m.ogc[...] += dot_nt(seen, m.exo[:128, cols])
                chosen = (cot * gates_wide(m.exo, cols)).astype(BF)
                m.acc[mem, :] += dot(chosen, m.sel[cols, :HD])
            for_wide(mixed)
            m.att[...] = m.acc[mem, :].astype(BF)
        pl.run_scoped(through_output, pltpu.VMEM((WIDE, D), BF))
        ex.tick(5)

        def values_back(h, _):
            probs = weights_of(h)
            cot = head_only(m.att[...], h)
            m.acc[...] += dot_tn(probs.astype(BF), cot)
            return 0

        m.acc[...] = jnp.zeros((2 * SEG, HD), F32)
        lax.fori_loop(0, H, values_back, 0)
        m.vc[...] = m.acc[...].astype(BF)

        @pl.when(t > 0)
        def _():
            vc_copy().start()
        ex.tick(6)
        m.acc[...] = jnp.zeros((2 * SEG, HD), F32)
        m.qc[...] = jnp.zeros((SEG, HD), F32)

        def scores_back(h, _):
            probs = weights_of(h)
            pc = dot_nt(head_only(m.att[...], h), m.v[...])
            sc = (probs * (pc - jnp.sum(probs * pc, axis=-1, keepdims=True))).astype(BF)
            m.qc[...] += dot(sc, head_only(m.k[...], h)) * scale
            m.acc[...] += dot_tn(sc, head_only(m.q[...], h)) * scale
            return 0
        lax.fori_loop(0, H, scores_back, 0)
        m.kc[...] = m.acc[...].astype(BF)

        @pl.when(t > 0)
        def _():
            kc_copy().start()
        m.g_p[mem, HD:512] = jnp.zeros((SEG, 512 - HD), BF)
        m.g_p[mem, 512 + HD:1024] = jnp.zeros((SEG, 512 - HD), BF)
        m.g_p[mem, :HD] = m.qc[...].astype(BF)
        ex.tick(7)

        @pl.when(t < last_t)
        def _():
            vc_copy().wait_recv()
            kc_copy().wait_recv()

        @pl.when(t == last_t)
        def _():
            m.kn[...] = jnp.zeros((SEG, HD), BF)
            m.vn[...] = jnp.zeros((SEG, HD), BF)
        m.g_p[mem, 512:512 + HD] = (m.kc[own, :].astype(F32) + m.kn[...].astype(F32)).astype(BF)
        l_lo.wait()

        own_cot, next_cot = m.mid, m.nsc

        def through_values(wv, vg):
            load(5, wv_h, wv).wait()
            own_cot[...] = dot(m.kc[own, :], m.wk[...]) + dot(m.g_p[mem, :HD], m.wq[...])
            next_cot[...] = dot(m.kn[...], m.wk[...])
            vg[...] = jnp.zeros((2, SEG, 128), F32)

            def values(cols, lo):
                proj = dot_nt(m.xn[...], wv[cols, :])
                gate = gates_wide(m.exv, cols)
                vo = dot_nt(m.vc[own, :], m.sel[cols, :HD])
                vn = dot_nt(m.vn[...], m.sel[cols, :HD])
                for i, v in enumerate((vo, vn)):
                    vg[i] += dot_nt((v * proj).astype(BF), m.exv[:128, cols])
                po = (gate * vo).astype(BF)
                pn = (gate * vn).astype(BF)
                own_cot[...] += dot(po, wv[cols, :])
                next_cot[...] += dot(pn, wv[cols, :])
                both = (po.astype(F32) + pn.astype(F32)).astype(BF)
                if isinstance(lo, int):
                    m.g_p[mem, 1024 + lo:1024 + WIDE] = both
                else:
                    m.g_p[mem, pl.ds(pl.multiple_of(1024 + lo, WB), WB)] = both
            for_wide(values)
            slope = m.sig[...] * (1.0 - m.sig[...]) * m.hot[...]
            lo_cot = ((vg[0] + m.ogc[...]) * slope).astype(BF)
            ln_cot = (vg[1] * slope).astype(BF)
            own_cot[...] += dot(lo_cot, m.wrp[...])
            next_cot[...] += dot(ln_cot, m.wrp[...])
            both = (lo_cot.astype(F32) + ln_cot.astype(F32)).astype(BF)
            lane = lax.broadcasted_iota(jnp.int32, (SEG, 128), 1)
            m.g_p[mem, 3200:3328] = jnp.where(lane < LOGIT, m.g_p[mem, 3200:3328], both)
            gp_copy().start()

            def norm1_back(rows):
                unit, inv = unit_rows(m.x[rows, :].astype(F32))
                cot = own_cot[rows, :]
                m.lo[rows, :] += norm_back(unit, inv, cot * m.gains[0:1, :].astype(F32))
                m.hn[rows, :] = ((cot + next_cot[rows, :]) * unit).astype(BF)
            for_rows(32, norm1_back)
        pl.run_scoped(through_values, pltpu.VMEM((WIDE, D), BF), pltpu.VMEM((2, SEG, 128), F32))
        l_ig = pltpu.make_async_copy(m.lo, ig_h, m.st.at[1])
        l_ig.start()
        at_copy(2, 1).wait_send()
        turn(4, 1, m.hn[...])
        ex.tick(8)
        gp_copy().wait_recv()
        at_copy(3, 1).wait_recv()

        def proj_grad(i, _):
            tiles(3, m.g_p[:, two(i)], 82 + 2 * i)
            return 0
        lax.fori_loop(0, 12, proj_grad, 0)
        last = product(3, m.g_p[:, 3072:3328])
        store_tile(parts, 106, last[:, :TILE])
        last = last[:, TILE:]
        lane = lax.broadcasted_iota(jnp.int32, (2 * SEG, TILE), 1)
        at_copy(5, 0).wait_recv()
        at_copy(4, 1).wait_recv()
        for i, at in ((4, 104), (5, 105)):
            last += product(i, jnp.where(lane == at, 1.0, 0.0).astype(BF))
        store_tile(parts, 107, last)

        def run(i, _):
            ex.tick(i)
            return 0
        lax.fori_loop(9, NS + 5, run, 0)
        ex.finish()
        l_ig.wait()

    pl.run_scoped(backward, *P_SCRATCH)
    at_copy(5, 0).wait_send()
    at_copy(4, 1).wait_send()
    go_copy().wait_send()
    gp_copy().wait_send()

    @pl.when(t < last_t)
    def _():
        k_copy().wait_send()
        v_copy().wait_send()

    @pl.when(t > 0)
    def _():
        kc_copy().wait_send()
        vc_copy().wait_send()


def tables():
    col = np.arange(WIDE)
    sel = (col // (E * DH) * DH + col % DH)[:, None] == np.arange(HD)[None, :]
    branch = np.arange(128)[:, None]
    exv = branch == LOGIT + col[None, :] // DH
    exo = branch == LOGIT + H * E + col[None, :] // DH
    exv, exo = (np.concatenate([v, v]) for v in (exv, exo))
    sel = np.pad(sel, ((0, 0), (0, 512 - HD)))
    exv, exo = (np.pad(v, ((0, 0), (0, 2304 - WIDE))) for v in (exv, exo))
    lane = np.arange(128) - LOGIT
    inside = (lane >= 0) & (lane < 2 * H * E)
    pick = (np.arange(2 * H)[:, None] == lane[None, :] // E) & inside
    spread = np.zeros((128, 256), np.float32)
    spread[:2 * H, :128] = pick
    spread[16:16 + 2 * H, 128:] = pick
    spread[127, :128] = np.where(inside, lane % E, -1)
    return tuple(v.astype(ml_dtypes.bfloat16) for v in (sel, exv, exo, spread))


def fused_device(layer_input, routes, memory_lengths, norm_gains, w_query, w_key, w_value,
                 w_router, w_output, w_up, w_down, output_cot):
    anywhere = pl.BlockSpec(memory_space=pl.ANY)
    specs = [anywhere] * 16
    specs[2] = pl.BlockSpec(memory_space=pltpu.SMEM)
    out, grad, flat = pl.pallas_call(
        layer_kernel,
        out_shape=(jax.ShapeDtypeStruct((SEG, D), BF), jax.ShapeDtypeStruct((SEG, D), F32),
                   jax.ShapeDtypeStruct((32, FLAT), F32)),
        in_specs=specs,
        out_specs=(anywhere,) * 3,
        scratch_shapes=layer_scratch() + RECV_SCRATCH,
        compiler_params=pltpu.CompilerParams(
            collective_id=0, has_side_effects=True, vmem_limit_bytes=VMEM_LIMIT),
        name="layer",
    )(layer_input[0], jnp.transpose(routes[0], (1, 2, 0)), memory_lengths, norm_gains, w_query.T, w_key.T, w_value.T, w_router.T,
      w_output, w_up, w_down, output_cot[0], *tables())
    shapes = ((SEG, D), BF), ((SEG, D), F32), ((2, 32), F32), ((32, HD), F32), ((32, HD), F32), \
        ((32, WIDE), F32), ((32, 2 * H * E), F32), ((32, WIDE), F32), ((32, FF), F32), ((32, FF), F32)
    vm = pl.BlockSpec(memory_space=pltpu.VMEM)
    res = pl.pallas_call(
        split_kernel,
        out_shape=tuple(jax.ShapeDtypeStruct(*v) for v in shapes),
        in_specs=(anywhere, anywhere, anywhere),
        out_specs=(vm,) * 10,
        scratch_shapes=[pltpu.VMEM((32, FLAT), F32), pltpu.SemaphoreType.DMA((3,))],
        compiler_params=pltpu.CompilerParams(vmem_limit_bytes=VMEM_LIMIT),
        name="split",
    )(out, grad, flat)
    return (res[0][None], res[1][None], *res[2:7], res[7].T, res[8], res[9].T)


def split_kernel(out_h, grad_h, flat_h, lo, ig, gains, dq, dk, dv, dr, do, du, dd, flat, sem):
    copies = [pltpu.make_async_copy(flat_h, flat, sem.at[2]), pltpu.make_async_copy(out_h, lo, sem.at[0]),
              pltpu.make_async_copy(grad_h, ig, sem.at[1])]
    for cp in copies:
        cp.start()
    copies.pop(0).wait()
    for j in range(NFF):
        dd[:, j * FFB:(j + 1) * FFB] = flat[:, 2 * j * FFB:(2 * j + 1) * FFB]
        du[:, j * FFB:(j + 1) * FFB] = flat[:, (2 * j + 1) * FFB:(2 * j + 2) * FFB]
    do[...] = flat[:, 2 * FF:2 * FF + WIDE]
    base = 82 * TILE
    dq[...] = flat[:, base:base + HD]
    dk[...] = flat[:, base + 512:base + 512 + HD]
    dv[...] = flat[:, base + 1024:base + 1024 + WIDE]
    tail = flat[:, 107 * TILE:108 * TILE]
    dr[...] = tail[:, LOGIT:LOGIT + 2 * H * E]
    gains[...] = jnp.transpose(tail)[104:106, :]
    for cp in copies:
        cp.wait()


def solution(mesh):
    placed = (
        P("seq", "tm", None),
        P("seq", "tm", None, None),
        P("seq", "tm"),
        P(),
        P(),
        P(),
        P(),
        P(),
        P(),
        P(),
        P(),
        P("seq", "tm", None),
    )
    fused = mesh.shape["seq"] == 2 and mesh.shape["tm"] == 16
    return jax.shard_map(
        fused_device if fused else per_device,
        mesh=mesh,
        in_specs=placed,
        out_specs=(
            P("seq", "tm", None),
            P("seq", "tm", None),
            P(None, ("seq", "tm")),
            P(("seq", "tm"), None),
            P(("seq", "tm"), None),
            P(("seq", "tm"), None),
            P(("seq", "tm"), None),
            P(None, ("seq", "tm")),
            P(("seq", "tm"), None),
            P(None, ("seq", "tm")),
        ),
        check_vma=False,
    )
```

```python
import types

import jax
import jax.numpy as jnp
import ml_dtypes
import numpy as np
from jax import lax
from jax.experimental import pallas as pl
from jax.experimental.pallas import tpu as pltpu
from jax.sharding import PartitionSpec as P

H = 4
DH = 112
E = 5


epsilon = 1e-05


def passed_along(value, axis, steps):
    count = lax.axis_size(axis)
    initial, last = (max(0, -steps), min(count, count - steps))
    return lax.ppermute(value, axis, [(source, source + steps) for source in range(initial, last)])


def normalize(values, gain_vec):
    centre = values - jnp.mean(values, axis=-1, keepdims=True)
    spread = jnp.mean(centre * centre, axis=-1, keepdims=True)
    return centre * lax.rsqrt(spread + epsilon) * gain_vec


def exact_gelu(arg_in):
    return jax.nn.gelu(arg_in, approximate=False)


def matmul(left_op, right_op):
    return jnp.dot(left_op, right_op, preferred_element_type=jnp.float32)


def times_tr(left_op, right_op):
    return lax.dot_general(
        left_op, right_op, (((1,), (1,)), ((), ())), preferred_element_type=jnp.float32
    )


def tr_times(left_op, right_op):
    return lax.dot_general(
        left_op, right_op, (((0,), (0,)), ((), ())), preferred_element_type=jnp.float32
    )


def one_hot_routes(route_ids):
    return jnp.sum(
        (route_ids[..., None] == jnp.arange(E, dtype=jnp.int32)).astype(jnp.float32), axis=-2
    )


def attention_mask(memory_length, seg_len):
    query_pos = jnp.arange(seg_len, dtype=jnp.int32)[:, None]
    key_pos = jnp.arange(2 * seg_len, dtype=jnp.int32)[None, :]
    return jnp.where(
        key_pos < seg_len, key_pos >= seg_len - memory_length, key_pos - seg_len <= query_pos
    )


def per_device(
    layer_input,
    routes,
    memory_lengths,
    norm_gains,
    w_query,
    w_key,
    w_value,
    w_router,
    w_output,
    w_up,
    w_down,
    output_cot,
):
    seg_len = layer_input.shape[1]
    own_rows = layer_input[0].astype(jnp.float32)
    memory_length = memory_lengths[0, 0]
    gains_f = norm_gains.astype(jnp.float32)
    first_gain = gains_f[0]
    second_gain = gains_f[1]
    scale_factor = DH ** (-0.5)
    allowed = attention_mask(memory_length, seg_len)
    onehot = one_hot_routes(routes[0])
    unit_normed = normalize(own_rows, jnp.ones_like(first_gain))
    own_normed = (unit_normed * first_gain).astype(jnp.bfloat16)

    def projections():
        queries = matmul(own_normed, w_query).astype(jnp.bfloat16)
        key_own = matmul(own_normed, w_key).astype(jnp.bfloat16)
        logits = matmul(own_normed, w_router).reshape(seg_len, 2 * H, E)
        gate_sig = jax.nn.sigmoid(logits)
        gate_vals = gate_sig * onehot
        projected = matmul(own_normed, w_value).reshape(seg_len, H, E, DH)
        value_own = (
            jnp.sum(gate_vals[:, :H, :, None] * projected, axis=2)
            .reshape(seg_len, H * DH)
            .astype(jnp.bfloat16)
        )
        return (queries, key_own, gate_sig, gate_vals, projected, value_own)

    queries, key_own, gate_sig, gate_vals, projected, value_own = projections()
    key_mem, value_mem = passed_along((key_own, value_own), "tm", 1)
    key_rows = jnp.concatenate([key_mem, key_own], axis=0)
    value_rows = jnp.concatenate([value_mem, value_own], axis=0)
    head_outs = []
    log_norms = []
    for head_idx in range(H):
        columns = slice(head_idx * DH, (head_idx + 1) * DH)
        scores = (
            jnp.einsum(
                "qd,kd->qk",
                queries[:, columns],
                key_rows[:, columns],
                preferred_element_type=jnp.float32,
            )
            * scale_factor
        )
        scores = jnp.where(allowed, scores, -1e30)
        peak = jnp.max(scores, axis=-1, keepdims=True)
        exp_scores = jnp.exp(scores - peak)
        total = jnp.sum(exp_scores, axis=-1, keepdims=True)
        weights = (exp_scores / total).astype(jnp.bfloat16)
        head_outs.append(matmul(weights, value_rows[:, columns]))
        log_norms.append(peak + jnp.log(total))
    attended = jnp.concatenate(head_outs, axis=1).astype(jnp.bfloat16)
    out_gates = gate_vals[:, H:]
    attended_f = attended.astype(jnp.float32).reshape(seg_len, H, 1, DH)
    mixed_in = (attended_f * out_gates[..., None]).reshape(seg_len, H * E * DH).astype(jnp.bfloat16)
    middle = own_rows + matmul(mixed_in, w_output)
    hidden_normed = normalize(middle, second_gain).astype(jnp.bfloat16)
    pre_act = matmul(hidden_normed, w_up)
    activated = exact_gelu(pre_act).astype(jnp.bfloat16)
    layer_out = middle + matmul(activated, w_down)
    output_block = layer_out.astype(jnp.bfloat16)[None]
    down_cot = output_cot[0]
    out_cot = down_cot.astype(jnp.float32)
    grad_down = tr_times(activated, down_cot)
    grad_act = times_tr(down_cot, w_down)
    unused_gelu, gelu_pull = jax.vjp(exact_gelu, pre_act)
    up_cot = gelu_pull(grad_act)[0].astype(jnp.bfloat16)
    grad_up = tr_times(hidden_normed, up_cot)
    normed_second_cot = times_tr(up_cot, w_up)
    unused_norm, second_pull = jax.vjp(normalize, middle, second_gain)
    middle_part, grad_second = second_pull(normed_second_cot)
    middle_cot = out_cot + middle_part
    branch_cot = middle_cot.astype(jnp.bfloat16)
    grad_output = tr_times(mixed_in, branch_cot)
    mixed_cot = times_tr(branch_cot, w_output).reshape(seg_len, H, E, DH)
    out_gate_cot = jnp.sum(mixed_cot * attended_f, axis=-1)
    attended_cot = (
        jnp.sum(mixed_cot * out_gates[..., None], axis=2)
        .reshape(seg_len, H * DH)
        .astype(jnp.bfloat16)
    )
    queries, key_own, gate_sig, gate_vals, projected, value_own = projections()
    key_back, value_back = passed_along((key_own, value_own), "tm", 1)
    key_rows = jnp.concatenate([key_back, key_own], axis=0)
    value_rows = jnp.concatenate([value_back, value_own], axis=0)
    query_grads = []
    key_grads = []
    value_grads = []
    for head_idx in range(H):
        columns = slice(head_idx * DH, (head_idx + 1) * DH)
        scores = (
            jnp.einsum(
                "qd,kd->qk",
                queries[:, columns],
                key_rows[:, columns],
                preferred_element_type=jnp.float32,
            )
            * scale_factor
        )
        scores = jnp.where(allowed, scores, -1e30)
        probs = jnp.exp(scores - log_norms[head_idx])
        weights = probs.astype(jnp.bfloat16)
        cot_head = attended_cot[:, columns]
        value_grads.append(tr_times(weights, cot_head))
        prob_cot = times_tr(cot_head, value_rows[:, columns])
        score_cot = (probs * (prob_cot - jnp.sum(probs * prob_cot, axis=-1, keepdims=True))).astype(
            jnp.bfloat16
        )
        query_grads.append(matmul(score_cot, key_rows[:, columns]) * scale_factor)
        key_grads.append(tr_times(score_cot, queries[:, columns]) * scale_factor)
    query_cot = jnp.concatenate(query_grads, axis=1).astype(jnp.bfloat16)
    key_cot_all = jnp.concatenate(key_grads, axis=1)
    value_cot_all = jnp.concatenate(value_grads, axis=1)
    key_mem_cot = key_cot_all[:seg_len].astype(jnp.bfloat16)
    key_own_cot = key_cot_all[seg_len:].astype(jnp.bfloat16)
    value_mem_cot = value_cot_all[:seg_len].astype(jnp.bfloat16)
    value_own_cot = value_cot_all[seg_len:].astype(jnp.bfloat16)
    key_next, value_next = passed_along((key_mem_cot, value_mem_cot), "tm", -1)
    own_vcot = value_own_cot.astype(jnp.float32).reshape(seg_len, H, 1, DH)
    next_vcot = value_next.astype(jnp.float32).reshape(seg_len, H, 1, DH)
    val_gates = gate_vals[:, :H, :, None]
    proj_own_cot = (val_gates * own_vcot).reshape(seg_len, H * E * DH).astype(jnp.bfloat16)
    proj_next_cot = (val_gates * next_vcot).reshape(seg_len, H * E * DH).astype(jnp.bfloat16)
    gate_own_cot = jnp.concatenate([jnp.sum(own_vcot * projected, axis=-1), out_gate_cot], axis=1)
    gate_next_cot = jnp.concatenate(
        [jnp.sum(next_vcot * projected, axis=-1), jnp.zeros_like(out_gate_cot)], axis=1
    )
    slope = gate_sig * (1.0 - gate_sig) * onehot
    logit_own_cot = (gate_own_cot * slope).reshape(seg_len, 2 * H * E).astype(jnp.bfloat16)
    logit_next_cot = (gate_next_cot * slope).reshape(seg_len, 2 * H * E).astype(jnp.bfloat16)
    twice_normed = jnp.concatenate([own_normed, own_normed], axis=0)
    key_both = jnp.concatenate([key_own_cot, key_next], axis=0)
    proj_both = jnp.concatenate([proj_own_cot, proj_next_cot], axis=0)
    logit_both = jnp.concatenate([logit_own_cot, logit_next_cot], axis=0)
    grad_query = tr_times(own_normed, query_cot)
    grad_key = tr_times(twice_normed, key_both)
    grad_value = tr_times(twice_normed, proj_both)
    grad_router = tr_times(twice_normed, logit_both)
    normed_both = (
        times_tr(key_both, w_key) + times_tr(proj_both, w_value) + times_tr(logit_both, w_router)
    )
    own_normed_cot = normed_both[:seg_len] + times_tr(query_cot, w_query)
    next_normed_cot = normed_both[seg_len:]
    grad_first = jnp.sum((own_normed_cot + next_normed_cot) * unit_normed, axis=0)
    unused_first, first_pull = jax.vjp(normalize, own_rows, first_gain)
    input_part = first_pull(own_normed_cot)[0]
    input_cot = middle_cot + input_part
    grad_gains = jnp.stack([grad_first, grad_second], axis=0)
    row_query, row_key, row_value, row_router, row_up = (
        lax.psum_scatter(grad_query, ("seq", "tm"), scatter_dimension=0, tiled=True),
        lax.psum_scatter(grad_key, ("seq", "tm"), scatter_dimension=0, tiled=True),
        lax.psum_scatter(grad_value, ("seq", "tm"), scatter_dimension=0, tiled=True),
        lax.psum_scatter(grad_router, ("seq", "tm"), scatter_dimension=0, tiled=True),
        lax.psum_scatter(grad_up, ("seq", "tm"), scatter_dimension=0, tiled=True),
    )
    col_gains, col_output, col_down = (
        lax.psum_scatter(grad_gains, ("seq", "tm"), scatter_dimension=1, tiled=True),
        lax.psum_scatter(grad_output, ("seq", "tm"), scatter_dimension=1, tiled=True),
        lax.psum_scatter(grad_down, ("seq", "tm"), scatter_dimension=1, tiled=True),
    )
    return (
        output_block,
        input_cot[None],
        col_gains,
        row_query,
        row_key,
        row_value,
        row_router,
        col_output,
        row_up,
        col_down,
    )


VMEM_LIMIT = 64 << 20

MESH_ID = pl.DeviceIdType.MESH
TILE = 128
PIECES = [(6, 2)] * 2 + [(7, 2)] * 8 + [(5, 2), (4, 1), (3, 1), (2, 0), (2, 0)]
NS = len(PIECES)
TILES = sum(a + b for a, b in PIECES)
FLAT = TILES * TILE
MOST_FIRST = max(a for a, _ in PIECES) * TILE
MOST_LAST = max(b for _, b in PIECES) * TILE
MOST = max(a + b for a, b in PIECES) * TILE
N1 = 6
NR = 4
NZ = 7
HALF = (slice(0, 16), slice(16, 32))


class Piece:
    def __init__(self, p):
        start = sum(a + b for a, b in PIECES[:p]) * TILE
        self.p, self.f, self.r, self.q = p, p % N1, p % NR, p % NZ
        self.wf, self.wl = (v * TILE for v in PIECES[p])
        self.first = slice(start, start + self.wf)
        self.last = slice(start + self.wf, start + self.wf + self.wl)
        self.all = slice(start, start + self.wf + self.wl)


def place():
    s = lax.axis_index("seq")
    t = lax.axis_index("tm")
    return s, t, t // 4, (t // 2) % 2, t % 2


def rem(a, n):
    return a % n if isinstance(a, int) else lax.rem(a, n)


def store_tile(parts, tile, value):
    at = tile * TILE
    width = value.shape[1]
    cols = slice(at, at + width) if isinstance(at, int) else pl.ds(pl.multiple_of(at, TILE), width)
    parts[:, :, :, :, cols] = value.reshape(2, 4, 2, 32, width).astype(jnp.bfloat16)


class Exchange:
    def __init__(self, parts, bufs, sems, stage, out_sem, out):
        self.parts, self.out = parts, out
        self.stage, self.out_sem = stage, out_sem
        (self.xa, self.yb, self.ya, self.xb, self.zu, self.zd, self.zuc, self.zdc, self.xc, self.yc) = bufs
        self.ssem, self.rsem = sems
        self.s, self.t, self.z, self.y, self.c = place()
        s, t = self.s, self.t
        self.to_x = {"seq": 1 - s, "tm": t}
        self.to_y = {"seq": s, "tm": t + 2 - 4 * self.y}
        self.to_up = {"seq": s, "tm": t + 4}
        self.to_down = {"seq": s, "tm": t - 4}

    def copy(self, kind, g, src, dst, dev):
        return pltpu.make_async_remote_copy(
            src_ref=src, dst_ref=dst, send_sem=self.ssem.at[kind, g.p],
            recv_sem=self.rsem.at[kind, g.p], device_id=dev, device_id_type=MESH_ID)

    def c_xa(self, g):
        return self.copy(0, g, self.parts.at[1 - self.s, :, :, HALF[0], g.first], self.xa.at[g.f, :, :, :, :g.wf], self.to_x)

    def c_yb(self, g):
        return self.copy(1, g, self.parts.at[:, :, 1 - self.y, HALF[1], g.first], self.yb.at[g.f, :, :, :, :g.wf], self.to_y)

    def c_ya(self, g):
        return self.copy(2, g, self.parts.at[self.s, :, 1 - self.y, HALF[0], g.first], self.ya.at[g.r, :, :, :g.wf], self.to_y)

    def c_xb(self, g):
        return self.copy(3, g, self.parts.at[1 - self.s, :, self.y, HALF[1], g.first], self.xb.at[g.r, :, :, :g.wf], self.to_x)

    def c_xc(self, g):
        return self.copy(4, g, self.parts.at[1 - self.s, self.z, :, :, g.last], self.xc.at[g.r, :, :, :g.wl], self.to_x)

    def c_yc(self, g):
        return self.copy(5, g, self.parts.at[self.s, self.z, 1 - self.y, :, g.last], self.yc.at[g.r, :, :g.wl], self.to_y)

    def c_up(self, g, z):
        return self.copy(6, g, self.parts.at[self.s, z + 1:4, self.y, :, g.first], self.zu.at[g.q, z:3, :, :g.wf], self.to_up)

    def c_down(self, g, z):
        return self.copy(7, g, self.parts.at[self.s, 0:z, self.y, :, g.first], self.zd.at[g.q, 0:z, :, :g.wf], self.to_down)

    def c_upc(self, g, z):
        return self.copy(8, g, self.parts.at[:, z + 1:4, :, :, g.last], self.zuc.at[g.q, :, z:3, :, :, :g.wl], self.to_up)

    def c_downc(self, g, z):
        return self.copy(9, g, self.parts.at[:, 0:z, :, :, g.last], self.zdc.at[g.q, :, 0:z, :, :, :g.wl], self.to_down)

    def add(self, at, cols, value):
        self.parts[(*at, cols)] = self.parts[(*at, cols)] + value

    def z_step(self, g, k, is_c):
        if is_c and not g.wl:
            return
        up, down = (self.c_upc, self.c_downc) if is_c else (self.c_up, self.c_down)
        rows = slice(None)

        def add(u, src, at):
            if is_c:
                def body(i, _):
                    a, b = i // 2, i % 2
                    self.add((a, u, b, rows), g.last, src[g.q, a, at, b, :, :g.wl])
                    return 0
                lax.fori_loop(0, 4, body, 0)
            else:
                self.add((self.s, u, self.y, rows), g.first, src[g.q, at, :, :g.wf])

        @pl.when(self.z == k - 1)
        def _():
            z = k - 1
            if z > 0:
                up(g, z - 1).wait_recv()
                for u in range(z + 1, 4):
                    add(u, self.zuc if is_c else self.zu, u - 1)
            if z < 3:
                up(g, z).start()

        @pl.when(self.z == 4 - k)
        def _():
            z = 4 - k
            if z < 3:
                down(g, z + 1).wait_recv()
                for u in range(0, z):
                    add(u, self.zdc if is_c else self.zd, u)
            if z > 0:
                down(g, z).start()

    def step1(self, g):
        self.c_xa(g).start()
        self.c_yb(g).start()
        self.z_step(g, 1, True)

    def step2(self, g):
        self.c_xa(g).wait_recv()

        def body(i, _):
            a, b = i // 2, i % 2
            self.add((self.s, a, b, HALF[0]), g.first, self.xa[g.f, a, b, :, :g.wf])
            return 0
        lax.fori_loop(0, 8, body, 0)
        self.c_ya(g).start()
        self.c_yb(g).wait_recv()

        def body(i, _):
            a, b = i // 4, i % 4
            self.add((a, b, self.y, HALF[1]), g.first, self.yb[g.f, a, b, :, :g.wf])
            return 0
        lax.fori_loop(0, 8, body, 0)
        self.c_xb(g).start()
        self.z_step(g, 2, True)

    def step3(self, g):
        self.c_ya(g).wait_recv()
        self.c_xb(g).wait_recv()

        def body(b, _):
            self.add((self.s, b, self.y, HALF[0]), g.first, self.ya[g.r, b, :, :g.wf])
            self.add((self.s, b, self.y, HALF[1]), g.first, self.xb[g.r, b, :, :g.wf])
            return 0
        lax.fori_loop(0, 4, body, 0)
        self.z_step(g, 1, False)
        self.z_step(g, 3, True)

    def step4(self, g):
        self.z_step(g, 2, False)
        if not g.wl:
            return
        self.z_step(g, 4, True)
        z = self.z
        rows = slice(None)

        @pl.when(z > 0)
        def _():
            def body(i, _):
                a, b = i // 2, i % 2
                self.add((a, z, b, rows), g.last, self.zuc[g.q, a, z - 1, b, :, :g.wl])
                return 0
            lax.fori_loop(0, 4, body, 0)

        @pl.when(z < 3)
        def _():
            def body(i, _):
                a, b = i // 2, i % 2
                self.add((a, z, b, rows), g.last, self.zdc[g.q, a, z, b, :, :g.wl])
                return 0
            lax.fori_loop(0, 4, body, 0)
        self.c_xc(g).start()

    def step5(self, g):
        self.z_step(g, 3, False)
        if not g.wl:
            return
        self.c_xc(g).wait_recv()
        for b in range(2):
            self.add((self.s, self.z, b, slice(None)), g.last, self.xc[g.r, b, :, :g.wl])
        self.c_yc(g).start()

    def step6(self, g):
        self.z_step(g, 4, False)
        z = self.z
        k = g.p % 2
        if g.p >= 2:
            self.c_out(Piece(g.p - 2)).wait()
        mine = self.parts[self.s, z, self.y, :, g.first].astype(jnp.float32)

        @pl.when(z == 0)
        def _():
            self.stage[k, :, :g.wf] = mine + self.zd[g.q, 0, :, :g.wf].astype(jnp.float32)

        @pl.when(z == 3)
        def _():
            self.stage[k, :, :g.wf] = mine + self.zu[g.q, 2, :, :g.wf].astype(jnp.float32)

        @pl.when((z > 0) & (z < 3))
        def _():
            self.stage[k, :, :g.wf] = ((mine + self.zu[g.q, z - 1, :, :g.wf].astype(jnp.float32))
                                       + self.zd[g.q, z, :, :g.wf].astype(jnp.float32))
        if g.wl:
            self.c_yc(g).wait_recv()
            self.stage[k, :, g.wf:g.wf + g.wl] = (self.parts[self.s, z, self.y, :, g.last].astype(jnp.float32)
                                                  + self.yc[g.r, :, :g.wl].astype(jnp.float32))
        self.c_out(g).start()

    def c_out(self, g):
        k = g.p % 2
        return pltpu.make_async_copy(self.stage.at[k, :, :g.wf + g.wl], self.out.at[:, g.all], self.out_sem.at[k])

    def tick(self, t):
        steps = (self.step2, self.step3, self.step4, self.step5, self.step6)
        for k, step in enumerate(steps):
            if 0 <= t - 1 - k < NS:
                step(Piece(t - 1 - k))

    def begin(self, p):
        if p < NS:
            self.step1(Piece(p))

    def finish(self):
        self.c_out(Piece(NS - 2)).wait()
        self.c_out(Piece(NS - 1)).wait()
        for p in range(NS):
            g = Piece(p)
            self.c_xa(g).wait_send()
            self.c_yb(g).wait_send()
            self.c_ya(g).wait_send()
            self.c_xb(g).wait_send()
            if g.wl:
                self.c_xc(g).wait_send()
                self.c_yc(g).wait_send()
        for z in range(4):
            @pl.when(self.z == z)
            def _(z=z):
                for p in range(NS):
                    g = Piece(p)
                    if z < 3:
                        self.c_up(g, z).wait_send()
                        if g.wl:
                            self.c_upc(g, z).wait_send()
                    if z > 0:
                        self.c_down(g, z).wait_send()
                        if g.wl:
                            self.c_downc(g, z).wait_send()


P_SCRATCH = [pltpu.VMEM((2, 4, 2, 32, FLAT), jnp.bfloat16)]
RECV_SCRATCH = [
    pltpu.VMEM((N1, 4, 2, 16, MOST_FIRST), jnp.bfloat16),
    pltpu.VMEM((N1, 2, 4, 16, MOST_FIRST), jnp.bfloat16),
    pltpu.VMEM((NR, 4, 16, MOST_FIRST), jnp.bfloat16),
    pltpu.VMEM((NR, 4, 16, MOST_FIRST), jnp.bfloat16),
    pltpu.VMEM((NZ, 3, 32, MOST_FIRST), jnp.bfloat16),
    pltpu.VMEM((NZ, 3, 32, MOST_FIRST), jnp.bfloat16),
    pltpu.VMEM((NZ, 2, 3, 2, 32, MOST_LAST), jnp.bfloat16),
    pltpu.VMEM((NZ, 2, 3, 2, 32, MOST_LAST), jnp.bfloat16),
    pltpu.VMEM((NR, 2, 32, MOST_LAST), jnp.bfloat16),
    pltpu.VMEM((NR, 32, MOST_LAST), jnp.bfloat16),
]

def greet():
    s, t, z, y, c = place()
    bar = pltpu.get_barrier_semaphore()

    def tell(dev):
        pl.semaphore_signal(bar, inc=1, device_id=dev, device_id_type=MESH_ID)
    tell({"seq": 1 - s, "tm": t})
    tell({"seq": s, "tm": t + 2 - 4 * y})
    tell({"seq": s, "tm": t + 1 - 2 * c})

    @pl.when(z < 3)
    def _():
        tell({"seq": s, "tm": t + 4})

    @pl.when(z > 0)
    def _():
        tell({"seq": s, "tm": t - 4})
    far = jnp.where(c == 1, t + 1, t - 1)
    has_far = (far >= 0) & (far < 16)

    @pl.when(has_far)
    def _():
        tell({"seq": s, "tm": far})
    return bar, 3 + jnp.where(has_far, 1, 0) + jnp.where(z < 3, 1, 0) + jnp.where(z > 0, 1, 0)


D = 1024
FF = 4096
SEG = 256
HD = H * DH
WIDE = H * E * DH
FFB = 512
NFF = FF // FFB
NG = 4
LOGIT = 64
OWN_SIB = 24
F32 = jnp.float32
BF = jnp.bfloat16


def dot(a, b):
    return jnp.dot(a, b, preferred_element_type=F32)


def dot_nt(a, b):
    return lax.dot_general(a, b, (((1,), (1,)), ((), ())), preferred_element_type=F32)


def dot_tn(a, b):
    return lax.dot_general(a, b, (((0,), (0,)), ((), ())), preferred_element_type=F32)


def halves(v):
    top = v.astype(BF)
    return top, (v - top.astype(F32)).astype(BF)


def unit_rows(v):
    centre = v - jnp.mean(v, axis=-1, keepdims=True)
    spread = jnp.mean(centre * centre, axis=-1, keepdims=True)
    inv = lax.rsqrt(spread + epsilon)
    return centre * inv, inv


def norm_back(unit, inv, cot):
    return inv * (cot - jnp.mean(cot, axis=-1, keepdims=True)
                  - unit * jnp.mean(cot * unit, axis=-1, keepdims=True))


def for_rows(step, body):
    def inner(i, _):
        body(pl.ds(pl.multiple_of(i * step, step), step))
        return 0
    lax.fori_loop(0, SEG // step, inner, 0)


def side_by_side(blocks):
    return jnp.concatenate(blocks, axis=1)


NAMES = (
    "x", "oc", "gains", "rt", "rf", "spread", "hot", "wq", "wk", "wr", "wrp", "wu", "wd", "exv", "exo",
    "xn", "hn", "mid", "lo", "nsc", "q", "k", "v", "sig", "att", "acc", "g_o", "g_p",
    "act", "uc", "bc", "kc", "vc", "kn", "vn", "ob", "gg", "ogc", "qc", "vg", "ac", "acc2",
    "at", "full",
    "ld", "ld2", "lde", "kv_s", "kv_r", "sib_s", "sib_r", "st", "stage", "out_sem", "ssem", "rsem",
)


def layer_scratch():
    dma = pltpu.SemaphoreType.DMA
    v = pltpu.VMEM
    return [
        v((SEG, D), BF), v((SEG, D), BF), v((2, D), BF), v((2 * H, 2, SEG), jnp.int32), v((128, SEG), BF),
        v((128, 256), BF), v((SEG, 128), F32),
        v((HD, D), BF), v((HD, D), BF), v((2 * H * E, D), BF), v((128, D), BF),
        v((2, D, FFB), BF), v((2, FFB, D), BF), v((E, 256, HD), BF), v((E, 256, HD), BF),
        v((SEG, D), BF), v((SEG, D), BF), v((SEG, D), F32), v((SEG, D), F32), v((SEG, D), F32),
        v((SEG, HD), BF), v((2 * SEG, HD), BF), v((2 * SEG, HD), BF), v((SEG, 128), F32),
        v((SEG, HD), BF), v((2 * SEG, HD), F32), v((2 * SEG, 2304), BF), v((2 * SEG, 3328), BF),
        v((NG, 2 * SEG, FFB), BF), v((NG, 2 * SEG, FFB), BF), v((SEG, D), BF),
        v((2 * SEG, HD), BF), v((2 * SEG, HD), BF), v((SEG, HD), BF), v((SEG, HD), BF), v((SEG, D), BF), v((SEG, 256), BF), v((SEG, 128), F32), v((SEG, HD), F32), v((2, SEG, 128), F32),
        v((SEG, HD), BF), v((2 * SEG, HD), F32),
        v((6, 16, 32, 2 * SEG), BF), v((2, 16, 2, 32, SEG), BF),
        dma((16,)), dma((4,)), dma((2, 2 * E)), dma((4,)), dma((4,)), dma((OWN_SIB,)), dma((OWN_SIB,)), dma((2,)),
        v((2, 32, MOST), F32), dma((2,)), dma((10, NS)), dma((10, NS)),
    ]


def layer_kernel(x_h, rt_h, len_s, gains_h, wq_h, wk_h, wv_h, wr_h, wo_h, wu_h, wd_h, oc_h,
                 exv_h, exo_h, spread_h, lo_h, ig_h, flat_h, *scratch):
    m = types.SimpleNamespace(**dict(zip(NAMES, scratch[:len(NAMES)])))
    recv = scratch[len(NAMES):]
    s, t, z, y, c = place()
    last_t = lax.axis_size("tm") - 1
    sib = {"seq": s, "tm": t + 1 - 2 * c}
    scale = DH ** -0.5
    own = slice(SEG, 2 * SEG)
    mem = slice(0, SEG)

    bar, peers = greet()

    def load(i, src, dst):
        cp = pltpu.make_async_copy(src, dst, m.ld.at[i])
        cp.start()
        return cp

    def sibling(i, src, dst):
        return pltpu.make_async_remote_copy(
            src_ref=src, dst_ref=dst, send_sem=m.sib_s.at[i], recv_sem=m.sib_r.at[i],
            device_id=sib, device_id_type=MESH_ID)

    def at_copy(i, slot):
        return sibling(i, m.full.at[slot, :, 1 - c], m.at.at[i, :, :, SEG:])

    def turn(i, slot, value):
        m.full[slot] = jnp.transpose(value).reshape(16, 2, 32, SEG)
        m.at[i, :, :, :SEG] = m.full[slot, :, c]
        at_copy(i, slot).start()

    def go_copy():
        return sibling(6, m.g_o.at[mem], m.g_o.at[own])

    def gp_copy():
        return sibling(7, m.g_p.at[mem], m.g_p.at[own])

    def ff_copies(j):
        g = rem(j, NG)
        return (sibling(8 + 2 * j, m.act.at[g, mem], m.act.at[g, own]),
                sibling(9 + 2 * j, m.uc.at[g, mem], m.uc.at[g, own]))

    def ff_loads(j):
        cols = pl.ds(pl.multiple_of(j * FFB, FFB), FFB)
        return (pltpu.make_async_copy(wu_h.at[:, cols], m.wu.at[j % 2], m.ld2.at[j % 2]),
                pltpu.make_async_copy(wd_h.at[cols, :], m.wd.at[j % 2], m.ld2.at[2 + j % 2]))

    def along(i, src, dst, by):
        return pltpu.make_async_remote_copy(
            src_ref=src, dst_ref=dst, send_sem=m.kv_s.at[i], recv_sem=m.kv_r.at[i],
            device_id={"seq": s, "tm": t + by}, device_id_type=MESH_ID)

    def k_copy():
        return along(0, m.k.at[own], m.k.at[mem], 1)

    def v_copy():
        return along(1, m.v.at[own], m.v.at[mem], 1)

    def kc_copy():
        return along(2, m.kc.at[mem], m.kn, -1)

    def vc_copy():
        return along(3, m.vc.at[mem], m.vn, -1)

    def head_lanes(rows, h):
        lane = lax.broadcasted_iota(jnp.int32, (rows, HD), 1)
        return (lane >= h * DH) & (lane < (h + 1) * DH)

    def head_only(v, h):
        return jnp.where(head_lanes(v.shape[0], h), v, jnp.zeros_like(v))

    def gates_wide(table, e):
        return dot(m.gg[...], table[e])

    def expert_loads(which, n, e, src, dst):
        return [pltpu.make_async_copy(src.at[pl.ds((h * E + e) * DH, DH)], dst.at[pl.ds(h * DH, DH)], m.lde.at[which, n])
                for h in range(H)]

    def ring(n):
        return expert_loads(0, n, n % E, wo_h if n < E else wv_h, m.wd.at[n % 2])

    def weights_of(h):
        scores = dot_nt(head_only(m.q[...], h), m.k[...]) * scale
        length = len_s[0, 0]
        row = lax.broadcasted_iota(jnp.int32, (SEG, 2 * SEG), 0)
        col = lax.broadcasted_iota(jnp.int32, (SEG, 2 * SEG), 1)
        allowed = ((col < SEG) & (col >= SEG - length)) | ((col >= SEG) & (col - SEG <= row))
        scores = jnp.where(allowed, scores, -1e30)
        e = jnp.exp(scores - jnp.max(scores, axis=-1, keepdims=True))
        return e / jnp.sum(e, axis=-1, keepdims=True)

    l_x = load(0, x_h, m.x)
    l_g = load(1, gains_h, m.gains)
    l_k = load(2, wk_h, m.wk)
    l_r = load(3, wr_h, m.wr)
    l_rt = load(4, rt_h, m.rt)
    l_sp = load(12, spread_h, m.spread)

    def forward(wv, wo):
        l_ev = load(6, exv_h, m.exv)
        l_v = [expert_loads(0, e, e, wv_h, wv.at[e]) for e in range(E)]
        for group in l_v:
            for cp in group:
                cp.start()
        l_x.wait()
        l_g.wait()

        def norm1(rows):
            unit, _ = unit_rows(m.x[rows, :].astype(F32))
            m.xn[rows, :] = (unit * m.gains[0:1, :].astype(F32)).astype(BF)
        for_rows(32, norm1)
        l_k.wait()
        m.k[own, :] = dot_nt(m.xn[...], m.wk[...]).astype(BF)
        l_q = load(8, wq_h, m.wq)
        l_oc = load(9, oc_h, m.oc)
        l_eo = load(10, exo_h, m.exo)
        l_wo = [expert_loads(1, e, e, wo_h, wo.at[e]) for e in range(E)]
        for group in l_wo:
            for cp in group:
                cp.start()
        for j in range(2):
            for cp in ff_loads(j):
                cp.start()
        pl.semaphore_wait(bar, peers)

        @pl.when(t < last_t)
        def _():
            k_copy().start()
        l_r.wait()
        m.wrp[...] = jnp.zeros((128, D), BF)
        m.wrp[LOGIT:LOGIT + 2 * H * E, :] = m.wr[...]
        sig = jax.nn.sigmoid(dot_nt(m.xn[...], m.wrp[...]))
        l_rt.wait()
        l_sp.wait()
        m.rf[...] = jnp.zeros((128, SEG), BF)
        for i in range(2):
            m.rf[16 * i:16 * i + 2 * H, :] = m.rt[:, i, :].astype(F32).astype(BF)
        named = dot_tn(m.rf[...], m.spread[...])
        expert = m.spread[127:128, :128].astype(F32)
        hit = (named[:, :128] == expert) | (named[:, 128:] == expert)
        m.hot[...] = jnp.where(hit, 1.0, 0.0)
        m.sig[...] = sig
        top, low = halves(sig * m.hot[...])
        m.gg[:, :128] = top
        m.gg[:, 128:] = low
        l_ev.wait()
        total = jnp.zeros((SEG, HD), F32)
        for e in range(E):
            for cp in l_v[e]:
                cp.wait()
            total = total + dot_nt(m.xn[...], wv[e]) * gates_wide(m.exv, e)
        m.v[own, :] = total.astype(BF)

        @pl.when(t < last_t)
        def _():
            v_copy().start()
        l_q.wait()
        m.q[...] = dot_nt(m.xn[...], m.wq[...]).astype(BF)
        l_oc.wait()
        turn(0, 0, m.oc[...])
        turn(3, 1, m.xn[...])

        @pl.when(t > 0)
        def _():
            k_copy().wait_recv()

        @pl.when(t == 0)
        def _():
            m.k[mem, :] = jnp.zeros((SEG, HD), BF)
            m.v[mem, :] = jnp.zeros((SEG, HD), BF)
        for h in range(H):
            m.act[h, mem] = weights_of(h).astype(BF)

        @pl.when(t > 0)
        def _():
            v_copy().wait_recv()
        total = jnp.zeros((SEG, HD), F32)
        for h in range(H):
            total = total + dot(m.act[h, mem], head_only(m.v[...], h))
        m.att[...] = total.astype(BF)
        l_eo.wait()
        m.g_o[mem, 2176:2304] = jnp.zeros((SEG, 128), BF)
        total = m.x[...].astype(F32)
        blocks = []
        for e in range(E):
            blocks.append((gates_wide(m.exo, e) * m.att[...].astype(F32)).astype(BF))
            for cp in l_wo[e]:
                cp.wait()
            total = total + dot(blocks[e], wo[e])
        m.mid[...] = total
        for e in range(0, E, 2):
            m.g_o[mem, e * HD:min(e + 2, E) * HD] = side_by_side(blocks[e:e + 2])
        go_copy().start()

        def norm2(rows):
            unit, _ = unit_rows(m.mid[rows, :])
            m.hn[rows, :] = (unit * m.gains[1:2, :].astype(F32)).astype(BF)
        for_rows(32, norm2)
        at_copy(0, 0).wait_send()
        turn(1, 0, m.hn[...])

    pl.run_scoped(forward, pltpu.VMEM((E, HD, D), BF), pltpu.VMEM((E, HD, D), BF))

    def backward(parts):
        ex = Exchange(parts, recv, (m.ssem, m.rsem), m.stage, m.out_sem, flat_h)

        def product(i, g):
            return dot(m.at[i].reshape(512, 2 * SEG), g)

        def tiles(i, g, tile):
            store_tile(parts, tile, product(i, g))

        def two(i):
            return pl.ds(pl.multiple_of(i * 2 * TILE, 2 * TILE), 2 * TILE)

        m.lo[...] = m.mid[...]
        m.nsc[...] = jnp.zeros((SEG, D), F32)
        at_copy(0, 0).wait_recv()
        at_copy(1, 0).wait_recv()

        def block(j, _):
            b = rem(j, 2)
            g = rem(j, NG)
            for cp in ff_loads(j):
                cp.wait()
            pre = dot(m.hn[...], m.wu[b])
            cdf = 0.5 * (1.0 + lax.erf(pre * 0.7071067811865476))
            pdf = jnp.exp(-0.5 * pre * pre) * 0.3989422804014327
            up = dot_nt(m.oc[...], m.wd[b])

            @pl.when(j >= NG)
            def _():
                for cp in ff_copies(j - NG):
                    cp.wait_send()
            m.act[g, mem] = (pre * cdf).astype(BF)
            m.uc[g, mem] = (up * (cdf + pre * pdf)).astype(BF)
            for cp in ff_copies(j):
                cp.start()

            @pl.when(j > 1)
            def _():
                weights_grad(j - 1)
            m.lo[...] += dot(m.act[g, mem], m.wd[b])
            m.nsc[...] += dot_nt(m.uc[g, mem], m.wu[b])

            @pl.when(j + 2 < NFF)
            def _():
                for cp in ff_loads(j + 2):
                    cp.start()

            @pl.when(j == 0)
            def _():
                weights_grad(0)
                ex.begin(0)

            @pl.when(j == 2)
            def _():
                ex.begin(1)

            @pl.when(j == 3)
            def _():
                ex.tick(1)

            @pl.when(j == 4)
            def _():
                ex.begin(2)

            @pl.when(j == 5)
            def _():
                ex.tick(2)
                ex.begin(3)
            return 0

        def weights_grad(j):
            for cp in ff_copies(j):
                cp.wait_recv()
            tiles(0, m.act[rem(j, NG)], 8 * j)
            tiles(1, m.uc[rem(j, NG)], 8 * j + 4)
        lax.fori_loop(0, NFF, block, 0)
        for n in range(2):
            for cp in ring(n):
                cp.start()
        weights_grad(NFF - 1)
        ex.tick(3)
        ex.begin(4)
        for j in range(NFF - NG, NFF):
            for cp in ff_copies(j):
                cp.wait_send()
        m.ob[...] = m.lo[...].astype(BF)
        l_lo = pltpu.make_async_copy(m.ob, lo_h, m.st.at[0])
        l_lo.start()

        def norm2_back(rows):
            unit, inv = unit_rows(m.mid[rows, :])
            cot = m.nsc[rows, :]
            mcot = m.oc[rows, :].astype(F32) + norm_back(unit, inv, cot * m.gains[1:2, :].astype(F32))
            m.lo[rows, :] = mcot
            m.bc[rows, :] = mcot.astype(BF)
            m.hn[rows, :] = (cot * unit).astype(BF)
        for_rows(32, norm2_back)
        at_copy(3, 1).wait_send()
        turn(2, 1, m.bc[...])
        at_copy(1, 0).wait_send()
        turn(5, 0, m.hn[...])
        def ring_next(n):
            if n + 2 < 2 * E:
                for cp in ring(n + 2):
                    cp.start()

        att = m.att[...].astype(F32)
        seen = jnp.zeros((SEG, 128), F32)
        total = jnp.zeros((SEG, HD), F32)
        for e in range(E):
            for cp in ring(e):
                cp.wait()
            cot = dot_nt(m.bc[...], m.wd[e % 2, :HD])
            ring_next(e)
            seen = seen + dot_nt((cot * att).astype(BF), m.exo[e, :128])
            total = total + cot * gates_wide(m.exo, e)
        m.ogc[...] = seen
        m.ac[...] = total.astype(BF)
        ex.tick(4)
        ex.begin(5)

        m.acc[...] = jnp.zeros((2 * SEG, HD), F32)
        m.acc2[...] = jnp.zeros((2 * SEG, HD), F32)
        m.qc[...] = jnp.zeros((SEG, HD), F32)

        def scores_back(h, _):
            probs = weights_of(h)
            cot = head_only(m.ac[...], h)
            m.acc2[...] += dot_tn(probs.astype(BF), cot)
            pc = dot_nt(cot, m.v[...])
            sc = (probs * (pc - jnp.sum(probs * pc, axis=-1, keepdims=True))).astype(BF)
            m.qc[...] += dot(sc, head_only(m.k[...], h)) * scale
            m.acc[...] += dot_tn(sc, head_only(m.q[...], h)) * scale
            return 0
        lax.fori_loop(0, H, scores_back, 0)
        m.vc[...] = m.acc2[...].astype(BF)
        m.kc[...] = m.acc[...].astype(BF)

        @pl.when(t > 0)
        def _():
            vc_copy().start()
            kc_copy().start()
        go_copy().wait_recv()
        at_copy(2, 1).wait_recv()

        def out_grad(i, _):
            tiles(2, m.g_o[:, two(i)], 64 + 2 * i)
            return 0
        lax.fori_loop(0, 9, out_grad, 0)
        m.g_p[mem, HD:512] = jnp.zeros((SEG, 512 - HD), BF)
        m.g_p[mem, 512 + HD:1024] = jnp.zeros((SEG, 512 - HD), BF)
        m.g_p[mem, :HD] = m.qc[...].astype(BF)
        ex.tick(5)
        ex.begin(6)

        @pl.when(t < last_t)
        def _():
            vc_copy().wait_recv()
            kc_copy().wait_recv()

        @pl.when(t == last_t)
        def _():
            m.kn[...] = jnp.zeros((SEG, HD), BF)
            m.vn[...] = jnp.zeros((SEG, HD), BF)
        m.g_p[mem, 512:512 + HD] = (m.kc[own, :].astype(F32) + m.kn[...].astype(F32)).astype(BF)
        l_lo.wait()

        own_cot, next_cot = m.mid, m.nsc

        own_cot[...] = dot(m.kc[own, :], m.wk[...]) + dot(m.g_p[mem, :HD], m.wq[...])
        next_cot[...] = dot(m.kn[...], m.wk[...])
        m.vg[...] = jnp.zeros((2, SEG, 128), F32)
        blocks = []
        for e in range(E):
            for cp in ring(E + e):
                cp.wait()
            wv = m.wd.at[(E + e) % 2]
            proj = dot_nt(m.xn[...], wv[:HD])
            gate = gates_wide(m.exv, e)
            pair = []
            for i, (v, acc) in enumerate(((m.vc[own, :], own_cot), (m.vn[...], next_cot))):
                v = v.astype(F32)
                m.vg[i] += dot_nt((v * proj).astype(BF), m.exv[e, :128])
                pair.append((gate * v).astype(BF))
                acc[...] += dot(pair[i], wv[:HD])
            ring_next(E + e)
            if e == 2:
                ex.tick(6)
                ex.begin(7)
            blocks.append((pair[0].astype(F32) + pair[1].astype(F32)).astype(BF))
            if e % 2 == 1 or e == E - 1:
                first = e - 1 if e % 2 == 1 else e
                m.g_p[mem, 1024 + first * HD:1024 + (e + 1) * HD] = side_by_side(blocks[first:])
        slope = m.sig[...] * (1.0 - m.sig[...]) * m.hot[...]
        lo_cot = ((m.vg[0] + m.ogc[...]) * slope).astype(BF)
        ln_cot = (m.vg[1] * slope).astype(BF)
        own_cot[...] += dot(lo_cot, m.wrp[...])
        next_cot[...] += dot(ln_cot, m.wrp[...])
        both = (lo_cot.astype(F32) + ln_cot.astype(F32)).astype(BF)
        lane = lax.broadcasted_iota(jnp.int32, (SEG, 128), 1)
        m.g_p[mem, 3200:3328] = jnp.where(lane < LOGIT, m.g_p[mem, 3200:3328], both)
        gp_copy().start()
        ex.tick(7)
        ex.begin(8)

        def norm1_back(rows):
            unit, inv = unit_rows(m.x[rows, :].astype(F32))
            cot = own_cot[rows, :]
            m.lo[rows, :] += norm_back(unit, inv, cot * m.gains[0:1, :].astype(F32))
            m.hn[rows, :] = ((cot + next_cot[rows, :]) * unit).astype(BF)
        for_rows(32, norm1_back)
        l_ig = pltpu.make_async_copy(m.lo, ig_h, m.st.at[1])
        l_ig.start()
        at_copy(2, 1).wait_send()
        turn(4, 1, m.hn[...])
        ex.tick(8)
        gp_copy().wait_recv()
        at_copy(3, 1).wait_recv()

        def proj_grad(i, _):
            tiles(3, m.g_p[:, two(i)], 82 + 2 * i)
            return 0
        lax.fori_loop(0, 12, proj_grad, 0)
        last = product(3, m.g_p[:, 3072:3328])
        store_tile(parts, 106, last[:, :TILE])
        last = last[:, TILE:]
        lane = lax.broadcasted_iota(jnp.int32, (2 * SEG, TILE), 1)
        at_copy(5, 0).wait_recv()
        at_copy(4, 1).wait_recv()
        for i, at in ((4, 104), (5, 105)):
            last += product(i, jnp.where(lane == at, 1.0, 0.0).astype(BF))
        store_tile(parts, 107, last)

        ex.begin(9)
        for i in range(9, NS + 5):
            ex.tick(i)
            ex.begin(i + 1)
        ex.finish()
        l_ig.wait()

    pl.run_scoped(backward, *P_SCRATCH)
    at_copy(5, 0).wait_send()
    at_copy(4, 1).wait_send()
    go_copy().wait_send()
    gp_copy().wait_send()

    @pl.when(t < last_t)
    def _():
        k_copy().wait_send()
        v_copy().wait_send()

    @pl.when(t > 0)
    def _():
        kc_copy().wait_send()
        vc_copy().wait_send()


def tables():
    col = np.arange(HD)[None, None, :] // DH * E + np.arange(E)[:, None, None]
    branch = np.arange(128)[None, :, None]
    exv = branch == LOGIT + col
    exo = branch == LOGIT + H * E + col
    exv, exo = (np.concatenate([v, v], axis=1) for v in (exv, exo))
    lane = np.arange(128) - LOGIT
    inside = (lane >= 0) & (lane < 2 * H * E)
    pick = (np.arange(2 * H)[:, None] == lane[None, :] // E) & inside
    spread = np.zeros((128, 256), np.float32)
    spread[:2 * H, :128] = pick
    spread[16:16 + 2 * H, 128:] = pick
    spread[127, :128] = np.where(inside, lane % E, -1)
    return tuple(v.astype(ml_dtypes.bfloat16) for v in (exv, exo, spread))


def fused_device(layer_input, routes, memory_lengths, norm_gains, w_query, w_key, w_value,
                 w_router, w_output, w_up, w_down, output_cot):
    anywhere = pl.BlockSpec(memory_space=pl.ANY)
    specs = [anywhere] * 15
    specs[2] = pl.BlockSpec(memory_space=pltpu.SMEM)
    out, grad, flat = pl.pallas_call(
        layer_kernel,
        out_shape=(jax.ShapeDtypeStruct((SEG, D), BF), jax.ShapeDtypeStruct((SEG, D), F32),
                   jax.ShapeDtypeStruct((32, FLAT), F32)),
        in_specs=specs,
        out_specs=(anywhere,) * 3,
        scratch_shapes=layer_scratch() + RECV_SCRATCH,
        compiler_params=pltpu.CompilerParams(
            collective_id=0, has_side_effects=True, vmem_limit_bytes=VMEM_LIMIT),
        name="layer",
    )(layer_input[0], jnp.transpose(routes[0], (1, 2, 0)), memory_lengths, norm_gains, w_query.T, w_key.T, w_value.T, w_router.T,
      w_output, w_up, w_down, output_cot[0], *tables())
    shapes = ((SEG, D), BF), ((SEG, D), F32), ((2, 32), F32), ((32, HD), F32), ((32, HD), F32), \
        ((32, WIDE), F32), ((32, 2 * H * E), F32), ((32, WIDE), F32), ((32, FF), F32), ((32, FF), F32)
    vm = pl.BlockSpec(memory_space=pltpu.VMEM)
    res = pl.pallas_call(
        split_kernel,
        out_shape=tuple(jax.ShapeDtypeStruct(*v) for v in shapes),
        in_specs=(anywhere, anywhere, anywhere),
        out_specs=(vm,) * 10,
        scratch_shapes=[pltpu.VMEM((32, FLAT), F32), pltpu.SemaphoreType.DMA((3,))],
        compiler_params=pltpu.CompilerParams(vmem_limit_bytes=VMEM_LIMIT),
        name="split",
    )(out, grad, flat)
    return (res[0][None], res[1][None], *res[2:7], res[7].T, res[8], res[9].T)


def split_kernel(out_h, grad_h, flat_h, lo, ig, gains, dq, dk, dv, dr, do, du, dd, flat, sem):
    copies = [pltpu.make_async_copy(flat_h, flat, sem.at[2]), pltpu.make_async_copy(out_h, lo, sem.at[0]),
              pltpu.make_async_copy(grad_h, ig, sem.at[1])]
    for cp in copies:
        cp.start()
    copies.pop(0).wait()
    for j in range(NFF):
        dd[:, j * FFB:(j + 1) * FFB] = flat[:, 2 * j * FFB:(2 * j + 1) * FFB]
        du[:, j * FFB:(j + 1) * FFB] = flat[:, (2 * j + 1) * FFB:(2 * j + 2) * FFB]
    base = 82 * TILE
    dq[...] = flat[:, base:base + HD]
    dk[...] = flat[:, base + 512:base + 512 + HD]
    for h in range(H):
        for e in range(E):
            to = slice((h * E + e) * DH, (h * E + e + 1) * DH)
            at = e * HD + h * DH
            do[:, to] = flat[:, 2 * FF + at:2 * FF + at + DH]
            dv[:, to] = flat[:, base + 1024 + at:base + 1024 + at + DH]
    tail = flat[:, 107 * TILE:108 * TILE]
    dr[...] = tail[:, LOGIT:LOGIT + 2 * H * E]
    gains[...] = jnp.transpose(tail)[104:106, :]
    for cp in copies:
        cp.wait()


def solution(mesh):
    placed = (
        P("seq", "tm", None),
        P("seq", "tm", None, None),
        P("seq", "tm"),
        P(),
        P(),
        P(),
        P(),
        P(),
        P(),
        P(),
        P(),
        P("seq", "tm", None),
    )
    fused = mesh.shape["seq"] == 2 and mesh.shape["tm"] == 16
    return jax.shard_map(
        fused_device if fused else per_device,
        mesh=mesh,
        in_specs=placed,
        out_specs=(
            P("seq", "tm", None),
            P("seq", "tm", None),
            P(None, ("seq", "tm")),
            P(("seq", "tm"), None),
            P(("seq", "tm"), None),
            P(("seq", "tm"), None),
            P(("seq", "tm"), None),
            P(None, ("seq", "tm")),
            P(("seq", "tm"), None),
            P(None, ("seq", "tm")),
        ),
        check_vma=False,
    )
```

```python
import types

import jax
import jax.numpy as jnp
import ml_dtypes
import numpy as np
from jax import lax
from jax.experimental import pallas as pl
from jax.experimental.pallas import tpu as pltpu
from jax.sharding import PartitionSpec as P

H = 4
DH = 112
E = 5


epsilon = 1e-05


def passed_along(value, axis, steps):
    count = lax.axis_size(axis)
    initial, last = (max(0, -steps), min(count, count - steps))
    return lax.ppermute(value, axis, [(source, source + steps) for source in range(initial, last)])


def normalize(values, gain_vec):
    centre = values - jnp.mean(values, axis=-1, keepdims=True)
    spread = jnp.mean(centre * centre, axis=-1, keepdims=True)
    return centre * lax.rsqrt(spread + epsilon) * gain_vec


def exact_gelu(arg_in):
    return jax.nn.gelu(arg_in, approximate=False)


def matmul(left_op, right_op):
    return jnp.dot(left_op, right_op, preferred_element_type=jnp.float32)


def times_tr(left_op, right_op):
    return lax.dot_general(
        left_op, right_op, (((1,), (1,)), ((), ())), preferred_element_type=jnp.float32
    )


def tr_times(left_op, right_op):
    return lax.dot_general(
        left_op, right_op, (((0,), (0,)), ((), ())), preferred_element_type=jnp.float32
    )


def one_hot_routes(route_ids):
    return jnp.sum(
        (route_ids[..., None] == jnp.arange(E, dtype=jnp.int32)).astype(jnp.float32), axis=-2
    )


def attention_mask(memory_length, seg_len):
    query_pos = jnp.arange(seg_len, dtype=jnp.int32)[:, None]
    key_pos = jnp.arange(2 * seg_len, dtype=jnp.int32)[None, :]
    return jnp.where(
        key_pos < seg_len, key_pos >= seg_len - memory_length, key_pos - seg_len <= query_pos
    )


def per_device(
    layer_input,
    routes,
    memory_lengths,
    norm_gains,
    w_query,
    w_key,
    w_value,
    w_router,
    w_output,
    w_up,
    w_down,
    output_cot,
):
    seg_len = layer_input.shape[1]
    own_rows = layer_input[0].astype(jnp.float32)
    memory_length = memory_lengths[0, 0]
    gains_f = norm_gains.astype(jnp.float32)
    first_gain = gains_f[0]
    second_gain = gains_f[1]
    scale_factor = DH ** (-0.5)
    allowed = attention_mask(memory_length, seg_len)
    onehot = one_hot_routes(routes[0])
    unit_normed = normalize(own_rows, jnp.ones_like(first_gain))
    own_normed = (unit_normed * first_gain).astype(jnp.bfloat16)

    def projections():
        queries = matmul(own_normed, w_query).astype(jnp.bfloat16)
        key_own = matmul(own_normed, w_key).astype(jnp.bfloat16)
        logits = matmul(own_normed, w_router).reshape(seg_len, 2 * H, E)
        gate_sig = jax.nn.sigmoid(logits)
        gate_vals = gate_sig * onehot
        projected = matmul(own_normed, w_value).reshape(seg_len, H, E, DH)
        value_own = (
            jnp.sum(gate_vals[:, :H, :, None] * projected, axis=2)
            .reshape(seg_len, H * DH)
            .astype(jnp.bfloat16)
        )
        return (queries, key_own, gate_sig, gate_vals, projected, value_own)

    queries, key_own, gate_sig, gate_vals, projected, value_own = projections()
    key_mem, value_mem = passed_along((key_own, value_own), "tm", 1)
    key_rows = jnp.concatenate([key_mem, key_own], axis=0)
    value_rows = jnp.concatenate([value_mem, value_own], axis=0)
    head_outs = []
    log_norms = []
    for head_idx in range(H):
        columns = slice(head_idx * DH, (head_idx + 1) * DH)
        scores = (
            jnp.einsum(
                "qd,kd->qk",
                queries[:, columns],
                key_rows[:, columns],
                preferred_element_type=jnp.float32,
            )
            * scale_factor
        )
        scores = jnp.where(allowed, scores, -1e30)
        peak = jnp.max(scores, axis=-1, keepdims=True)
        exp_scores = jnp.exp(scores - peak)
        total = jnp.sum(exp_scores, axis=-1, keepdims=True)
        weights = (exp_scores / total).astype(jnp.bfloat16)
        head_outs.append(matmul(weights, value_rows[:, columns]))
        log_norms.append(peak + jnp.log(total))
    attended = jnp.concatenate(head_outs, axis=1).astype(jnp.bfloat16)
    out_gates = gate_vals[:, H:]
    attended_f = attended.astype(jnp.float32).reshape(seg_len, H, 1, DH)
    mixed_in = (attended_f * out_gates[..., None]).reshape(seg_len, H * E * DH).astype(jnp.bfloat16)
    middle = own_rows + matmul(mixed_in, w_output)
    hidden_normed = normalize(middle, second_gain).astype(jnp.bfloat16)
    pre_act = matmul(hidden_normed, w_up)
    activated = exact_gelu(pre_act).astype(jnp.bfloat16)
    layer_out = middle + matmul(activated, w_down)
    output_block = layer_out.astype(jnp.bfloat16)[None]
    down_cot = output_cot[0]
    out_cot = down_cot.astype(jnp.float32)
    grad_down = tr_times(activated, down_cot)
    grad_act = times_tr(down_cot, w_down)
    unused_gelu, gelu_pull = jax.vjp(exact_gelu, pre_act)
    up_cot = gelu_pull(grad_act)[0].astype(jnp.bfloat16)
    grad_up = tr_times(hidden_normed, up_cot)
    normed_second_cot = times_tr(up_cot, w_up)
    unused_norm, second_pull = jax.vjp(normalize, middle, second_gain)
    middle_part, grad_second = second_pull(normed_second_cot)
    middle_cot = out_cot + middle_part
    branch_cot = middle_cot.astype(jnp.bfloat16)
    grad_output = tr_times(mixed_in, branch_cot)
    mixed_cot = times_tr(branch_cot, w_output).reshape(seg_len, H, E, DH)
    out_gate_cot = jnp.sum(mixed_cot * attended_f, axis=-1)
    attended_cot = (
        jnp.sum(mixed_cot * out_gates[..., None], axis=2)
        .reshape(seg_len, H * DH)
        .astype(jnp.bfloat16)
    )
    queries, key_own, gate_sig, gate_vals, projected, value_own = projections()
    key_back, value_back = passed_along((key_own, value_own), "tm", 1)
    key_rows = jnp.concatenate([key_back, key_own], axis=0)
    value_rows = jnp.concatenate([value_back, value_own], axis=0)
    query_grads = []
    key_grads = []
    value_grads = []
    for head_idx in range(H):
        columns = slice(head_idx * DH, (head_idx + 1) * DH)
        scores = (
            jnp.einsum(
                "qd,kd->qk",
                queries[:, columns],
                key_rows[:, columns],
                preferred_element_type=jnp.float32,
            )
            * scale_factor
        )
        scores = jnp.where(allowed, scores, -1e30)
        probs = jnp.exp(scores - log_norms[head_idx])
        weights = probs.astype(jnp.bfloat16)
        cot_head = attended_cot[:, columns]
        value_grads.append(tr_times(weights, cot_head))
        prob_cot = times_tr(cot_head, value_rows[:, columns])
        score_cot = (probs * (prob_cot - jnp.sum(probs * prob_cot, axis=-1, keepdims=True))).astype(
            jnp.bfloat16
        )
        query_grads.append(matmul(score_cot, key_rows[:, columns]) * scale_factor)
        key_grads.append(tr_times(score_cot, queries[:, columns]) * scale_factor)
    query_cot = jnp.concatenate(query_grads, axis=1).astype(jnp.bfloat16)
    key_cot_all = jnp.concatenate(key_grads, axis=1)
    value_cot_all = jnp.concatenate(value_grads, axis=1)
    key_mem_cot = key_cot_all[:seg_len].astype(jnp.bfloat16)
    key_own_cot = key_cot_all[seg_len:].astype(jnp.bfloat16)
    value_mem_cot = value_cot_all[:seg_len].astype(jnp.bfloat16)
    value_own_cot = value_cot_all[seg_len:].astype(jnp.bfloat16)
    key_next, value_next = passed_along((key_mem_cot, value_mem_cot), "tm", -1)
    own_vcot = value_own_cot.astype(jnp.float32).reshape(seg_len, H, 1, DH)
    next_vcot = value_next.astype(jnp.float32).reshape(seg_len, H, 1, DH)
    val_gates = gate_vals[:, :H, :, None]
    proj_own_cot = (val_gates * own_vcot).reshape(seg_len, H * E * DH).astype(jnp.bfloat16)
    proj_next_cot = (val_gates * next_vcot).reshape(seg_len, H * E * DH).astype(jnp.bfloat16)
    gate_own_cot = jnp.concatenate([jnp.sum(own_vcot * projected, axis=-1), out_gate_cot], axis=1)
    gate_next_cot = jnp.concatenate(
        [jnp.sum(next_vcot * projected, axis=-1), jnp.zeros_like(out_gate_cot)], axis=1
    )
    slope = gate_sig * (1.0 - gate_sig) * onehot
    logit_own_cot = (gate_own_cot * slope).reshape(seg_len, 2 * H * E).astype(jnp.bfloat16)
    logit_next_cot = (gate_next_cot * slope).reshape(seg_len, 2 * H * E).astype(jnp.bfloat16)
    twice_normed = jnp.concatenate([own_normed, own_normed], axis=0)
    key_both = jnp.concatenate([key_own_cot, key_next], axis=0)
    proj_both = jnp.concatenate([proj_own_cot, proj_next_cot], axis=0)
    logit_both = jnp.concatenate([logit_own_cot, logit_next_cot], axis=0)
    grad_query = tr_times(own_normed, query_cot)
    grad_key = tr_times(twice_normed, key_both)
    grad_value = tr_times(twice_normed, proj_both)
    grad_router = tr_times(twice_normed, logit_both)
    normed_both = (
        times_tr(key_both, w_key) + times_tr(proj_both, w_value) + times_tr(logit_both, w_router)
    )
    own_normed_cot = normed_both[:seg_len] + times_tr(query_cot, w_query)
    next_normed_cot = normed_both[seg_len:]
    grad_first = jnp.sum((own_normed_cot + next_normed_cot) * unit_normed, axis=0)
    unused_first, first_pull = jax.vjp(normalize, own_rows, first_gain)
    input_part = first_pull(own_normed_cot)[0]
    input_cot = middle_cot + input_part
    grad_gains = jnp.stack([grad_first, grad_second], axis=0)
    row_query, row_key, row_value, row_router, row_up = (
        lax.psum_scatter(grad_query, ("seq", "tm"), scatter_dimension=0, tiled=True),
        lax.psum_scatter(grad_key, ("seq", "tm"), scatter_dimension=0, tiled=True),
        lax.psum_scatter(grad_value, ("seq", "tm"), scatter_dimension=0, tiled=True),
        lax.psum_scatter(grad_router, ("seq", "tm"), scatter_dimension=0, tiled=True),
        lax.psum_scatter(grad_up, ("seq", "tm"), scatter_dimension=0, tiled=True),
    )
    col_gains, col_output, col_down = (
        lax.psum_scatter(grad_gains, ("seq", "tm"), scatter_dimension=1, tiled=True),
        lax.psum_scatter(grad_output, ("seq", "tm"), scatter_dimension=1, tiled=True),
        lax.psum_scatter(grad_down, ("seq", "tm"), scatter_dimension=1, tiled=True),
    )
    return (
        output_block,
        input_cot[None],
        col_gains,
        row_query,
        row_key,
        row_value,
        row_router,
        col_output,
        row_up,
        col_down,
    )


VMEM_LIMIT = 64 << 20

MESH_ID = pl.DeviceIdType.MESH
TILE = 128
PIECES = [(4, 2), (7, 2), (6, 2), (7, 2), (7, 2), (6, 2), (7, 2), (7, 2), (7, 2), (6, 2), (5, 2), (5, 2), (5, 1), (3, 1)]
NS = len(PIECES)
TILES = sum(a + b for a, b in PIECES)
FLAT = TILES * TILE
MOST_FIRST = max(a for a, _ in PIECES) * TILE
MOST_LAST = max(b for _, b in PIECES) * TILE
MOST = max(a + b for a, b in PIECES) * TILE
N1 = 6
NR = 4
NZ = 6
NZ1 = 7
HALF = (slice(0, 16), slice(16, 32))


POINTS = ([("d0", 4), ("u0", 8), ("j1", 16)] + [(f"j{j}", 8 * j) for j in range(2, 8)] + [("dw7", 64), ("ln2b", 64)]
          + [(f"tho{e}", 64) for e in range(E)] + [("sb0", 64), ("sb1", 64), ("dwo0", 70), ("dwo1", 76), ("dwo2", 82)]
          + [(f"tv{e}", 82) for e in range(E)] + [("ln1b", 82), ("dwp0", 90), ("dwp1", 98), ("dwp2", 108)])
ROUNDS = ['j2', 'j4', 'j6', 'tho0', 'sb0', 'dwo1', 'tv1', 'tv4', 'dwp1']


def plan():
    ends = [sum(a + b for a, b in PIECES[:p + 1]) for p in range(NS)]
    begun, t, todo = 0, 1, {}
    for name, ready in POINTS:
        ops = todo[name] = []
        for again in range(1 + ROUNDS.count(name)):
            if again:
                assert begun >= t
                ops.append(("round", t))
                t += 1
            while begun < NS and ends[begun] <= ready and (begun <= t or begun < 3):
                ops.append(("begin", begun))
                begun += 1
    rest = []
    while t < NS + 5:
        rest.append(("round", t))
        t += 1
        while begun < NS and begun <= t:
            rest.append(("begin", begun))
            begun += 1
    todo["rest"] = rest
    return todo


PLAN = plan()


class Piece:
    def __init__(self, p):
        start = sum(a + b for a, b in PIECES[:p]) * TILE
        self.p, self.f, self.r, self.q, self.g = p, p % N1, p % NR, p % NZ, p % NZ1
        self.wf, self.wl = (v * TILE for v in PIECES[p])
        self.first = slice(start, start + self.wf)
        self.last = slice(start + self.wf, start + self.wf + self.wl)
        self.all = slice(start, start + self.wf + self.wl)


def place():
    s = lax.axis_index("seq")
    t = lax.axis_index("tm")
    return s, t, t // 4, (t // 2) % 2, t % 2


def rem(a, n):
    return a % n if isinstance(a, int) else lax.rem(a, n)


def store_tile(parts, tile, value):
    at = tile * TILE
    width = value.shape[1]
    cols = slice(at, at + width) if isinstance(at, int) else pl.ds(pl.multiple_of(at, TILE), width)
    parts[:, :, :, :, cols] = value.reshape(2, 4, 2, 32, width).astype(jnp.bfloat16)


class Exchange:
    def __init__(self, parts, bufs, sems, stage, out_sem, out):
        self.parts, self.out = parts, out
        self.stage, self.out_sem = stage, out_sem
        (self.xa, self.yb, self.ya, self.xb, self.zu, self.zd, self.zuc, self.zdc, self.xc, self.yc) = bufs
        self.ssem, self.rsem = sems
        self.s, self.t, self.z, self.y, self.c = place()
        s, t = self.s, self.t
        self.to_x = {"seq": 1 - s, "tm": t}
        self.to_y = {"seq": s, "tm": t + 2 - 4 * self.y}
        self.to_up = {"seq": s, "tm": t + 4}
        self.to_down = {"seq": s, "tm": t - 4}

    def copy(self, kind, g, src, dst, dev):
        return pltpu.make_async_remote_copy(
            src_ref=src, dst_ref=dst, send_sem=self.ssem.at[kind, g.p],
            recv_sem=self.rsem.at[kind, g.p], device_id=dev, device_id_type=MESH_ID)

    def c_xa(self, g):
        return self.copy(0, g, self.parts.at[1 - self.s, :, :, HALF[0], g.first], self.xa.at[g.f, :, :, :, :g.wf], self.to_x)

    def c_yb(self, g):
        return self.copy(1, g, self.parts.at[:, :, 1 - self.y, HALF[1], g.first], self.yb.at[g.f, :, :, :, :g.wf], self.to_y)

    def c_ya(self, g):
        return self.copy(2, g, self.parts.at[self.s, :, 1 - self.y, HALF[0], g.first], self.ya.at[g.r, :, :, :g.wf], self.to_y)

    def c_xb(self, g):
        return self.copy(3, g, self.parts.at[1 - self.s, :, self.y, HALF[1], g.first], self.xb.at[g.r, :, :, :g.wf], self.to_x)

    def c_xc(self, g):
        return self.copy(4, g, self.parts.at[1 - self.s, self.z, :, :, g.last], self.xc.at[g.r, :, :, :g.wl], self.to_x)

    def c_yc(self, g):
        return self.copy(5, g, self.parts.at[self.s, self.z, 1 - self.y, :, g.last], self.yc.at[g.r, :, :g.wl], self.to_y)

    def c_up(self, g, z):
        return self.copy(6, g, self.parts.at[self.s, z + 1:4, self.y, :, g.first], self.zu.at[g.q, z:3, :, :g.wf], self.to_up)

    def c_down(self, g, z):
        return self.copy(7, g, self.parts.at[self.s, 0:z, self.y, :, g.first], self.zd.at[g.q, 0:z, :, :g.wf], self.to_down)

    def c_upc(self, g, z):
        return self.copy(8, g, self.parts.at[:, z + 1:4, :, :, g.last], self.zuc.at[g.g, :, z:3, :, :, :g.wl], self.to_up)

    def c_downc(self, g, z):
        return self.copy(9, g, self.parts.at[:, 0:z, :, :, g.last], self.zdc.at[g.g, :, 0:z, :, :, :g.wl], self.to_down)

    def add(self, at, cols, value):
        self.parts[(*at, cols)] = self.parts[(*at, cols)] + value

    def z_step(self, g, k, is_c):
        if is_c and not g.wl:
            return
        up, down = (self.c_upc, self.c_downc) if is_c else (self.c_up, self.c_down)
        rows = slice(None)

        def add(u, src, at):
            if is_c:
                def body(i, _):
                    a, b = i // 2, i % 2
                    self.add((a, u, b, rows), g.last, src[g.g, a, at, b, :, :g.wl])
                    return 0
                lax.fori_loop(0, 4, body, 0)
            else:
                self.add((self.s, u, self.y, rows), g.first, src[g.q, at, :, :g.wf])

        @pl.when(self.z == k - 1)
        def _():
            z = k - 1
            if z > 0:
                up(g, z - 1).wait_recv()
                for u in range(z + 1, 4):
                    add(u, self.zuc if is_c else self.zu, u - 1)
            if z < 3:
                up(g, z).start()

        @pl.when(self.z == 4 - k)
        def _():
            z = 4 - k
            if z < 3:
                down(g, z + 1).wait_recv()
                for u in range(0, z):
                    add(u, self.zdc if is_c else self.zd, u)
            if z > 0:
                down(g, z).start()

    def step1(self, g):
        self.c_xa(g).start()
        self.c_yb(g).start()
        self.z_step(g, 1, True)

    def step2(self, g):
        self.c_xa(g).wait_recv()

        def body(i, _):
            a, b = i // 2, i % 2
            self.add((self.s, a, b, HALF[0]), g.first, self.xa[g.f, a, b, :, :g.wf])
            return 0
        lax.fori_loop(0, 8, body, 0)
        self.c_ya(g).start()
        self.c_yb(g).wait_recv()

        def body(i, _):
            a, b = i // 4, i % 4
            self.add((a, b, self.y, HALF[1]), g.first, self.yb[g.f, a, b, :, :g.wf])
            return 0
        lax.fori_loop(0, 8, body, 0)
        self.c_xb(g).start()
        self.z_step(g, 2, True)

    def step3(self, g):
        self.c_ya(g).wait_recv()
        self.c_xb(g).wait_recv()

        def body(b, _):
            self.add((self.s, b, self.y, HALF[0]), g.first, self.ya[g.r, b, :, :g.wf])
            self.add((self.s, b, self.y, HALF[1]), g.first, self.xb[g.r, b, :, :g.wf])
            return 0
        lax.fori_loop(0, 4, body, 0)
        self.z_step(g, 1, False)
        self.z_step(g, 3, True)

    def step4(self, g):
        self.z_step(g, 2, False)
        if not g.wl:
            return
        self.z_step(g, 4, True)
        z = self.z
        rows = slice(None)

        @pl.when(z > 0)
        def _():
            def body(i, _):
                a, b = i // 2, i % 2
                self.add((a, z, b, rows), g.last, self.zuc[g.g, a, z - 1, b, :, :g.wl])
                return 0
            lax.fori_loop(0, 4, body, 0)

        @pl.when(z < 3)
        def _():
            def body(i, _):
                a, b = i // 2, i % 2
                self.add((a, z, b, rows), g.last, self.zdc[g.g, a, z, b, :, :g.wl])
                return 0
            lax.fori_loop(0, 4, body, 0)
        self.c_xc(g).start()

    def step5(self, g):
        self.z_step(g, 3, False)
        if not g.wl:
            return
        self.c_xc(g).wait_recv()
        for b in range(2):
            self.add((self.s, self.z, b, slice(None)), g.last, self.xc[g.r, b, :, :g.wl])
        self.c_yc(g).start()

    def step6(self, g):
        self.z_step(g, 4, False)
        z = self.z
        k = g.p % 2
        if g.p >= 2:
            self.c_out(Piece(g.p - 2)).wait()
        mine = self.parts[self.s, z, self.y, :, g.first].astype(jnp.float32)

        @pl.when(z == 0)
        def _():
            self.stage[k, :, :g.wf] = mine + self.zd[g.q, 0, :, :g.wf].astype(jnp.float32)

        @pl.when(z == 3)
        def _():
            self.stage[k, :, :g.wf] = mine + self.zu[g.q, 2, :, :g.wf].astype(jnp.float32)

        @pl.when((z > 0) & (z < 3))
        def _():
            self.stage[k, :, :g.wf] = ((mine + self.zu[g.q, z - 1, :, :g.wf].astype(jnp.float32))
                                       + self.zd[g.q, z, :, :g.wf].astype(jnp.float32))
        if g.wl:
            self.c_yc(g).wait_recv()
            self.stage[k, :, g.wf:g.wf + g.wl] = (self.parts[self.s, z, self.y, :, g.last].astype(jnp.float32)
                                                  + self.yc[g.r, :, :g.wl].astype(jnp.float32))
        self.c_out(g).start()

    def c_out(self, g):
        k = g.p % 2
        return pltpu.make_async_copy(self.stage.at[k, :, :g.wf + g.wl], self.out.at[:, g.all], self.out_sem.at[k])

    def tick(self, t):
        steps = (self.step2, self.step3, self.step4, self.step5, self.step6)
        for k, step in enumerate(steps):
            if 0 <= t - 1 - k < NS:
                step(Piece(t - 1 - k))

    def serve(self, point):
        for what, n in PLAN[point]:
            self.tick(n) if what == "round" else self.step1(Piece(n))

    def finish(self):
        self.c_out(Piece(NS - 2)).wait()
        self.c_out(Piece(NS - 1)).wait()
        for p in range(NS):
            g = Piece(p)
            self.c_xa(g).wait_send()
            self.c_yb(g).wait_send()
            self.c_ya(g).wait_send()
            self.c_xb(g).wait_send()
            if g.wl:
                self.c_xc(g).wait_send()
                self.c_yc(g).wait_send()
        for z in range(4):
            @pl.when(self.z == z)
            def _(z=z):
                for p in range(NS):
                    g = Piece(p)
                    if z < 3:
                        self.c_up(g, z).wait_send()
                        if g.wl:
                            self.c_upc(g, z).wait_send()
                    if z > 0:
                        self.c_down(g, z).wait_send()
                        if g.wl:
                            self.c_downc(g, z).wait_send()


P_SCRATCH = [pltpu.VMEM((2, 4, 2, 32, FLAT), jnp.bfloat16)]
RECV_SCRATCH = [
    pltpu.VMEM((N1, 4, 2, 16, MOST_FIRST), jnp.bfloat16),
    pltpu.VMEM((N1, 2, 4, 16, MOST_FIRST), jnp.bfloat16),
    pltpu.VMEM((NR, 4, 16, MOST_FIRST), jnp.bfloat16),
    pltpu.VMEM((NR, 4, 16, MOST_FIRST), jnp.bfloat16),
    pltpu.VMEM((NZ, 3, 32, MOST_FIRST), jnp.bfloat16),
    pltpu.VMEM((NZ, 3, 32, MOST_FIRST), jnp.bfloat16),
    pltpu.VMEM((NZ1, 2, 3, 2, 32, MOST_LAST), jnp.bfloat16),
    pltpu.VMEM((NZ1, 2, 3, 2, 32, MOST_LAST), jnp.bfloat16),
    pltpu.VMEM((NR, 2, 32, MOST_LAST), jnp.bfloat16),
    pltpu.VMEM((NR, 32, MOST_LAST), jnp.bfloat16),
]

def greet():
    s, t, z, y, c = place()
    bar = pltpu.get_barrier_semaphore()

    def tell(dev):
        pl.semaphore_signal(bar, inc=1, device_id=dev, device_id_type=MESH_ID)
    tell({"seq": 1 - s, "tm": t})
    tell({"seq": s, "tm": t + 2 - 4 * y})
    tell({"seq": s, "tm": t + 1 - 2 * c})

    @pl.when(z < 3)
    def _():
        tell({"seq": s, "tm": t + 4})

    @pl.when(z > 0)
    def _():
        tell({"seq": s, "tm": t - 4})
    far = jnp.where(c == 1, t + 1, t - 1)
    has_far = (far >= 0) & (far < 16)

    @pl.when(has_far)
    def _():
        tell({"seq": s, "tm": far})
    return bar, 3 + jnp.where(has_far, 1, 0) + jnp.where(z < 3, 1, 0) + jnp.where(z > 0, 1, 0)


D = 1024
FF = 4096
SEG = 256
HD = H * DH
HH = HD // 2
WIDE = H * E * DH
FFB = 512
NFF = FF // FFB
NG = 4
LOGIT = 64
OWN_SIB = 24
F32 = jnp.float32
BF = jnp.bfloat16


def dot(a, b):
    return jnp.dot(a, b, preferred_element_type=F32)


def dot_nt(a, b):
    return lax.dot_general(a, b, (((1,), (1,)), ((), ())), preferred_element_type=F32)


def dot_tn(a, b):
    return lax.dot_general(a, b, (((0,), (0,)), ((), ())), preferred_element_type=F32)


def halves(v):
    top = v.astype(BF)
    return top, (v - top.astype(F32)).astype(BF)


def unit_rows(v):
    centre = v - jnp.mean(v, axis=-1, keepdims=True)
    spread = jnp.mean(centre * centre, axis=-1, keepdims=True)
    inv = lax.rsqrt(spread + epsilon)
    return centre * inv, inv


def norm_back(unit, inv, cot):
    return inv * (cot - jnp.mean(cot, axis=-1, keepdims=True)
                  - unit * jnp.mean(cot * unit, axis=-1, keepdims=True))


def normal_cdf(v, bell):
    u = 1.0 / (1.0 + 0.23164189 * jnp.abs(v))
    poly = ((((0.5307027145 * u - 0.7265760135) * u + 0.7107068705) * u - 0.142248368) * u + 0.127414796) * u
    tail = poly * bell
    return jnp.where(v < 0.0, tail, 1.0 - tail)


def for_rows(step, body):
    def inner(i, _):
        body(pl.ds(pl.multiple_of(i * step, step), step))
        return 0
    lax.fori_loop(0, SEG // step, inner, 0)


def side_by_side(blocks):
    return jnp.concatenate(blocks, axis=1)


NAMES = (
    "x", "oc", "gains", "rt", "rf", "spread", "hot", "wq", "wk", "wr", "wrp", "wu", "wd", "exv", "exo",
    "xn", "hn", "mid", "lo", "nsc", "q", "k", "v", "sig", "att", "acc", "g_o", "g_p",
    "act", "uc", "bc", "kc", "vc", "kn", "vn", "ob", "gg", "ogc", "qc", "vg", "ac", "acc2", "up",
    "at", "full",
    "ld", "ld2", "lde", "kv_s", "kv_r", "sib_s", "sib_r", "st", "stage", "out_sem", "ssem", "rsem",
)


def layer_scratch():
    dma = pltpu.SemaphoreType.DMA
    v = pltpu.VMEM
    return [
        v((SEG, D), BF), v((SEG, D), BF), v((2, D), BF), v((2 * H, 2, SEG), jnp.int32), v((128, SEG), BF),
        v((128, 256), BF), v((SEG, 128), F32),
        v((HD, D), BF), v((HD, D), BF), v((2 * H * E, D), BF), v((128, D), BF),
        v((2, D, FFB), BF), v((2, FFB, D), BF), v((2, E, 256, HH), BF), v((2, E, 256, HH), BF),
        v((SEG, D), BF), v((SEG, D), BF), v((SEG, D), F32), v((SEG, D), F32), v((SEG, D), F32),
        v((2, SEG, HH), BF), v((2, 2 * SEG, HH), BF), v((2, 2 * SEG, HH), BF), v((SEG, 128), F32),
        v((2, SEG, HH), BF), v((2, 2 * SEG, HH), F32), v((2 * SEG, 2304), BF), v((2 * SEG, 3328), BF),
        v((NG, 2 * SEG, FFB), BF), v((NG, 2 * SEG, FFB), BF), v((SEG, D), BF),
        v((2, 2 * SEG, HH), BF), v((2, 2 * SEG, HH), BF), v((2, SEG, HH), BF), v((2, SEG, HH), BF), v((SEG, D), BF), v((SEG, 256), BF),
        v((SEG, 128), F32), v((2, SEG, HH), F32), v((2, SEG, 128), F32),
        v((2, SEG, HH), BF), v((2, 2 * SEG, HH), F32), v((SEG, FFB), F32),
        v((6, 16, 32, 2 * SEG), BF), v((2, 16, 2, 32, SEG), BF),
        dma((16,)), dma((4,)), dma((2, 2 * E)), dma((5,)), dma((5,)), dma((OWN_SIB,)), dma((OWN_SIB,)), dma((2,)),
        v((2, 32, MOST), F32), dma((2,)), dma((10, NS)), dma((10, NS)),
    ]


def layer_kernel(x_h, rt_h, len_s, gains_h, wq_h, wk_h, wv_h, wr_h, wo_h, wu_h, wd_h, oc_h,
                 spread_h, lo_h, ig_h, flat_h, *scratch):
    m = types.SimpleNamespace(**dict(zip(NAMES, scratch[:len(NAMES)])))
    recv = scratch[len(NAMES):]
    s, t, z, y, c = place()
    last_t = lax.axis_size("tm") - 1
    sib = {"seq": s, "tm": t + 1 - 2 * c}
    scale = DH ** -0.5
    own = slice(SEG, 2 * SEG)
    mem = slice(0, SEG)

    bar, peers = greet()

    def load(i, src, dst):
        cp = pltpu.make_async_copy(src, dst, m.ld.at[i])
        cp.start()
        return cp

    def sibling(i, src, dst):
        return pltpu.make_async_remote_copy(
            src_ref=src, dst_ref=dst, send_sem=m.sib_s.at[i], recv_sem=m.sib_r.at[i],
            device_id=sib, device_id_type=MESH_ID)

    def at_copy(i, slot):
        return sibling(i, m.full.at[slot, :, 1 - c], m.at.at[i, :, :, SEG:])

    def turn(i, slot, value):
        m.full[slot] = jnp.transpose(value).reshape(16, 2, 32, SEG)
        m.at[i, :, :, :SEG] = m.full[slot, :, c]
        at_copy(i, slot).start()

    def go_copy():
        return sibling(6, m.g_o.at[mem], m.g_o.at[own])

    def gp_copy():
        return sibling(7, m.g_p.at[mem], m.g_p.at[own])

    def ff_copies(j):
        return act_copy(j), uc_copy(j)

    def act_copy(j):
        g = rem(j, NG)
        return sibling(8 + 2 * j, m.act.at[g, mem], m.act.at[g, own])

    def uc_copy(j):
        g = rem(j, NG)
        return sibling(9 + 2 * j, m.uc.at[g, mem], m.uc.at[g, own])

    def ff_loads(j):
        return wu_load(j), wd_load(j)

    def wu_load(j):
        cols = pl.ds(pl.multiple_of(j * FFB, FFB), FFB)
        return pltpu.make_async_copy(wu_h.at[:, cols], m.wu.at[rem(j, 2)], m.ld2.at[rem(j, 2)])

    def wd_load(j):
        rows = pl.ds(pl.multiple_of(j * FFB, FFB), FFB)
        return pltpu.make_async_copy(wd_h.at[rows, :], m.wd.at[rem(j, 2)], m.ld2.at[2 + rem(j, 2)])

    def along(i, src, dst, by):
        return pltpu.make_async_remote_copy(
            src_ref=src, dst_ref=dst, send_sem=m.kv_s.at[i], recv_sem=m.kv_r.at[i],
            device_id={"seq": s, "tm": t + by}, device_id_type=MESH_ID)

    def k_copy():
        return along(0, m.k.at[:, own], m.k.at[:, mem], 1)

    def v_copy(half):
        return along(1 + half, m.v.at[half, own], m.v.at[half, mem], 1)

    def kc_copy():
        return along(3, m.kc.at[:, mem], m.kn, -1)

    def vc_copy():
        return along(4, m.vc.at[:, mem], m.vn, -1)

    def half_rows(half):
        return slice(half * HH, (half + 1) * HH)

    def head_only(v, h):
        lane = lax.broadcasted_iota(jnp.int32, v.shape, 1)
        lo = rem(h, 2) * DH
        return jnp.where((lane >= lo) & (lane < lo + DH), v, jnp.zeros_like(v))

    def gates_wide(table, half, e):
        return dot(m.gg[...], table[half, e])

    def make_table(table, first):
        row = lax.broadcasted_iota(jnp.int32, (256, HH), 0)
        lane = lax.broadcasted_iota(jnp.int32, (256, HH), 1)
        row = jnp.where(row >= 128, row - 128, row) - first - jnp.where(lane >= DH, E, 0)
        for half in range(2):
            for e in range(E):
                table[half, e] = jnp.where(row == 2 * E * half + e, 1.0, 0.0).astype(BF)

    def expert_loads(which, n, e, src, dst):
        return [pltpu.make_async_copy(src.at[pl.ds((h * E + e) * DH, DH)], dst.at[pl.ds(h * DH, DH)], m.lde.at[which, n])
                for h in range(H)]

    def ring(n):
        return expert_loads(0, n, n % E, wo_h if n < E else wv_h, m.wd.at[n % 2])

    def weights_of(h):
        half = h // 2
        scores = dot_nt(head_only(m.q[half], h), m.k[half]) * scale
        length = len_s[0, 0]
        row = lax.broadcasted_iota(jnp.int32, (SEG, 2 * SEG), 0)
        col = lax.broadcasted_iota(jnp.int32, (SEG, 2 * SEG), 1)
        allowed = ((col < SEG) & (col >= SEG - length)) | ((col >= SEG) & (col - SEG <= row))
        scores = jnp.where(allowed, scores, -1e30)
        e = jnp.exp(scores - jnp.max(scores, axis=-1, keepdims=True))
        return e / jnp.sum(e, axis=-1, keepdims=True)

    l_x = load(0, x_h, m.x)
    l_g = load(1, gains_h, m.gains)
    l_k = load(2, wk_h, m.wk)
    l_r = load(3, wr_h, m.wr)
    l_rt = load(4, rt_h, m.rt)
    l_sp = load(12, spread_h, m.spread)

    def forward(wv, wo, wide):
        l_v = [expert_loads(0, e, e, wv_h, wv.at[e]) for e in range(E)]
        for group in l_v:
            for cp in group:
                cp.start()
        make_table(m.exv, LOGIT)
        l_x.wait()
        l_g.wait()

        def norm1(rows):
            unit, _ = unit_rows(m.x[rows, :].astype(F32))
            m.xn[rows, :] = (unit * m.gains[0:1, :].astype(F32)).astype(BF)
        for_rows(32, norm1)
        l_k.wait()
        for half in range(2):
            m.k[half, own] = dot_nt(m.xn[...], m.wk[half_rows(half), :]).astype(BF)
        l_q = load(8, wq_h, m.wq)
        l_oc = load(9, oc_h, m.oc)
        l_wo = [expert_loads(1, e, e, wo_h, wo.at[pl.ds(e * HD, HD)]) for e in range(E)]
        for group in l_wo:
            for cp in group:
                cp.start()
        for j in range(2):
            for cp in ff_loads(j):
                cp.start()
        pl.semaphore_wait(bar, peers)

        @pl.when(t < last_t)
        def _():
            k_copy().start()
        l_r.wait()
        m.wrp[...] = jnp.zeros((128, D), BF)
        m.wrp[LOGIT:LOGIT + 2 * H * E, :] = m.wr[...]
        sig = jax.nn.sigmoid(dot_nt(m.xn[...], m.wrp[...]))
        l_rt.wait()
        l_sp.wait()
        m.rf[...] = jnp.zeros((128, SEG), BF)
        for i in range(2):
            m.rf[16 * i:16 * i + 2 * H, :] = m.rt[:, i, :].astype(F32).astype(BF)
        named = dot_tn(m.rf[...], m.spread[...])
        expert = m.spread[127:128, :128].astype(F32)
        hit = (named[:, :128] == expert) | (named[:, 128:] == expert)
        m.hot[...] = jnp.where(hit, 1.0, 0.0)
        m.sig[...] = sig
        top, low = halves(sig * m.hot[...])
        m.gg[:, :128] = top
        m.gg[:, 128:] = low
        for half in range(2):
            total = jnp.zeros((SEG, HH), F32)
            for e in range(E):
                if half == 0:
                    for cp in l_v[e]:
                        cp.wait()
                total = total + dot_nt(m.xn[...], wv[e, half_rows(half)]) * gates_wide(m.exv, half, e)
            m.v[half, own] = total.astype(BF)

            @pl.when(t < last_t)
            def _():
                v_copy(half).start()
        l_q.wait()
        for half in range(2):
            m.q[half] = dot_nt(m.xn[...], m.wq[half_rows(half), :]).astype(BF)
        l_oc.wait()
        turn(0, 0, m.oc[...])
        turn(3, 1, m.xn[...])
        make_table(m.exo, LOGIT + H * E)

        @pl.when(t > 0)
        def _():
            k_copy().wait_recv()

        @pl.when(t == 0)
        def _():
            m.k[:, mem] = jnp.zeros((2, SEG, HH), BF)
            m.v[:, mem] = jnp.zeros((2, SEG, HH), BF)
        for h in range(H):
            m.act[h, mem] = weights_of(h).astype(BF)
        for half in range(2):
            for e in range(E):
                wide[half, e] = gates_wide(m.exo, half, e)
        for cp in ff_loads(0):
            cp.wait()
        m.up[...] = dot_nt(m.oc[...], m.wd[0])
        m.g_o[mem, 2176:2304] = jnp.zeros((SEG, 128), BF)
        for half in range(2):
            @pl.when(t > 0)
            def _():
                v_copy(half).wait_recv()
            total = jnp.zeros((SEG, HH), F32)
            for h in (2 * half, 2 * half + 1):
                total = total + dot(m.act[h, mem], head_only(m.v[half], h))
            m.att[half] = total.astype(BF)
        att = [m.att[half].astype(F32) for half in range(2)]
        for e in range(0, E, 2):
            blocks = [(wide[half, i] * att[half]).astype(BF) for i in range(e, min(e + 2, E)) for half in range(2)]
            m.g_o[mem, e * HD:min(e + 2, E) * HD] = side_by_side(blocks)
        go_copy().start()
        for group in l_wo:
            for cp in group:
                cp.wait()
        m.mid[...] = m.x[...].astype(F32) + dot(m.g_o[mem, :WIDE], wo[...])

        def norm2(rows):
            unit, _ = unit_rows(m.mid[rows, :])
            m.hn[rows, :] = (unit * m.gains[1:2, :].astype(F32)).astype(BF)
        for_rows(32, norm2)
        at_copy(0, 0).wait_send()
        turn(1, 0, m.hn[...])

    pl.run_scoped(forward, pltpu.VMEM((E, HD, D), BF), pltpu.VMEM((WIDE, D), BF), pltpu.VMEM((2, E, SEG, HH), F32))

    def backward(parts):
        ex = Exchange(parts, recv, (m.ssem, m.rsem), m.stage, m.out_sem, flat_h)

        def product(i, g):
            return dot(m.at[i].reshape(512, 2 * SEG), g)

        def tiles(i, g, tile):
            store_tile(parts, tile, product(i, g))

        m.lo[...] = m.mid[...]
        m.nsc[...] = jnp.zeros((SEG, D), F32)
        at_copy(0, 0).wait_recv()
        at_copy(1, 0).wait_recv()

        def block(j, _):
            b = rem(j, 2)
            g = rem(j, NG)

            @pl.when(j > 0)
            def _():
                wu_load(j).wait()

            @pl.when(j >= NG)
            def _():
                for cp in ff_copies(j - NG):
                    cp.wait_send()
            pre = dot(m.hn[...], m.wu[b])
            bell = jnp.exp(-0.5 * pre * pre)
            cdf = normal_cdf(pre, bell)
            m.act[g, mem] = (pre * cdf).astype(BF)
            act_copy(j).start()
            pdf = bell * 0.3989422804014327
            m.uc[g, mem] = (m.up[...] * (cdf + pre * pdf)).astype(BF)
            uc_copy(j).start()

            @pl.when(j > 2)
            def _():
                act_grad(j - 1)
                up_grad(j - 1)
            m.lo[...] += dot(m.act[g, mem], m.wd[b])
            m.nsc[...] += dot_nt(m.uc[g, mem], m.wu[b])

            @pl.when(j + 2 < NFF)
            def _():
                for cp in ff_loads(j + 2):
                    cp.start()

            @pl.when(j == 0)
            def _():
                act_grad(0)
                ex.serve("d0")
                up_grad(0)
                ex.serve("u0")

            @pl.when(j + 1 < NFF)
            def _():
                wd_load(j + 1).wait()
                m.up[...] = dot_nt(m.oc[...], m.wd[rem(j + 1, 2)])

            @pl.when(j == 1)
            def _():
                act_grad(1)
                up_grad(1)
            for i in range(1, NFF):
                if PLAN[f"j{i}"]:
                    pl.when(j == i)(lambda i=i: ex.serve(f"j{i}"))
            return 0

        def act_grad(j):
            act_copy(j).wait_recv()
            tiles(0, m.act[rem(j, NG)], 8 * j)

        def up_grad(j):
            uc_copy(j).wait_recv()
            tiles(1, m.uc[rem(j, NG)], 8 * j + 4)
        lax.fori_loop(0, NFF, block, 0)
        for n in range(2):
            for cp in ring(n):
                cp.start()
        act_grad(NFF - 1)
        up_grad(NFF - 1)
        ex.serve("dw7")
        for j in range(NFF - NG, NFF):
            for cp in ff_copies(j):
                cp.wait_send()
        m.ob[...] = m.lo[...].astype(BF)
        l_lo = pltpu.make_async_copy(m.ob, lo_h, m.st.at[0])
        l_lo.start()

        def norm2_back(rows):
            unit, inv = unit_rows(m.mid[rows, :])
            cot = m.nsc[rows, :]
            mcot = m.oc[rows, :].astype(F32) + norm_back(unit, inv, cot * m.gains[1:2, :].astype(F32))
            m.lo[rows, :] = mcot
            m.bc[rows, :] = mcot.astype(BF)
            m.hn[rows, :] = (cot * unit).astype(BF)
        for_rows(32, norm2_back)
        at_copy(3, 1).wait_send()
        turn(2, 1, m.bc[...])
        at_copy(1, 0).wait_send()
        turn(5, 0, m.hn[...])
        ex.serve("ln2b")

        def ring_next(n):
            if n + 2 < 2 * E:
                for cp in ring(n + 2):
                    cp.start()

        att = [m.att[half].astype(F32) for half in range(2)]
        seen = jnp.zeros((SEG, 128), F32)
        total = [jnp.zeros((SEG, HH), F32)] * 2
        for e in range(E):
            for cp in ring(e):
                cp.wait()
            cots = [dot_nt(m.bc[...], m.wd[e % 2, half_rows(half)]) for half in range(2)]
            ring_next(e)
            for half, cot in enumerate(cots):
                seen = seen + dot_nt((cot * att[half]).astype(BF), m.exo[half, e, :128])
                total[half] = total[half] + cot * gates_wide(m.exo, half, e)
            ex.serve(f"tho{e}")
        m.ogc[...] = seen
        for half in range(2):
            m.ac[half] = total[half].astype(BF)

        m.acc[...] = jnp.zeros((2, 2 * SEG, HH), F32)
        m.acc2[...] = jnp.zeros((2, 2 * SEG, HH), F32)
        m.qc[...] = jnp.zeros((2, SEG, HH), F32)

        def scores_back(h):
            half = h // 2
            probs = weights_of(h)
            cot = head_only(m.ac[half], h)
            m.acc2[half] += dot_tn(probs.astype(BF), cot)
            pc = dot_nt(cot, m.v[half])
            sc = (probs * (pc - jnp.sum(probs * pc, axis=-1, keepdims=True))).astype(BF)
            m.qc[half] += dot(sc, head_only(m.k[half], h)) * scale
            m.acc[half] += dot_tn(sc, head_only(m.q[half], h)) * scale
        for i in range(2):
            scores_back(2 * i)
            scores_back(2 * i + 1)
            ex.serve(f"sb{i}")
        m.vc[...] = m.acc2[...].astype(BF)
        m.kc[...] = m.acc[...].astype(BF)

        @pl.when(t > 0)
        def _():
            vc_copy().start()
            kc_copy().start()
        go_copy().wait_recv()
        at_copy(2, 1).wait_recv()

        for i in range(3):
            tiles(2, m.g_o[:, 6 * TILE * i:6 * TILE * (i + 1)], 64 + 6 * i)
            ex.serve(f"dwo{i}")
        m.g_p[mem, HD:512] = jnp.zeros((SEG, 512 - HD), BF)
        m.g_p[mem, 512 + HD:1024] = jnp.zeros((SEG, 512 - HD), BF)
        m.g_p[mem, :HD] = side_by_side([m.qc[half].astype(BF) for half in range(2)])

        @pl.when(t < last_t)
        def _():
            vc_copy().wait_recv()
            kc_copy().wait_recv()

        @pl.when(t == last_t)
        def _():
            m.kn[...] = jnp.zeros((2, SEG, HH), BF)
            m.vn[...] = jnp.zeros((2, SEG, HH), BF)
        m.g_p[mem, 512:512 + HD] = side_by_side(
            [(m.kc[half, own].astype(F32) + m.kn[half].astype(F32)).astype(BF) for half in range(2)])
        l_lo.wait()

        own_cot, next_cot = m.mid, m.nsc

        own_cot[...] = (dot(m.g_p[mem, :HD], m.wq[...])
                        + sum(dot(m.kc[half, own], m.wk[half_rows(half), :]) for half in range(2)))
        next_cot[...] = sum(dot(m.kn[half], m.wk[half_rows(half), :]) for half in range(2))
        m.vg[...] = jnp.zeros((2, SEG, 128), F32)
        blocks = []
        for e in range(E):
            for cp in ring(E + e):
                cp.wait()
            wv = m.wd.at[(E + e) % 2]
            pairs = []
            for half in range(2):
                proj = dot_nt(m.xn[...], wv[half_rows(half)])
                gate = gates_wide(m.exv, half, e)
                pair = []
                for i, v in enumerate((m.vc[half, own], m.vn[half])):
                    v = v.astype(F32)
                    m.vg[i] += dot_nt((v * proj).astype(BF), m.exv[half, e, :128])
                    pair.append((gate * v).astype(BF))
                blocks.append((pair[0].astype(F32) + pair[1].astype(F32)).astype(BF))
                pairs.append(pair)
            for i, acc in enumerate((own_cot, next_cot)):
                acc[...] += dot(side_by_side([pair[i] for pair in pairs]), wv[:HD])
            ring_next(E + e)
            ex.serve(f"tv{e}")
            if e % 2 == 1 or e == E - 1:
                first = e - 1 if e % 2 == 1 else e
                m.g_p[mem, 1024 + first * HD:1024 + (e + 1) * HD] = side_by_side(blocks[2 * first:])
        slope = m.sig[...] * (1.0 - m.sig[...]) * m.hot[...]
        lo_cot = ((m.vg[0] + m.ogc[...]) * slope).astype(BF)
        ln_cot = (m.vg[1] * slope).astype(BF)
        own_cot[...] += dot(lo_cot, m.wrp[...])
        next_cot[...] += dot(ln_cot, m.wrp[...])
        both = (lo_cot.astype(F32) + ln_cot.astype(F32)).astype(BF)
        lane = lax.broadcasted_iota(jnp.int32, (SEG, 128), 1)
        m.g_p[mem, 3200:3328] = jnp.where(lane < LOGIT, m.g_p[mem, 3200:3328], both)
        gp_copy().start()

        def norm1_back(rows):
            unit, inv = unit_rows(m.x[rows, :].astype(F32))
            cot = own_cot[rows, :]
            m.lo[rows, :] += norm_back(unit, inv, cot * m.gains[0:1, :].astype(F32))
            m.hn[rows, :] = ((cot + next_cot[rows, :]) * unit).astype(BF)
        for_rows(32, norm1_back)
        l_ig = pltpu.make_async_copy(m.lo, ig_h, m.st.at[1])
        l_ig.start()
        at_copy(2, 1).wait_send()
        turn(4, 1, m.hn[...])
        ex.serve("ln1b")
        gp_copy().wait_recv()
        at_copy(3, 1).wait_recv()

        for i in range(6):
            tiles(3, m.g_p[:, 4 * TILE * i:4 * TILE * (i + 1)], 82 + 4 * i)
            if i in (1, 3):
                ex.serve(f"dwp{i // 2}")
        last = product(3, m.g_p[:, 3072:3328])
        store_tile(parts, 106, last[:, :TILE])
        last = last[:, TILE:]
        lane = lax.broadcasted_iota(jnp.int32, (2 * SEG, TILE), 1)
        at_copy(5, 0).wait_recv()
        at_copy(4, 1).wait_recv()
        for i, at in ((4, 104), (5, 105)):
            last += product(i, jnp.where(lane == at, 1.0, 0.0).astype(BF))
        store_tile(parts, 107, last)

        ex.serve("dwp2")
        ex.serve("rest")
        ex.finish()
        l_ig.wait()

    pl.run_scoped(backward, *P_SCRATCH)
    at_copy(5, 0).wait_send()
    at_copy(4, 1).wait_send()
    go_copy().wait_send()
    gp_copy().wait_send()

    @pl.when(t < last_t)
    def _():
        k_copy().wait_send()
        v_copy(0).wait_send()
        v_copy(1).wait_send()

    @pl.when(t > 0)
    def _():
        kc_copy().wait_send()
        vc_copy().wait_send()


def tables():
    lane = np.arange(128) - LOGIT
    inside = (lane >= 0) & (lane < 2 * H * E)
    pick = (np.arange(2 * H)[:, None] == lane[None, :] // E) & inside
    spread = np.zeros((128, 256), np.float32)
    spread[:2 * H, :128] = pick
    spread[16:16 + 2 * H, 128:] = pick
    spread[127, :128] = np.where(inside, lane % E, -1)
    return spread.astype(ml_dtypes.bfloat16)


def fused_device(layer_input, routes, memory_lengths, norm_gains, w_query, w_key, w_value,
                 w_router, w_output, w_up, w_down, output_cot):
    anywhere = pl.BlockSpec(memory_space=pl.ANY)
    specs = [anywhere] * 13
    specs[2] = pl.BlockSpec(memory_space=pltpu.SMEM)
    out, grad, flat = pl.pallas_call(
        layer_kernel,
        out_shape=(jax.ShapeDtypeStruct((SEG, D), BF), jax.ShapeDtypeStruct((SEG, D), F32),
                   jax.ShapeDtypeStruct((32, FLAT), F32)),
        in_specs=specs,
        out_specs=(anywhere,) * 3,
        scratch_shapes=layer_scratch() + RECV_SCRATCH,
        compiler_params=pltpu.CompilerParams(
            collective_id=0, has_side_effects=True, vmem_limit_bytes=VMEM_LIMIT),
        name="layer",
    )(layer_input[0], jnp.transpose(routes[0], (1, 2, 0)), memory_lengths, norm_gains, w_query.T, w_key.T, w_value.T, w_router.T,
      w_output, w_up, w_down, output_cot[0], tables())
    shapes = ((SEG, D), BF), ((SEG, D), F32), ((2, 32), F32), ((32, HD), F32), ((32, HD), F32), \
        ((32, WIDE), F32), ((32, 2 * H * E), F32), ((32, WIDE), F32), ((32, FF), F32), ((32, FF), F32)
    vm = pl.BlockSpec(memory_space=pltpu.VMEM)
    res = pl.pallas_call(
        split_kernel,
        out_shape=tuple(jax.ShapeDtypeStruct(*v) for v in shapes),
        in_specs=(anywhere, anywhere, anywhere),
        out_specs=(vm,) * 10,
        scratch_shapes=[pltpu.VMEM((32, FLAT), F32), pltpu.SemaphoreType.DMA((3,))],
        compiler_params=pltpu.CompilerParams(vmem_limit_bytes=VMEM_LIMIT),
        name="split",
    )(out, grad, flat)
    return (res[0][None], res[1][None], *res[2:7], res[7].T, res[8], res[9].T)


def split_kernel(out_h, grad_h, flat_h, lo, ig, gains, dq, dk, dv, dr, do, du, dd, flat, sem):
    copies = [pltpu.make_async_copy(flat_h, flat, sem.at[2]), pltpu.make_async_copy(out_h, lo, sem.at[0]),
              pltpu.make_async_copy(grad_h, ig, sem.at[1])]
    for cp in copies:
        cp.start()
    copies.pop(0).wait()
    for j in range(NFF):
        dd[:, j * FFB:(j + 1) * FFB] = flat[:, 2 * j * FFB:(2 * j + 1) * FFB]
        du[:, j * FFB:(j + 1) * FFB] = flat[:, (2 * j + 1) * FFB:(2 * j + 2) * FFB]
    base = 82 * TILE
    dq[...] = flat[:, base:base + HD]
    dk[...] = flat[:, base + 512:base + 512 + HD]
    for h in range(H):
        for e in range(E):
            to = slice((h * E + e) * DH, (h * E + e + 1) * DH)
            at = e * HD + h * DH
            do[:, to] = flat[:, 2 * FF + at:2 * FF + at + DH]
            dv[:, to] = flat[:, base + 1024 + at:base + 1024 + at + DH]
    tail = flat[:, 107 * TILE:108 * TILE]
    dr[...] = tail[:, LOGIT:LOGIT + 2 * H * E]
    gains[...] = jnp.transpose(tail)[104:106, :]
    for cp in copies:
        cp.wait()


def solution(mesh):
    placed = (
        P("seq", "tm", None),
        P("seq", "tm", None, None),
        P("seq", "tm"),
        P(),
        P(),
        P(),
        P(),
        P(),
        P(),
        P(),
        P(),
        P("seq", "tm", None),
    )
    fused = mesh.shape["seq"] == 2 and mesh.shape["tm"] == 16
    return jax.shard_map(
        fused_device if fused else per_device,
        mesh=mesh,
        in_specs=placed,
        out_specs=(
            P("seq", "tm", None),
            P("seq", "tm", None),
            P(None, ("seq", "tm")),
            P(("seq", "tm"), None),
            P(("seq", "tm"), None),
            P(("seq", "tm"), None),
            P(("seq", "tm"), None),
            P(None, ("seq", "tm")),
            P(("seq", "tm"), None),
            P(None, ("seq", "tm")),
        ),
        check_vma=False,
    )
```

```python
import types

import jax
import jax.numpy as jnp
import ml_dtypes
import numpy as np
from jax import lax
from jax.experimental import pallas as pl
from jax.experimental.pallas import tpu as pltpu
from jax.sharding import PartitionSpec as P

H = 4
DH = 112
E = 5


epsilon = 1e-05


def passed_along(value, axis, steps):
    count = lax.axis_size(axis)
    initial, last = (max(0, -steps), min(count, count - steps))
    return lax.ppermute(value, axis, [(source, source + steps) for source in range(initial, last)])


def normalize(values, gain_vec):
    centre = values - jnp.mean(values, axis=-1, keepdims=True)
    spread = jnp.mean(centre * centre, axis=-1, keepdims=True)
    return centre * lax.rsqrt(spread + epsilon) * gain_vec


def exact_gelu(arg_in):
    return jax.nn.gelu(arg_in, approximate=False)


def matmul(left_op, right_op):
    return jnp.dot(left_op, right_op, preferred_element_type=jnp.float32)


def times_tr(left_op, right_op):
    return lax.dot_general(
        left_op, right_op, (((1,), (1,)), ((), ())), preferred_element_type=jnp.float32
    )


def tr_times(left_op, right_op):
    return lax.dot_general(
        left_op, right_op, (((0,), (0,)), ((), ())), preferred_element_type=jnp.float32
    )


def one_hot_routes(route_ids):
    return jnp.sum(
        (route_ids[..., None] == jnp.arange(E, dtype=jnp.int32)).astype(jnp.float32), axis=-2
    )


def attention_mask(memory_length, seg_len):
    query_pos = jnp.arange(seg_len, dtype=jnp.int32)[:, None]
    key_pos = jnp.arange(2 * seg_len, dtype=jnp.int32)[None, :]
    return jnp.where(
        key_pos < seg_len, key_pos >= seg_len - memory_length, key_pos - seg_len <= query_pos
    )


def per_device(
    layer_input,
    routes,
    memory_lengths,
    norm_gains,
    w_query,
    w_key,
    w_value,
    w_router,
    w_output,
    w_up,
    w_down,
    output_cot,
):
    seg_len = layer_input.shape[1]
    own_rows = layer_input[0].astype(jnp.float32)
    memory_length = memory_lengths[0, 0]
    gains_f = norm_gains.astype(jnp.float32)
    first_gain = gains_f[0]
    second_gain = gains_f[1]
    scale_factor = DH ** (-0.5)
    allowed = attention_mask(memory_length, seg_len)
    onehot = one_hot_routes(routes[0])
    unit_normed = normalize(own_rows, jnp.ones_like(first_gain))
    own_normed = (unit_normed * first_gain).astype(jnp.bfloat16)

    def projections():
        queries = matmul(own_normed, w_query).astype(jnp.bfloat16)
        key_own = matmul(own_normed, w_key).astype(jnp.bfloat16)
        logits = matmul(own_normed, w_router).reshape(seg_len, 2 * H, E)
        gate_sig = jax.nn.sigmoid(logits)
        gate_vals = gate_sig * onehot
        projected = matmul(own_normed, w_value).reshape(seg_len, H, E, DH)
        value_own = (
            jnp.sum(gate_vals[:, :H, :, None] * projected, axis=2)
            .reshape(seg_len, H * DH)
            .astype(jnp.bfloat16)
        )
        return (queries, key_own, gate_sig, gate_vals, projected, value_own)

    queries, key_own, gate_sig, gate_vals, projected, value_own = projections()
    key_mem, value_mem = passed_along((key_own, value_own), "tm", 1)
    key_rows = jnp.concatenate([key_mem, key_own], axis=0)
    value_rows = jnp.concatenate([value_mem, value_own], axis=0)
    head_outs = []
    log_norms = []
    for head_idx in range(H):
        columns = slice(head_idx * DH, (head_idx + 1) * DH)
        scores = (
            jnp.einsum(
                "qd,kd->qk",
                queries[:, columns],
                key_rows[:, columns],
                preferred_element_type=jnp.float32,
            )
            * scale_factor
        )
        scores = jnp.where(allowed, scores, -1e30)
        peak = jnp.max(scores, axis=-1, keepdims=True)
        exp_scores = jnp.exp(scores - peak)
        total = jnp.sum(exp_scores, axis=-1, keepdims=True)
        weights = (exp_scores / total).astype(jnp.bfloat16)
        head_outs.append(matmul(weights, value_rows[:, columns]))
        log_norms.append(peak + jnp.log(total))
    attended = jnp.concatenate(head_outs, axis=1).astype(jnp.bfloat16)
    out_gates = gate_vals[:, H:]
    attended_f = attended.astype(jnp.float32).reshape(seg_len, H, 1, DH)
    mixed_in = (attended_f * out_gates[..., None]).reshape(seg_len, H * E * DH).astype(jnp.bfloat16)
    middle = own_rows + matmul(mixed_in, w_output)
    hidden_normed = normalize(middle, second_gain).astype(jnp.bfloat16)
    pre_act = matmul(hidden_normed, w_up)
    activated = exact_gelu(pre_act).astype(jnp.bfloat16)
    layer_out = middle + matmul(activated, w_down)
    output_block = layer_out.astype(jnp.bfloat16)[None]
    down_cot = output_cot[0]
    out_cot = down_cot.astype(jnp.float32)
    grad_down = tr_times(activated, down_cot)
    grad_act = times_tr(down_cot, w_down)
    unused_gelu, gelu_pull = jax.vjp(exact_gelu, pre_act)
    up_cot = gelu_pull(grad_act)[0].astype(jnp.bfloat16)
    grad_up = tr_times(hidden_normed, up_cot)
    normed_second_cot = times_tr(up_cot, w_up)
    unused_norm, second_pull = jax.vjp(normalize, middle, second_gain)
    middle_part, grad_second = second_pull(normed_second_cot)
    middle_cot = out_cot + middle_part
    branch_cot = middle_cot.astype(jnp.bfloat16)
    grad_output = tr_times(mixed_in, branch_cot)
    mixed_cot = times_tr(branch_cot, w_output).reshape(seg_len, H, E, DH)
    out_gate_cot = jnp.sum(mixed_cot * attended_f, axis=-1)
    attended_cot = (
        jnp.sum(mixed_cot * out_gates[..., None], axis=2)
        .reshape(seg_len, H * DH)
        .astype(jnp.bfloat16)
    )
    queries, key_own, gate_sig, gate_vals, projected, value_own = projections()
    key_back, value_back = passed_along((key_own, value_own), "tm", 1)
    key_rows = jnp.concatenate([key_back, key_own], axis=0)
    value_rows = jnp.concatenate([value_back, value_own], axis=0)
    query_grads = []
    key_grads = []
    value_grads = []
    for head_idx in range(H):
        columns = slice(head_idx * DH, (head_idx + 1) * DH)
        scores = (
            jnp.einsum(
                "qd,kd->qk",
                queries[:, columns],
                key_rows[:, columns],
                preferred_element_type=jnp.float32,
            )
            * scale_factor
        )
        scores = jnp.where(allowed, scores, -1e30)
        probs = jnp.exp(scores - log_norms[head_idx])
        weights = probs.astype(jnp.bfloat16)
        cot_head = attended_cot[:, columns]
        value_grads.append(tr_times(weights, cot_head))
        prob_cot = times_tr(cot_head, value_rows[:, columns])
        score_cot = (probs * (prob_cot - jnp.sum(probs * prob_cot, axis=-1, keepdims=True))).astype(
            jnp.bfloat16
        )
        query_grads.append(matmul(score_cot, key_rows[:, columns]) * scale_factor)
        key_grads.append(tr_times(score_cot, queries[:, columns]) * scale_factor)
    query_cot = jnp.concatenate(query_grads, axis=1).astype(jnp.bfloat16)
    key_cot_all = jnp.concatenate(key_grads, axis=1)
    value_cot_all = jnp.concatenate(value_grads, axis=1)
    key_mem_cot = key_cot_all[:seg_len].astype(jnp.bfloat16)
    key_own_cot = key_cot_all[seg_len:].astype(jnp.bfloat16)
    value_mem_cot = value_cot_all[:seg_len].astype(jnp.bfloat16)
    value_own_cot = value_cot_all[seg_len:].astype(jnp.bfloat16)
    key_next, value_next = passed_along((key_mem_cot, value_mem_cot), "tm", -1)
    own_vcot = value_own_cot.astype(jnp.float32).reshape(seg_len, H, 1, DH)
    next_vcot = value_next.astype(jnp.float32).reshape(seg_len, H, 1, DH)
    val_gates = gate_vals[:, :H, :, None]
    proj_own_cot = (val_gates * own_vcot).reshape(seg_len, H * E * DH).astype(jnp.bfloat16)
    proj_next_cot = (val_gates * next_vcot).reshape(seg_len, H * E * DH).astype(jnp.bfloat16)
    gate_own_cot = jnp.concatenate([jnp.sum(own_vcot * projected, axis=-1), out_gate_cot], axis=1)
    gate_next_cot = jnp.concatenate(
        [jnp.sum(next_vcot * projected, axis=-1), jnp.zeros_like(out_gate_cot)], axis=1
    )
    slope = gate_sig * (1.0 - gate_sig) * onehot
    logit_own_cot = (gate_own_cot * slope).reshape(seg_len, 2 * H * E).astype(jnp.bfloat16)
    logit_next_cot = (gate_next_cot * slope).reshape(seg_len, 2 * H * E).astype(jnp.bfloat16)
    twice_normed = jnp.concatenate([own_normed, own_normed], axis=0)
    key_both = jnp.concatenate([key_own_cot, key_next], axis=0)
    proj_both = jnp.concatenate([proj_own_cot, proj_next_cot], axis=0)
    logit_both = jnp.concatenate([logit_own_cot, logit_next_cot], axis=0)
    grad_query = tr_times(own_normed, query_cot)
    grad_key = tr_times(twice_normed, key_both)
    grad_value = tr_times(twice_normed, proj_both)
    grad_router = tr_times(twice_normed, logit_both)
    normed_both = (
        times_tr(key_both, w_key) + times_tr(proj_both, w_value) + times_tr(logit_both, w_router)
    )
    own_normed_cot = normed_both[:seg_len] + times_tr(query_cot, w_query)
    next_normed_cot = normed_both[seg_len:]
    grad_first = jnp.sum((own_normed_cot + next_normed_cot) * unit_normed, axis=0)
    unused_first, first_pull = jax.vjp(normalize, own_rows, first_gain)
    input_part = first_pull(own_normed_cot)[0]
    input_cot = middle_cot + input_part
    grad_gains = jnp.stack([grad_first, grad_second], axis=0)
    row_query, row_key, row_value, row_router, row_up = (
        lax.psum_scatter(grad_query, ("seq", "tm"), scatter_dimension=0, tiled=True),
        lax.psum_scatter(grad_key, ("seq", "tm"), scatter_dimension=0, tiled=True),
        lax.psum_scatter(grad_value, ("seq", "tm"), scatter_dimension=0, tiled=True),
        lax.psum_scatter(grad_router, ("seq", "tm"), scatter_dimension=0, tiled=True),
        lax.psum_scatter(grad_up, ("seq", "tm"), scatter_dimension=0, tiled=True),
    )
    col_gains, col_output, col_down = (
        lax.psum_scatter(grad_gains, ("seq", "tm"), scatter_dimension=1, tiled=True),
        lax.psum_scatter(grad_output, ("seq", "tm"), scatter_dimension=1, tiled=True),
        lax.psum_scatter(grad_down, ("seq", "tm"), scatter_dimension=1, tiled=True),
    )
    return (
        output_block,
        input_cot[None],
        col_gains,
        row_query,
        row_key,
        row_value,
        row_router,
        col_output,
        row_up,
        col_down,
    )


VMEM_LIMIT = 64 << 20

MESH_ID = pl.DeviceIdType.MESH
TILE = 128
PIECES = [(4, 2)] + [(7, 2)] * 10 + [(6, 2), (3, 1)]
NS = len(PIECES)
TILES = sum(a + b for a, b in PIECES)
FLAT = TILES * TILE
MOST_FIRST = max(a for a, _ in PIECES) * TILE
MOST_LAST = max(b for _, b in PIECES) * TILE
MOST = max(a + b for a, b in PIECES) * TILE
N1 = 6
NR = 4
NZ = 6
NZ1 = 7
HALF = (slice(0, 16), slice(16, 32))


POINTS = ([("d0", 4), ("u0", 8), ("j1", 16)] + [(f"j{j}", 8 * j) for j in range(2, 8)] + [("dw7", 64), ("ln2b", 64)]
          + [(f"tho{e}", 64) for e in range(E)] + [("sb0", 64), ("sb1", 64), ("dwo0", 70), ("dwo1", 76), ("dwo2", 82)]
          + [(f"tv{e}", 82) for e in range(E)] + [("ln1b", 82), ("dwp0", 90), ("dwp1", 98), ("dwp2", 108)])
ROUNDS = ["j2", "j4", "j7", "tho1", "sb1", "dwo2", "tv2", "ln1b", "dwp1"]


def plan():
    ends = [sum(a + b for a, b in PIECES[:p + 1]) for p in range(NS)]
    begun, t, todo = 0, 1, {}
    for name, ready in POINTS:
        ops = todo[name] = []
        for again in range(1 + ROUNDS.count(name)):
            if again:
                assert begun >= t
                ops.append(("round", t))
                t += 1
            while begun < NS and ends[begun] <= ready and (begun <= t or begun < 3):
                ops.append(("begin", begun))
                begun += 1
    rest = []
    while t < NS + 5:
        rest.append(("round", t))
        t += 1
        while begun < NS and begun <= t:
            rest.append(("begin", begun))
            begun += 1
    todo["rest"] = rest
    return todo


PLAN = plan()


class Piece:
    def __init__(self, p):
        start = sum(a + b for a, b in PIECES[:p]) * TILE
        self.p, self.f, self.r, self.q, self.g = p, p % N1, p % NR, p % NZ, p % NZ1
        self.wf, self.wl = (v * TILE for v in PIECES[p])
        self.first = slice(start, start + self.wf)
        self.last = slice(start + self.wf, start + self.wf + self.wl)
        self.all = slice(start, start + self.wf + self.wl)


def place():
    s = lax.axis_index("seq")
    t = lax.axis_index("tm")
    return s, t, t // 4, (t // 2) % 2, t % 2


def rem(a, n):
    return a % n if isinstance(a, int) else lax.rem(a, n)


def store_tile(parts, tile, value):
    at = tile * TILE
    width = value.shape[1]
    cols = slice(at, at + width) if isinstance(at, int) else pl.ds(pl.multiple_of(at, TILE), width)
    parts[:, :, :, :, cols] = value.reshape(2, 4, 2, 32, width).astype(jnp.bfloat16)


class Exchange:
    def __init__(self, parts, bufs, sems, stage, out_sem, out):
        self.parts, self.out = parts, out
        self.stage, self.out_sem = stage, out_sem
        (self.xa, self.yb, self.ya, self.xb, self.zu, self.zd, self.zuc, self.zdc, self.xc, self.yc) = bufs
        self.ssem, self.rsem = sems
        self.s, self.t, self.z, self.y, self.c = place()
        s, t = self.s, self.t
        self.to_x = {"seq": 1 - s, "tm": t}
        self.to_y = {"seq": s, "tm": t + 2 - 4 * self.y}
        self.to_up = {"seq": s, "tm": t + 4}
        self.to_down = {"seq": s, "tm": t - 4}

    def copy(self, kind, g, src, dst, dev):
        return pltpu.make_async_remote_copy(
            src_ref=src, dst_ref=dst, send_sem=self.ssem.at[kind, g.p],
            recv_sem=self.rsem.at[kind, g.p], device_id=dev, device_id_type=MESH_ID)

    def c_xa(self, g):
        return self.copy(0, g, self.parts.at[1 - self.s, :, :, HALF[0], g.first], self.xa.at[g.f, :, :, :, :g.wf], self.to_x)

    def c_yb(self, g):
        return self.copy(1, g, self.parts.at[:, :, 1 - self.y, HALF[1], g.first], self.yb.at[g.f, :, :, :, :g.wf], self.to_y)

    def c_ya(self, g):
        return self.copy(2, g, self.parts.at[self.s, :, 1 - self.y, HALF[0], g.first], self.ya.at[g.r, :, :, :g.wf], self.to_y)

    def c_xb(self, g):
        return self.copy(3, g, self.parts.at[1 - self.s, :, self.y, HALF[1], g.first], self.xb.at[g.r, :, :, :g.wf], self.to_x)

    def c_xc(self, g):
        return self.copy(4, g, self.parts.at[1 - self.s, self.z, :, :, g.last], self.xc.at[g.r, :, :, :g.wl], self.to_x)

    def c_yc(self, g):
        return self.copy(5, g, self.parts.at[self.s, self.z, 1 - self.y, :, g.last], self.yc.at[g.r, :, :g.wl], self.to_y)

    def c_up(self, g, z):
        return self.copy(6, g, self.parts.at[self.s, z + 1:4, self.y, :, g.first], self.zu.at[g.q, z:3, :, :g.wf], self.to_up)

    def c_down(self, g, z):
        return self.copy(7, g, self.parts.at[self.s, 0:z, self.y, :, g.first], self.zd.at[g.q, 0:z, :, :g.wf], self.to_down)

    def c_upc(self, g, z):
        return self.copy(8, g, self.parts.at[:, z + 1:4, :, :, g.last], self.zuc.at[g.g, :, z:3, :, :, :g.wl], self.to_up)

    def c_downc(self, g, z):
        return self.copy(9, g, self.parts.at[:, 0:z, :, :, g.last], self.zdc.at[g.g, :, 0:z, :, :, :g.wl], self.to_down)

    def add(self, at, cols, value):
        self.parts[(*at, cols)] = self.parts[(*at, cols)] + value

    def z_step(self, g, k, is_c):
        if is_c and not g.wl:
            return
        up, down = (self.c_upc, self.c_downc) if is_c else (self.c_up, self.c_down)
        rows = slice(None)

        def add(u, src, at):
            if is_c:
                def body(i, _):
                    a, b = i // 2, i % 2
                    self.add((a, u, b, rows), g.last, src[g.g, a, at, b, :, :g.wl])
                    return 0
                lax.fori_loop(0, 4, body, 0)
            else:
                self.add((self.s, u, self.y, rows), g.first, src[g.q, at, :, :g.wf])

        @pl.when(self.z == k - 1)
        def _():
            z = k - 1
            if z > 0:
                up(g, z - 1).wait_recv()
                for u in range(z + 1, 4):
                    add(u, self.zuc if is_c else self.zu, u - 1)
            if z < 3:
                up(g, z).start()

        @pl.when(self.z == 4 - k)
        def _():
            z = 4 - k
            if z < 3:
                down(g, z + 1).wait_recv()
                for u in range(0, z):
                    add(u, self.zdc if is_c else self.zd, u)
            if z > 0:
                down(g, z).start()

    def step1(self, g):
        self.c_xa(g).start()
        self.c_yb(g).start()
        self.z_step(g, 1, True)

    def step2(self, g):
        self.c_xa(g).wait_recv()

        def body(i, _):
            a, b = i // 2, i % 2
            self.add((self.s, a, b, HALF[0]), g.first, self.xa[g.f, a, b, :, :g.wf])
            return 0
        lax.fori_loop(0, 8, body, 0)
        self.c_ya(g).start()
        self.c_yb(g).wait_recv()

        def body(i, _):
            a, b = i // 4, i % 4
            self.add((a, b, self.y, HALF[1]), g.first, self.yb[g.f, a, b, :, :g.wf])
            return 0
        lax.fori_loop(0, 8, body, 0)
        self.c_xb(g).start()
        self.z_step(g, 2, True)

    def step3(self, g):
        self.c_ya(g).wait_recv()
        self.c_xb(g).wait_recv()

        def body(b, _):
            self.add((self.s, b, self.y, HALF[0]), g.first, self.ya[g.r, b, :, :g.wf])
            self.add((self.s, b, self.y, HALF[1]), g.first, self.xb[g.r, b, :, :g.wf])
            return 0
        lax.fori_loop(0, 4, body, 0)
        self.z_step(g, 1, False)
        self.z_step(g, 3, True)

    def step4(self, g):
        self.z_step(g, 2, False)
        if not g.wl:
            return
        self.z_step(g, 4, True)
        z = self.z
        rows = slice(None)

        @pl.when(z > 0)
        def _():
            def body(i, _):
                a, b = i // 2, i % 2
                self.add((a, z, b, rows), g.last, self.zuc[g.g, a, z - 1, b, :, :g.wl])
                return 0
            lax.fori_loop(0, 4, body, 0)

        @pl.when(z < 3)
        def _():
            def body(i, _):
                a, b = i // 2, i % 2
                self.add((a, z, b, rows), g.last, self.zdc[g.g, a, z, b, :, :g.wl])
                return 0
            lax.fori_loop(0, 4, body, 0)
        self.c_xc(g).start()

    def step5(self, g):
        self.z_step(g, 3, False)
        if not g.wl:
            return
        self.c_xc(g).wait_recv()
        for b in range(2):
            self.add((self.s, self.z, b, slice(None)), g.last, self.xc[g.r, b, :, :g.wl])
        self.c_yc(g).start()

    def step6(self, g):
        self.z_step(g, 4, False)
        z = self.z
        k = g.p % 2
        if g.p >= 2:
            self.c_out(Piece(g.p - 2)).wait()
        mine = self.parts[self.s, z, self.y, :, g.first].astype(jnp.float32)

        @pl.when(z == 0)
        def _():
            self.stage[k, :, :g.wf] = mine + self.zd[g.q, 0, :, :g.wf].astype(jnp.float32)

        @pl.when(z == 3)
        def _():
            self.stage[k, :, :g.wf] = mine + self.zu[g.q, 2, :, :g.wf].astype(jnp.float32)

        @pl.when((z > 0) & (z < 3))
        def _():
            self.stage[k, :, :g.wf] = ((mine + self.zu[g.q, z - 1, :, :g.wf].astype(jnp.float32))
                                       + self.zd[g.q, z, :, :g.wf].astype(jnp.float32))
        if g.wl:
            self.c_yc(g).wait_recv()
            self.stage[k, :, g.wf:g.wf + g.wl] = (self.parts[self.s, z, self.y, :, g.last].astype(jnp.float32)
                                                  + self.yc[g.r, :, :g.wl].astype(jnp.float32))
        self.c_out(g).start()

    def c_out(self, g):
        k = g.p % 2
        return pltpu.make_async_copy(self.stage.at[k, :, :g.wf + g.wl], self.out.at[:, g.all], self.out_sem.at[k])

    def tick(self, t):
        steps = (self.step2, self.step3, self.step4, self.step5, self.step6)
        for k, step in enumerate(steps):
            if 0 <= t - 1 - k < NS:
                step(Piece(t - 1 - k))

    def serve(self, point):
        for what, n in PLAN[point]:
            self.tick(n) if what == "round" else self.step1(Piece(n))

    def finish(self):
        self.c_out(Piece(NS - 2)).wait()
        self.c_out(Piece(NS - 1)).wait()
        for p in range(NS):
            g = Piece(p)
            self.c_xa(g).wait_send()
            self.c_yb(g).wait_send()
            self.c_ya(g).wait_send()
            self.c_xb(g).wait_send()
            if g.wl:
                self.c_xc(g).wait_send()
                self.c_yc(g).wait_send()
        for z in range(4):
            @pl.when(self.z == z)
            def _(z=z):
                for p in range(NS):
                    g = Piece(p)
                    if z < 3:
                        self.c_up(g, z).wait_send()
                        if g.wl:
                            self.c_upc(g, z).wait_send()
                    if z > 0:
                        self.c_down(g, z).wait_send()
                        if g.wl:
                            self.c_downc(g, z).wait_send()


P_SCRATCH = [pltpu.VMEM((2, 4, 2, 32, FLAT), jnp.bfloat16)]
RECV_SCRATCH = [
    pltpu.VMEM((N1, 4, 2, 16, MOST_FIRST), jnp.bfloat16),
    pltpu.VMEM((N1, 2, 4, 16, MOST_FIRST), jnp.bfloat16),
    pltpu.VMEM((NR, 4, 16, MOST_FIRST), jnp.bfloat16),
    pltpu.VMEM((NR, 4, 16, MOST_FIRST), jnp.bfloat16),
    pltpu.VMEM((NZ, 3, 32, MOST_FIRST), jnp.bfloat16),
    pltpu.VMEM((NZ, 3, 32, MOST_FIRST), jnp.bfloat16),
    pltpu.VMEM((NZ1, 2, 3, 2, 32, MOST_LAST), jnp.bfloat16),
    pltpu.VMEM((NZ1, 2, 3, 2, 32, MOST_LAST), jnp.bfloat16),
    pltpu.VMEM((NR, 2, 32, MOST_LAST), jnp.bfloat16),
    pltpu.VMEM((NR, 32, MOST_LAST), jnp.bfloat16),
]

def greet():
    s, t, z, y, c = place()
    bar = pltpu.get_barrier_semaphore()

    def tell(dev):
        pl.semaphore_signal(bar, inc=1, device_id=dev, device_id_type=MESH_ID)
    tell({"seq": 1 - s, "tm": t})
    tell({"seq": s, "tm": t + 2 - 4 * y})
    tell({"seq": s, "tm": t + 1 - 2 * c})

    @pl.when(z < 3)
    def _():
        tell({"seq": s, "tm": t + 4})

    @pl.when(z > 0)
    def _():
        tell({"seq": s, "tm": t - 4})
    far = jnp.where(c == 1, t + 1, t - 1)
    has_far = (far >= 0) & (far < 16)

    @pl.when(has_far)
    def _():
        tell({"seq": s, "tm": far})
    return bar, 3 + jnp.where(has_far, 1, 0) + jnp.where(z < 3, 1, 0) + jnp.where(z > 0, 1, 0)


D = 1024
FF = 4096
SEG = 256
HD = H * DH
HH = HD // 2
WIDE = H * E * DH
FFB = 512
NFF = FF // FFB
NG = 4
LOGIT = 64
OWN_SIB = 24
F32 = jnp.float32
BF = jnp.bfloat16


def dot(a, b):
    return jnp.dot(a, b, preferred_element_type=F32)


def dot_nt(a, b):
    return lax.dot_general(a, b, (((1,), (1,)), ((), ())), preferred_element_type=F32)


def dot_tn(a, b):
    return lax.dot_general(a, b, (((0,), (0,)), ((), ())), preferred_element_type=F32)


def halves(v):
    top = v.astype(BF)
    return top, (v - top.astype(F32)).astype(BF)


def unit_rows(v):
    centre = v - jnp.mean(v, axis=-1, keepdims=True)
    spread = jnp.mean(centre * centre, axis=-1, keepdims=True)
    inv = lax.rsqrt(spread + epsilon)
    return centre * inv, inv


def norm_back(unit, inv, cot):
    return inv * (cot - jnp.mean(cot, axis=-1, keepdims=True)
                  - unit * jnp.mean(cot * unit, axis=-1, keepdims=True))


def normal_cdf(v, bell):
    u = 1.0 / (1.0 + 0.23164189 * jnp.abs(v))
    poly = ((((0.5307027145 * u - 0.7265760135) * u + 0.7107068705) * u - 0.142248368) * u + 0.127414796) * u
    tail = poly * bell
    return jnp.where(v < 0.0, tail, 1.0 - tail)


def for_rows(step, body):
    def inner(i, _):
        body(pl.ds(pl.multiple_of(i * step, step), step))
        return 0
    lax.fori_loop(0, SEG // step, inner, 0)


def side_by_side(blocks):
    return jnp.concatenate(blocks, axis=1)


NAMES = (
    "x", "oc", "gains", "rt", "rf", "spread", "hot", "wq", "wk", "wr", "wrp", "wu", "wd", "exv", "exo",
    "xn", "hn", "mid", "lo", "nsc", "q", "k", "v", "sig", "att", "acc", "g_o", "g_p",
    "act", "uc", "bc", "kc", "vc", "kn", "vn", "ob", "gg", "ogc", "qc", "vg", "ac", "acc2", "up",
    "at", "full",
    "ld", "ld2", "lde", "kv_s", "kv_r", "sib_s", "sib_r", "st", "stage", "out_sem", "ssem", "rsem",
)


def layer_scratch():
    dma = pltpu.SemaphoreType.DMA
    v = pltpu.VMEM
    return [
        v((SEG, D), BF), v((SEG, D), BF), v((2, D), BF), v((2 * H, 2, SEG), jnp.int32), v((128, SEG), BF),
        v((128, 256), BF), v((SEG, 128), F32),
        v((HD, D), BF), v((HD, D), BF), v((2 * H * E, D), BF), v((128, D), BF),
        v((2, D, FFB), BF), v((2, FFB, D), BF), v((2, E, 256, HH), BF), v((2, E, 256, HH), BF),
        v((SEG, D), BF), v((SEG, D), BF), v((SEG, D), F32), v((SEG, D), F32), v((SEG, D), F32),
        v((2, SEG, HH), BF), v((2, 2 * SEG, HH), BF), v((2, 2 * SEG, HH), BF), v((SEG, 128), F32),
        v((2, SEG, HH), BF), v((2, 2 * SEG, HH), F32), v((2 * SEG, 2304), BF), v((2 * SEG, 3328), BF),
        v((NG, 2 * SEG, FFB), BF), v((NG, 2 * SEG, FFB), BF), v((SEG, D), BF),
        v((2, 2 * SEG, HH), BF), v((2, 2 * SEG, HH), BF), v((2, SEG, HH), BF), v((2, SEG, HH), BF), v((SEG, D), BF), v((SEG, 256), BF),
        v((SEG, 128), F32), v((2, SEG, HH), F32), v((2, SEG, 128), F32),
        v((2, SEG, HH), BF), v((2, 2 * SEG, HH), F32), v((SEG, FFB), F32),
        v((6, 16, 32, 2 * SEG), BF), v((2, 16, 2, 32, SEG), BF),
        dma((16,)), dma((4,)), dma((2, 2 * E)), dma((5,)), dma((5,)), dma((OWN_SIB,)), dma((OWN_SIB,)), dma((2,)),
        v((2, 32, MOST), F32), dma((2,)), dma((10, NS)), dma((10, NS)),
    ]


def layer_kernel(x_h, rt_h, len_s, gains_h, wq_h, wk_h, wv_h, wr_h, wo_h, wu_h, wd_h, oc_h,
                 spread_h, lo_h, ig_h, flat_h, *scratch):
    m = types.SimpleNamespace(**dict(zip(NAMES, scratch[:len(NAMES)])))
    recv = scratch[len(NAMES):]
    s, t, z, y, c = place()
    last_t = lax.axis_size("tm") - 1
    sib = {"seq": s, "tm": t + 1 - 2 * c}
    scale = DH ** -0.5
    own = slice(SEG, 2 * SEG)
    mem = slice(0, SEG)

    bar, peers = greet()

    def load(i, src, dst):
        cp = pltpu.make_async_copy(src, dst, m.ld.at[i])
        cp.start()
        return cp

    def sibling(i, src, dst):
        return pltpu.make_async_remote_copy(
            src_ref=src, dst_ref=dst, send_sem=m.sib_s.at[i], recv_sem=m.sib_r.at[i],
            device_id=sib, device_id_type=MESH_ID)

    def at_copy(i, slot):
        return sibling(i, m.full.at[slot, :, 1 - c], m.at.at[i, :, :, SEG:])

    def turn(i, slot, value):
        m.full[slot] = jnp.transpose(value).reshape(16, 2, 32, SEG)
        m.at[i, :, :, :SEG] = m.full[slot, :, c]
        at_copy(i, slot).start()

    def go_copy():
        return sibling(6, m.g_o.at[mem], m.g_o.at[own])

    def gp_copy():
        return sibling(7, m.g_p.at[mem], m.g_p.at[own])

    def ff_copies(j):
        return act_copy(j), uc_copy(j)

    def act_copy(j):
        g = rem(j, NG)
        return sibling(8 + 2 * j, m.act.at[g, mem], m.act.at[g, own])

    def uc_copy(j):
        g = rem(j, NG)
        return sibling(9 + 2 * j, m.uc.at[g, mem], m.uc.at[g, own])

    def ff_loads(j):
        return wu_load(j), wd_load(j)

    def wu_load(j):
        cols = pl.ds(pl.multiple_of(j * FFB, FFB), FFB)
        return pltpu.make_async_copy(wu_h.at[:, cols], m.wu.at[rem(j, 2)], m.ld2.at[rem(j, 2)])

    def wd_load(j):
        rows = pl.ds(pl.multiple_of(j * FFB, FFB), FFB)
        return pltpu.make_async_copy(wd_h.at[rows, :], m.wd.at[rem(j, 2)], m.ld2.at[2 + rem(j, 2)])

    def along(i, src, dst, by):
        return pltpu.make_async_remote_copy(
            src_ref=src, dst_ref=dst, send_sem=m.kv_s.at[i], recv_sem=m.kv_r.at[i],
            device_id={"seq": s, "tm": t + by}, device_id_type=MESH_ID)

    def k_copy():
        return along(0, m.k.at[:, own], m.k.at[:, mem], 1)

    def v_copy(half):
        return along(1 + half, m.v.at[half, own], m.v.at[half, mem], 1)

    def kc_copy():
        return along(3, m.kc.at[:, mem], m.kn, -1)

    def vc_copy():
        return along(4, m.vc.at[:, mem], m.vn, -1)

    def half_rows(half):
        return slice(half * HH, (half + 1) * HH)

    def head_only(v, h):
        lane = lax.broadcasted_iota(jnp.int32, v.shape, 1)
        lo = rem(h, 2) * DH
        return jnp.where((lane >= lo) & (lane < lo + DH), v, jnp.zeros_like(v))

    def gates_wide(table, half, e):
        return dot(m.gg[...], table[half, e])

    def make_table(table, first):
        row = lax.broadcasted_iota(jnp.int32, (256, HH), 0)
        lane = lax.broadcasted_iota(jnp.int32, (256, HH), 1)
        row = jnp.where(row >= 128, row - 128, row) - first - jnp.where(lane >= DH, E, 0)
        for half in range(2):
            for e in range(E):
                table[half, e] = jnp.where(row == 2 * E * half + e, 1.0, 0.0).astype(BF)

    def expert_loads(which, n, e, src, dst):
        return [pltpu.make_async_copy(src.at[pl.ds((h * E + e) * DH, DH)], dst.at[pl.ds(h * DH, DH)], m.lde.at[which, n])
                for h in range(H)]

    def ring(n):
        return expert_loads(0, n, n % E, wo_h if n < E else wv_h, m.wd.at[n % 2])

    def weights_of(h):
        half = h // 2
        scores = dot_nt(head_only(m.q[half], h), m.k[half]) * scale
        length = len_s[0, 0]
        row = lax.broadcasted_iota(jnp.int32, (SEG, 2 * SEG), 0)
        col = lax.broadcasted_iota(jnp.int32, (SEG, 2 * SEG), 1)
        allowed = ((col < SEG) & (col >= SEG - length)) | ((col >= SEG) & (col - SEG <= row))
        scores = jnp.where(allowed, scores, -1e30)
        e = jnp.exp(scores - jnp.max(scores, axis=-1, keepdims=True))
        return e / jnp.sum(e, axis=-1, keepdims=True)

    l_x = load(0, x_h, m.x)
    l_g = load(1, gains_h, m.gains)
    l_k = load(2, wk_h, m.wk)
    l_r = load(3, wr_h, m.wr)
    l_rt = load(4, rt_h, m.rt)
    l_sp = load(12, spread_h, m.spread)

    def forward(wv, wo, wide):
        l_v = [expert_loads(0, e, e, wv_h, wv.at[e]) for e in range(E)]
        for group in l_v:
            for cp in group:
                cp.start()
        make_table(m.exv, LOGIT)
        l_x.wait()
        l_g.wait()

        def norm1(rows):
            unit, _ = unit_rows(m.x[rows, :].astype(F32))
            m.xn[rows, :] = (unit * m.gains[0:1, :].astype(F32)).astype(BF)
        for_rows(32, norm1)
        l_k.wait()
        for half in range(2):
            m.k[half, own] = dot_nt(m.xn[...], m.wk[half_rows(half), :]).astype(BF)
        l_q = load(8, wq_h, m.wq)
        l_oc = load(9, oc_h, m.oc)
        l_wo = [expert_loads(1, e, e, wo_h, wo.at[pl.ds(e * HD, HD)]) for e in range(E)]
        for group in l_wo:
            for cp in group:
                cp.start()
        for j in range(2):
            for cp in ff_loads(j):
                cp.start()
        pl.semaphore_wait(bar, peers)

        @pl.when(t < last_t)
        def _():
            k_copy().start()
        l_r.wait()
        m.wrp[...] = jnp.zeros((128, D), BF)
        m.wrp[LOGIT:LOGIT + 2 * H * E, :] = m.wr[...]
        sig = jax.nn.sigmoid(dot_nt(m.xn[...], m.wrp[...]))
        l_rt.wait()
        l_sp.wait()
        m.rf[...] = jnp.zeros((128, SEG), BF)
        for i in range(2):
            m.rf[16 * i:16 * i + 2 * H, :] = m.rt[:, i, :].astype(F32).astype(BF)
        named = dot_tn(m.rf[...], m.spread[...])
        expert = m.spread[127:128, :128].astype(F32)
        hit = (named[:, :128] == expert) | (named[:, 128:] == expert)
        m.hot[...] = jnp.where(hit, 1.0, 0.0)
        m.sig[...] = sig
        top, low = halves(sig * m.hot[...])
        m.gg[:, :128] = top
        m.gg[:, 128:] = low
        for half in range(2):
            total = jnp.zeros((SEG, HH), F32)
            for e in range(E):
                if half == 0:
                    for cp in l_v[e]:
                        cp.wait()
                total = total + dot_nt(m.xn[...], wv[e, half_rows(half)]) * gates_wide(m.exv, half, e)
            m.v[half, own] = total.astype(BF)

            @pl.when(t < last_t)
            def _():
                v_copy(half).start()
        l_q.wait()
        for half in range(2):
            m.q[half] = dot_nt(m.xn[...], m.wq[half_rows(half), :]).astype(BF)
        l_oc.wait()
        turn(0, 0, m.oc[...])
        turn(3, 1, m.xn[...])
        make_table(m.exo, LOGIT + H * E)

        @pl.when(t > 0)
        def _():
            k_copy().wait_recv()

        @pl.when(t == 0)
        def _():
            m.k[:, mem] = jnp.zeros((2, SEG, HH), BF)
            m.v[:, mem] = jnp.zeros((2, SEG, HH), BF)
        for h in range(H):
            m.act[h, mem] = weights_of(h).astype(BF)
        for half in range(2):
            for e in range(E):
                wide[half, e] = gates_wide(m.exo, half, e)
        for cp in ff_loads(0):
            cp.wait()
        m.up[...] = dot_nt(m.oc[...], m.wd[0])
        m.g_o[mem, 2176:2304] = jnp.zeros((SEG, 128), BF)
        for half in range(2):
            @pl.when(t > 0)
            def _():
                v_copy(half).wait_recv()
            total = jnp.zeros((SEG, HH), F32)
            for h in (2 * half, 2 * half + 1):
                total = total + dot(m.act[h, mem], head_only(m.v[half], h))
            m.att[half] = total.astype(BF)
        att = [m.att[half].astype(F32) for half in range(2)]
        for e in range(0, E, 2):
            blocks = [(wide[half, i] * att[half]).astype(BF) for i in range(e, min(e + 2, E)) for half in range(2)]
            m.g_o[mem, e * HD:min(e + 2, E) * HD] = side_by_side(blocks)
        go_copy().start()
        for group in l_wo:
            for cp in group:
                cp.wait()
        m.mid[...] = m.x[...].astype(F32) + dot(m.g_o[mem, :WIDE], wo[...])

        def norm2(rows):
            unit, _ = unit_rows(m.mid[rows, :])
            m.hn[rows, :] = (unit * m.gains[1:2, :].astype(F32)).astype(BF)
        for_rows(32, norm2)
        at_copy(0, 0).wait_send()
        turn(1, 0, m.hn[...])

    pl.run_scoped(forward, pltpu.VMEM((E, HD, D), BF), pltpu.VMEM((WIDE, D), BF), pltpu.VMEM((2, E, SEG, HH), F32))

    def backward(parts):
        ex = Exchange(parts, recv, (m.ssem, m.rsem), m.stage, m.out_sem, flat_h)

        def product(i, g):
            return dot(m.at[i].reshape(512, 2 * SEG), g)

        def tiles(i, g, tile):
            store_tile(parts, tile, product(i, g))

        m.lo[...] = m.mid[...]
        m.nsc[...] = jnp.zeros((SEG, D), F32)
        at_copy(0, 0).wait_recv()
        at_copy(1, 0).wait_recv()

        def block(j, _):
            b = rem(j, 2)
            g = rem(j, NG)

            @pl.when(j > 0)
            def _():
                wu_load(j).wait()

            @pl.when(j >= NG)
            def _():
                for cp in ff_copies(j - NG):
                    cp.wait_send()
            pre = dot(m.hn[...], m.wu[b])
            bell = jnp.exp(-0.5 * pre * pre)
            cdf = normal_cdf(pre, bell)
            m.act[g, mem] = (pre * cdf).astype(BF)
            act_copy(j).start()
            pdf = bell * 0.3989422804014327
            m.uc[g, mem] = (m.up[...] * (cdf + pre * pdf)).astype(BF)
            uc_copy(j).start()

            @pl.when(j > 2)
            def _():
                act_grad(j - 1)
                up_grad(j - 1)
            m.lo[...] += dot(m.act[g, mem], m.wd[b])
            m.nsc[...] += dot_nt(m.uc[g, mem], m.wu[b])

            @pl.when(j + 2 < NFF)
            def _():
                for cp in ff_loads(j + 2):
                    cp.start()

            @pl.when(j == 0)
            def _():
                act_grad(0)
                ex.serve("d0")
                up_grad(0)
                ex.serve("u0")

            @pl.when(j + 1 < NFF)
            def _():
                wd_load(j + 1).wait()
                m.up[...] = dot_nt(m.oc[...], m.wd[rem(j + 1, 2)])

            @pl.when(j == 1)
            def _():
                act_grad(1)
                up_grad(1)
            for i in range(1, NFF):
                if PLAN[f"j{i}"]:
                    pl.when(j == i)(lambda i=i: ex.serve(f"j{i}"))
            return 0

        def act_grad(j):
            act_copy(j).wait_recv()
            tiles(0, m.act[rem(j, NG)], 8 * j)

        def up_grad(j):
            uc_copy(j).wait_recv()
            tiles(1, m.uc[rem(j, NG)], 8 * j + 4)
        lax.fori_loop(0, NFF, block, 0)
        for n in range(2):
            for cp in ring(n):
                cp.start()
        act_grad(NFF - 1)
        up_grad(NFF - 1)
        ex.serve("dw7")
        for j in range(NFF - NG, NFF):
            for cp in ff_copies(j):
                cp.wait_send()
        m.ob[...] = m.lo[...].astype(BF)
        l_lo = pltpu.make_async_copy(m.ob, lo_h, m.st.at[0])
        l_lo.start()

        def norm2_back(rows):
            unit, inv = unit_rows(m.mid[rows, :])
            cot = m.nsc[rows, :]
            mcot = m.oc[rows, :].astype(F32) + norm_back(unit, inv, cot * m.gains[1:2, :].astype(F32))
            m.lo[rows, :] = mcot
            m.bc[rows, :] = mcot.astype(BF)
            m.hn[rows, :] = (cot * unit).astype(BF)
        for_rows(32, norm2_back)
        at_copy(3, 1).wait_send()
        turn(2, 1, m.bc[...])
        at_copy(1, 0).wait_send()
        turn(5, 0, m.hn[...])
        ex.serve("ln2b")

        def ring_next(n):
            if n + 2 < 2 * E:
                for cp in ring(n + 2):
                    cp.start()

        att = [m.att[half].astype(F32) for half in range(2)]
        seen = jnp.zeros((SEG, 128), F32)
        total = [jnp.zeros((SEG, HH), F32)] * 2
        for e in range(E):
            for cp in ring(e):
                cp.wait()
            cots = [dot_nt(m.bc[...], m.wd[e % 2, half_rows(half)]) for half in range(2)]
            ring_next(e)
            for half, cot in enumerate(cots):
                seen = seen + dot_nt((cot * att[half]).astype(BF), m.exo[half, e, :128])
                total[half] = total[half] + cot * gates_wide(m.exo, half, e)
            ex.serve(f"tho{e}")
        m.ogc[...] = seen
        for half in range(2):
            m.ac[half] = total[half].astype(BF)

        m.acc[...] = jnp.zeros((2, 2 * SEG, HH), F32)
        m.acc2[...] = jnp.zeros((2, 2 * SEG, HH), F32)
        m.qc[...] = jnp.zeros((2, SEG, HH), F32)

        def scores_back(h):
            half = h // 2
            probs = weights_of(h)
            cot = head_only(m.ac[half], h)
            m.acc2[half] += dot_tn(probs.astype(BF), cot)
            pc = dot_nt(cot, m.v[half])
            sc = (probs * (pc - jnp.sum(probs * pc, axis=-1, keepdims=True))).astype(BF)
            m.qc[half] += dot(sc, head_only(m.k[half], h)) * scale
            m.acc[half] += dot_tn(sc, head_only(m.q[half], h)) * scale
        for i in range(2):
            scores_back(2 * i)
            scores_back(2 * i + 1)
            ex.serve(f"sb{i}")
        m.vc[...] = m.acc2[...].astype(BF)
        m.kc[...] = m.acc[...].astype(BF)

        @pl.when(t > 0)
        def _():
            vc_copy().start()
            kc_copy().start()
        go_copy().wait_recv()
        at_copy(2, 1).wait_recv()

        for i in range(3):
            tiles(2, m.g_o[:, 6 * TILE * i:6 * TILE * (i + 1)], 64 + 6 * i)
            ex.serve(f"dwo{i}")
        m.g_p[mem, HD:512] = jnp.zeros((SEG, 512 - HD), BF)
        m.g_p[mem, 512 + HD:1024] = jnp.zeros((SEG, 512 - HD), BF)
        m.g_p[mem, :HD] = side_by_side([m.qc[half].astype(BF) for half in range(2)])

        @pl.when(t < last_t)
        def _():
            vc_copy().wait_recv()
            kc_copy().wait_recv()

        @pl.when(t == last_t)
        def _():
            m.kn[...] = jnp.zeros((2, SEG, HH), BF)
            m.vn[...] = jnp.zeros((2, SEG, HH), BF)
        m.g_p[mem, 512:512 + HD] = side_by_side(
            [(m.kc[half, own].astype(F32) + m.kn[half].astype(F32)).astype(BF) for half in range(2)])
        l_lo.wait()

        own_cot, next_cot = m.mid, m.nsc

        own_cot[...] = (dot(m.g_p[mem, :HD], m.wq[...])
                        + sum(dot(m.kc[half, own], m.wk[half_rows(half), :]) for half in range(2)))
        next_cot[...] = sum(dot(m.kn[half], m.wk[half_rows(half), :]) for half in range(2))
        m.vg[...] = jnp.zeros((2, SEG, 128), F32)
        blocks = []
        for e in range(E):
            for cp in ring(E + e):
                cp.wait()
            wv = m.wd.at[(E + e) % 2]
            pairs = []
            for half in range(2):
                proj = dot_nt(m.xn[...], wv[half_rows(half)])
                gate = gates_wide(m.exv, half, e)
                pair = []
                for i, v in enumerate((m.vc[half, own], m.vn[half])):
                    v = v.astype(F32)
                    m.vg[i] += dot_nt((v * proj).astype(BF), m.exv[half, e, :128])
                    pair.append((gate * v).astype(BF))
                blocks.append((pair[0].astype(F32) + pair[1].astype(F32)).astype(BF))
                pairs.append(pair)
            for i, acc in enumerate((own_cot, next_cot)):
                acc[...] += dot(side_by_side([pair[i] for pair in pairs]), wv[:HD])
            ring_next(E + e)
            ex.serve(f"tv{e}")
            if e % 2 == 1 or e == E - 1:
                first = e - 1 if e % 2 == 1 else e
                m.g_p[mem, 1024 + first * HD:1024 + (e + 1) * HD] = side_by_side(blocks[2 * first:])
        slope = m.sig[...] * (1.0 - m.sig[...]) * m.hot[...]
        lo_cot = ((m.vg[0] + m.ogc[...]) * slope).astype(BF)
        ln_cot = (m.vg[1] * slope).astype(BF)
        own_cot[...] += dot(lo_cot, m.wrp[...])
        next_cot[...] += dot(ln_cot, m.wrp[...])
        both = (lo_cot.astype(F32) + ln_cot.astype(F32)).astype(BF)
        lane = lax.broadcasted_iota(jnp.int32, (SEG, 128), 1)
        m.g_p[mem, 3200:3328] = jnp.where(lane < LOGIT, m.g_p[mem, 3200:3328], both)
        gp_copy().start()

        def norm1_back(rows):
            unit, inv = unit_rows(m.x[rows, :].astype(F32))
            cot = own_cot[rows, :]
            m.lo[rows, :] += norm_back(unit, inv, cot * m.gains[0:1, :].astype(F32))
            m.hn[rows, :] = ((cot + next_cot[rows, :]) * unit).astype(BF)
        for_rows(32, norm1_back)
        l_ig = pltpu.make_async_copy(m.lo, ig_h, m.st.at[1])
        l_ig.start()
        at_copy(2, 1).wait_send()
        turn(4, 1, m.hn[...])
        ex.serve("ln1b")
        gp_copy().wait_recv()
        at_copy(3, 1).wait_recv()

        for i in range(6):
            tiles(3, m.g_p[:, 4 * TILE * i:4 * TILE * (i + 1)], 82 + 4 * i)
            if i in (1, 3):
                ex.serve(f"dwp{i // 2}")
        last = product(3, m.g_p[:, 3072:3328])
        store_tile(parts, 106, last[:, :TILE])
        last = last[:, TILE:]
        lane = lax.broadcasted_iota(jnp.int32, (2 * SEG, TILE), 1)
        at_copy(5, 0).wait_recv()
        at_copy(4, 1).wait_recv()
        for i, at in ((4, 104), (5, 105)):
            last += product(i, jnp.where(lane == at, 1.0, 0.0).astype(BF))
        store_tile(parts, 107, last)

        ex.serve("dwp2")
        ex.serve("rest")
        ex.finish()
        l_ig.wait()

    pl.run_scoped(backward, *P_SCRATCH)
    at_copy(5, 0).wait_send()
    at_copy(4, 1).wait_send()
    go_copy().wait_send()
    gp_copy().wait_send()

    @pl.when(t < last_t)
    def _():
        k_copy().wait_send()
        v_copy(0).wait_send()
        v_copy(1).wait_send()

    @pl.when(t > 0)
    def _():
        kc_copy().wait_send()
        vc_copy().wait_send()


def tables():
    lane = np.arange(128) - LOGIT
    inside = (lane >= 0) & (lane < 2 * H * E)
    pick = (np.arange(2 * H)[:, None] == lane[None, :] // E) & inside
    spread = np.zeros((128, 256), np.float32)
    spread[:2 * H, :128] = pick
    spread[16:16 + 2 * H, 128:] = pick
    spread[127, :128] = np.where(inside, lane % E, -1)
    return spread.astype(ml_dtypes.bfloat16)


def fused_device(layer_input, routes, memory_lengths, norm_gains, w_query, w_key, w_value,
                 w_router, w_output, w_up, w_down, output_cot):
    anywhere = pl.BlockSpec(memory_space=pl.ANY)
    specs = [anywhere] * 13
    specs[2] = pl.BlockSpec(memory_space=pltpu.SMEM)
    out, grad, flat = pl.pallas_call(
        layer_kernel,
        out_shape=(jax.ShapeDtypeStruct((SEG, D), BF), jax.ShapeDtypeStruct((SEG, D), F32),
                   jax.ShapeDtypeStruct((32, FLAT), F32)),
        in_specs=specs,
        out_specs=(anywhere,) * 3,
        scratch_shapes=layer_scratch() + RECV_SCRATCH,
        compiler_params=pltpu.CompilerParams(
            collective_id=0, has_side_effects=True, vmem_limit_bytes=VMEM_LIMIT),
        name="layer",
    )(layer_input[0], jnp.transpose(routes[0], (1, 2, 0)), memory_lengths, norm_gains, w_query.T, w_key.T, w_value.T, w_router.T,
      w_output, w_up, w_down, output_cot[0], tables())
    shapes = ((SEG, D), BF), ((SEG, D), F32), ((2, 32), F32), ((32, HD), F32), ((32, HD), F32), \
        ((32, WIDE), F32), ((32, 2 * H * E), F32), ((32, WIDE), F32), ((32, FF), F32), ((32, FF), F32)
    vm = pl.BlockSpec(memory_space=pltpu.VMEM)
    res = pl.pallas_call(
        split_kernel,
        out_shape=tuple(jax.ShapeDtypeStruct(*v) for v in shapes),
        in_specs=(anywhere, anywhere, anywhere),
        out_specs=(vm,) * 10,
        scratch_shapes=[pltpu.VMEM((32, FLAT), F32), pltpu.SemaphoreType.DMA((3,))],
        compiler_params=pltpu.CompilerParams(vmem_limit_bytes=VMEM_LIMIT),
        name="split",
    )(out, grad, flat)
    return (res[0][None], res[1][None], *res[2:7], res[7].T, res[8], res[9].T)


def split_kernel(out_h, grad_h, flat_h, lo, ig, gains, dq, dk, dv, dr, do, du, dd, flat, sem):
    copies = [pltpu.make_async_copy(flat_h, flat, sem.at[2]), pltpu.make_async_copy(out_h, lo, sem.at[0]),
              pltpu.make_async_copy(grad_h, ig, sem.at[1])]
    for cp in copies:
        cp.start()
    copies.pop(0).wait()
    for j in range(NFF):
        dd[:, j * FFB:(j + 1) * FFB] = flat[:, 2 * j * FFB:(2 * j + 1) * FFB]
        du[:, j * FFB:(j + 1) * FFB] = flat[:, (2 * j + 1) * FFB:(2 * j + 2) * FFB]
    base = 82 * TILE
    dq[...] = flat[:, base:base + HD]
    dk[...] = flat[:, base + 512:base + 512 + HD]
    for h in range(H):
        for e in range(E):
            to = slice((h * E + e) * DH, (h * E + e + 1) * DH)
            at = e * HD + h * DH
            do[:, to] = flat[:, 2 * FF + at:2 * FF + at + DH]
            dv[:, to] = flat[:, base + 1024 + at:base + 1024 + at + DH]
    tail = flat[:, 107 * TILE:108 * TILE]
    dr[...] = tail[:, LOGIT:LOGIT + 2 * H * E]
    gains[...] = jnp.transpose(tail)[104:106, :]
    for cp in copies:
        cp.wait()


def solution(mesh):
    placed = (
        P("seq", "tm", None),
        P("seq", "tm", None, None),
        P("seq", "tm"),
        P(),
        P(),
        P(),
        P(),
        P(),
        P(),
        P(),
        P(),
        P("seq", "tm", None),
    )
    fused = mesh.shape["seq"] == 2 and mesh.shape["tm"] == 16
    return jax.shard_map(
        fused_device if fused else per_device,
        mesh=mesh,
        in_specs=placed,
        out_specs=(
            P("seq", "tm", None),
            P("seq", "tm", None),
            P(None, ("seq", "tm")),
            P(("seq", "tm"), None),
            P(("seq", "tm"), None),
            P(("seq", "tm"), None),
            P(("seq", "tm"), None),
            P(None, ("seq", "tm")),
            P(("seq", "tm"), None),
            P(None, ("seq", "tm")),
        ),
        check_vma=False,
    )
```

```python
import types

import jax
import jax.numpy as jnp
import ml_dtypes
import numpy as np
from jax import lax
from jax.experimental import pallas as pl
from jax.experimental.pallas import tpu as pltpu
from jax.sharding import PartitionSpec as P

H = 4
DH = 112
E = 5


epsilon = 1e-05


def passed_along(value, axis, steps):
    count = lax.axis_size(axis)
    initial, last = (max(0, -steps), min(count, count - steps))
    return lax.ppermute(value, axis, [(source, source + steps) for source in range(initial, last)])


def normalize(values, gain_vec):
    centre = values - jnp.mean(values, axis=-1, keepdims=True)
    spread = jnp.mean(centre * centre, axis=-1, keepdims=True)
    return centre * lax.rsqrt(spread + epsilon) * gain_vec


def exact_gelu(arg_in):
    return jax.nn.gelu(arg_in, approximate=False)


def matmul(left_op, right_op):
    return jnp.dot(left_op, right_op, preferred_element_type=jnp.float32)


def times_tr(left_op, right_op):
    return lax.dot_general(
        left_op, right_op, (((1,), (1,)), ((), ())), preferred_element_type=jnp.float32
    )


def tr_times(left_op, right_op):
    return lax.dot_general(
        left_op, right_op, (((0,), (0,)), ((), ())), preferred_element_type=jnp.float32
    )


def one_hot_routes(route_ids):
    return jnp.sum(
        (route_ids[..., None] == jnp.arange(E, dtype=jnp.int32)).astype(jnp.float32), axis=-2
    )


def attention_mask(memory_length, seg_len):
    query_pos = jnp.arange(seg_len, dtype=jnp.int32)[:, None]
    key_pos = jnp.arange(2 * seg_len, dtype=jnp.int32)[None, :]
    return jnp.where(
        key_pos < seg_len, key_pos >= seg_len - memory_length, key_pos - seg_len <= query_pos
    )


def per_device(
    layer_input,
    routes,
    memory_lengths,
    norm_gains,
    w_query,
    w_key,
    w_value,
    w_router,
    w_output,
    w_up,
    w_down,
    output_cot,
):
    seg_len = layer_input.shape[1]
    own_rows = layer_input[0].astype(jnp.float32)
    memory_length = memory_lengths[0, 0]
    gains_f = norm_gains.astype(jnp.float32)
    first_gain = gains_f[0]
    second_gain = gains_f[1]
    scale_factor = DH ** (-0.5)
    allowed = attention_mask(memory_length, seg_len)
    onehot = one_hot_routes(routes[0])
    unit_normed = normalize(own_rows, jnp.ones_like(first_gain))
    own_normed = (unit_normed * first_gain).astype(jnp.bfloat16)

    def projections():
        queries = matmul(own_normed, w_query).astype(jnp.bfloat16)
        key_own = matmul(own_normed, w_key).astype(jnp.bfloat16)
        logits = matmul(own_normed, w_router).reshape(seg_len, 2 * H, E)
        gate_sig = jax.nn.sigmoid(logits)
        gate_vals = gate_sig * onehot
        projected = matmul(own_normed, w_value).reshape(seg_len, H, E, DH)
        value_own = (
            jnp.sum(gate_vals[:, :H, :, None] * projected, axis=2)
            .reshape(seg_len, H * DH)
            .astype(jnp.bfloat16)
        )
        return (queries, key_own, gate_sig, gate_vals, projected, value_own)

    queries, key_own, gate_sig, gate_vals, projected, value_own = projections()
    key_mem, value_mem = passed_along((key_own, value_own), "tm", 1)
    key_rows = jnp.concatenate([key_mem, key_own], axis=0)
    value_rows = jnp.concatenate([value_mem, value_own], axis=0)
    head_outs = []
    log_norms = []
    for head_idx in range(H):
        columns = slice(head_idx * DH, (head_idx + 1) * DH)
        scores = (
            jnp.einsum(
                "qd,kd->qk",
                queries[:, columns],
                key_rows[:, columns],
                preferred_element_type=jnp.float32,
            )
            * scale_factor
        )
        scores = jnp.where(allowed, scores, -1e30)
        peak = jnp.max(scores, axis=-1, keepdims=True)
        exp_scores = jnp.exp(scores - peak)
        total = jnp.sum(exp_scores, axis=-1, keepdims=True)
        weights = (exp_scores / total).astype(jnp.bfloat16)
        head_outs.append(matmul(weights, value_rows[:, columns]))
        log_norms.append(peak + jnp.log(total))
    attended = jnp.concatenate(head_outs, axis=1).astype(jnp.bfloat16)
    out_gates = gate_vals[:, H:]
    attended_f = attended.astype(jnp.float32).reshape(seg_len, H, 1, DH)
    mixed_in = (attended_f * out_gates[..., None]).reshape(seg_len, H * E * DH).astype(jnp.bfloat16)
    middle = own_rows + matmul(mixed_in, w_output)
    hidden_normed = normalize(middle, second_gain).astype(jnp.bfloat16)
    pre_act = matmul(hidden_normed, w_up)
    activated = exact_gelu(pre_act).astype(jnp.bfloat16)
    layer_out = middle + matmul(activated, w_down)
    output_block = layer_out.astype(jnp.bfloat16)[None]
    down_cot = output_cot[0]
    out_cot = down_cot.astype(jnp.float32)
    grad_down = tr_times(activated, down_cot)
    grad_act = times_tr(down_cot, w_down)
    unused_gelu, gelu_pull = jax.vjp(exact_gelu, pre_act)
    up_cot = gelu_pull(grad_act)[0].astype(jnp.bfloat16)
    grad_up = tr_times(hidden_normed, up_cot)
    normed_second_cot = times_tr(up_cot, w_up)
    unused_norm, second_pull = jax.vjp(normalize, middle, second_gain)
    middle_part, grad_second = second_pull(normed_second_cot)
    middle_cot = out_cot + middle_part
    branch_cot = middle_cot.astype(jnp.bfloat16)
    grad_output = tr_times(mixed_in, branch_cot)
    mixed_cot = times_tr(branch_cot, w_output).reshape(seg_len, H, E, DH)
    out_gate_cot = jnp.sum(mixed_cot * attended_f, axis=-1)
    attended_cot = (
        jnp.sum(mixed_cot * out_gates[..., None], axis=2)
        .reshape(seg_len, H * DH)
        .astype(jnp.bfloat16)
    )
    queries, key_own, gate_sig, gate_vals, projected, value_own = projections()
    key_back, value_back = passed_along((key_own, value_own), "tm", 1)
    key_rows = jnp.concatenate([key_back, key_own], axis=0)
    value_rows = jnp.concatenate([value_back, value_own], axis=0)
    query_grads = []
    key_grads = []
    value_grads = []
    for head_idx in range(H):
        columns = slice(head_idx * DH, (head_idx + 1) * DH)
        scores = (
            jnp.einsum(
                "qd,kd->qk",
                queries[:, columns],
                key_rows[:, columns],
                preferred_element_type=jnp.float32,
            )
            * scale_factor
        )
        scores = jnp.where(allowed, scores, -1e30)
        probs = jnp.exp(scores - log_norms[head_idx])
        weights = probs.astype(jnp.bfloat16)
        cot_head = attended_cot[:, columns]
        value_grads.append(tr_times(weights, cot_head))
        prob_cot = times_tr(cot_head, value_rows[:, columns])
        score_cot = (probs * (prob_cot - jnp.sum(probs * prob_cot, axis=-1, keepdims=True))).astype(
            jnp.bfloat16
        )
        query_grads.append(matmul(score_cot, key_rows[:, columns]) * scale_factor)
        key_grads.append(tr_times(score_cot, queries[:, columns]) * scale_factor)
    query_cot = jnp.concatenate(query_grads, axis=1).astype(jnp.bfloat16)
    key_cot_all = jnp.concatenate(key_grads, axis=1)
    value_cot_all = jnp.concatenate(value_grads, axis=1)
    key_mem_cot = key_cot_all[:seg_len].astype(jnp.bfloat16)
    key_own_cot = key_cot_all[seg_len:].astype(jnp.bfloat16)
    value_mem_cot = value_cot_all[:seg_len].astype(jnp.bfloat16)
    value_own_cot = value_cot_all[seg_len:].astype(jnp.bfloat16)
    key_next, value_next = passed_along((key_mem_cot, value_mem_cot), "tm", -1)
    own_vcot = value_own_cot.astype(jnp.float32).reshape(seg_len, H, 1, DH)
    next_vcot = value_next.astype(jnp.float32).reshape(seg_len, H, 1, DH)
    val_gates = gate_vals[:, :H, :, None]
    proj_own_cot = (val_gates * own_vcot).reshape(seg_len, H * E * DH).astype(jnp.bfloat16)
    proj_next_cot = (val_gates * next_vcot).reshape(seg_len, H * E * DH).astype(jnp.bfloat16)
    gate_own_cot = jnp.concatenate([jnp.sum(own_vcot * projected, axis=-1), out_gate_cot], axis=1)
    gate_next_cot = jnp.concatenate(
        [jnp.sum(next_vcot * projected, axis=-1), jnp.zeros_like(out_gate_cot)], axis=1
    )
    slope = gate_sig * (1.0 - gate_sig) * onehot
    logit_own_cot = (gate_own_cot * slope).reshape(seg_len, 2 * H * E).astype(jnp.bfloat16)
    logit_next_cot = (gate_next_cot * slope).reshape(seg_len, 2 * H * E).astype(jnp.bfloat16)
    twice_normed = jnp.concatenate([own_normed, own_normed], axis=0)
    key_both = jnp.concatenate([key_own_cot, key_next], axis=0)
    proj_both = jnp.concatenate([proj_own_cot, proj_next_cot], axis=0)
    logit_both = jnp.concatenate([logit_own_cot, logit_next_cot], axis=0)
    grad_query = tr_times(own_normed, query_cot)
    grad_key = tr_times(twice_normed, key_both)
    grad_value = tr_times(twice_normed, proj_both)
    grad_router = tr_times(twice_normed, logit_both)
    normed_both = (
        times_tr(key_both, w_key) + times_tr(proj_both, w_value) + times_tr(logit_both, w_router)
    )
    own_normed_cot = normed_both[:seg_len] + times_tr(query_cot, w_query)
    next_normed_cot = normed_both[seg_len:]
    grad_first = jnp.sum((own_normed_cot + next_normed_cot) * unit_normed, axis=0)
    unused_first, first_pull = jax.vjp(normalize, own_rows, first_gain)
    input_part = first_pull(own_normed_cot)[0]
    input_cot = middle_cot + input_part
    grad_gains = jnp.stack([grad_first, grad_second], axis=0)
    row_query, row_key, row_value, row_router, row_up = (
        lax.psum_scatter(grad_query, ("seq", "tm"), scatter_dimension=0, tiled=True),
        lax.psum_scatter(grad_key, ("seq", "tm"), scatter_dimension=0, tiled=True),
        lax.psum_scatter(grad_value, ("seq", "tm"), scatter_dimension=0, tiled=True),
        lax.psum_scatter(grad_router, ("seq", "tm"), scatter_dimension=0, tiled=True),
        lax.psum_scatter(grad_up, ("seq", "tm"), scatter_dimension=0, tiled=True),
    )
    col_gains, col_output, col_down = (
        lax.psum_scatter(grad_gains, ("seq", "tm"), scatter_dimension=1, tiled=True),
        lax.psum_scatter(grad_output, ("seq", "tm"), scatter_dimension=1, tiled=True),
        lax.psum_scatter(grad_down, ("seq", "tm"), scatter_dimension=1, tiled=True),
    )
    return (
        output_block,
        input_cot[None],
        col_gains,
        row_query,
        row_key,
        row_value,
        row_router,
        col_output,
        row_up,
        col_down,
    )


VMEM_LIMIT = 64 << 20

MESH_ID = pl.DeviceIdType.MESH
TILE = 128
PIECES = [(4, 2)] + [(7, 2)] * 10 + [(6, 2), (3, 1)]
NS = len(PIECES)
TILES = sum(a + b for a, b in PIECES)
FLAT = TILES * TILE
MOST_FIRST = max(a for a, _ in PIECES) * TILE
MOST_LAST = max(b for _, b in PIECES) * TILE
MOST = max(a + b for a, b in PIECES) * TILE
N1 = 6
NR = 4
NZ = 6
NZ1 = 7
HALF = (slice(0, 16), slice(16, 32))


POINTS = ([("d0", 4), ("u0", 8), ("j1", 16)] + [(f"j{j}", 8 * j) for j in range(2, 8)] + [("dw7", 64), ("ln2b", 64)]
          + [(f"tho{e}", 64) for e in range(E)] + [("sb0", 64), ("sb1", 64), ("dwo0", 70), ("dwo1", 76), ("dwo2", 82)]
          + [(f"tv{e}", 82) for e in range(E)] + [("ln1b", 82), ("dwp0", 90), ("dwp1", 98), ("dwp2", 108)])
ROUNDS = ["j2", "j4", "j7", "tho1", "sb1", "dwo2", "tv2", "ln1b", "dwp1"]


def plan():
    ends = [sum(a + b for a, b in PIECES[:p + 1]) for p in range(NS)]
    begun, t, todo = 0, 1, {}
    for name, ready in POINTS:
        ops = todo[name] = []
        for again in range(1 + ROUNDS.count(name)):
            if again:
                assert begun >= t
                ops.append(("round", t))
                t += 1
            while begun < NS and ends[begun] <= ready and (begun <= t or begun < 3):
                ops.append(("begin", begun))
                begun += 1
    rest = []
    while t < NS + 5:
        rest.append(("round", t))
        t += 1
        while begun < NS and begun <= t:
            rest.append(("begin", begun))
            begun += 1
    todo["rest"] = rest
    return todo


PLAN = plan()


class Piece:
    def __init__(self, p):
        start = sum(a + b for a, b in PIECES[:p]) * TILE
        self.p, self.f, self.r, self.q, self.g = p, p % N1, p % NR, p % NZ, p % NZ1
        self.wf, self.wl = (v * TILE for v in PIECES[p])
        self.first = slice(start, start + self.wf)
        self.last = slice(start + self.wf, start + self.wf + self.wl)
        self.all = slice(start, start + self.wf + self.wl)


def place():
    s = lax.axis_index("seq")
    t = lax.axis_index("tm")
    return s, t, t // 4, (t // 2) % 2, t % 2


def rem(a, n):
    return a % n if isinstance(a, int) else lax.rem(a, n)


def store_tile(parts, tile, value):
    at = tile * TILE
    width = value.shape[1]
    cols = slice(at, at + width) if isinstance(at, int) else pl.ds(pl.multiple_of(at, TILE), width)
    parts[:, :, :, :, cols] = value.reshape(2, 4, 2, 32, width).astype(jnp.bfloat16)


class Exchange:
    def __init__(self, parts, bufs, sems, stage, out_sem, out):
        self.parts, self.out = parts, out
        self.stage, self.out_sem = stage, out_sem
        (self.xa, self.yb, self.ya, self.xb, self.zu, self.zd, self.zuc, self.zdc, self.xc, self.yc) = bufs
        self.ssem, self.rsem = sems
        self.s, self.t, self.z, self.y, self.c = place()
        s, t = self.s, self.t
        self.to_x = {"seq": 1 - s, "tm": t}
        self.to_y = {"seq": s, "tm": t + 2 - 4 * self.y}
        self.to_up = {"seq": s, "tm": t + 4}
        self.to_down = {"seq": s, "tm": t - 4}

    def copy(self, kind, g, src, dst, dev):
        return pltpu.make_async_remote_copy(
            src_ref=src, dst_ref=dst, send_sem=self.ssem.at[kind, g.p],
            recv_sem=self.rsem.at[kind, g.p], device_id=dev, device_id_type=MESH_ID)

    def c_xa(self, g):
        return self.copy(0, g, self.parts.at[1 - self.s, :, :, HALF[0], g.first], self.xa.at[g.f, :, :, :, :g.wf], self.to_x)

    def c_yb(self, g):
        return self.copy(1, g, self.parts.at[:, :, 1 - self.y, HALF[1], g.first], self.yb.at[g.f, :, :, :, :g.wf], self.to_y)

    def c_ya(self, g):
        return self.copy(2, g, self.parts.at[self.s, :, 1 - self.y, HALF[0], g.first], self.ya.at[g.r, :, :, :g.wf], self.to_y)

    def c_xb(self, g):
        return self.copy(3, g, self.parts.at[1 - self.s, :, self.y, HALF[1], g.first], self.xb.at[g.r, :, :, :g.wf], self.to_x)

    def c_xc(self, g):
        return self.copy(4, g, self.parts.at[1 - self.s, self.z, :, :, g.last], self.xc.at[g.r, :, :, :g.wl], self.to_x)

    def c_yc(self, g):
        return self.copy(5, g, self.parts.at[self.s, self.z, 1 - self.y, :, g.last], self.yc.at[g.r, :, :g.wl], self.to_y)

    def c_up(self, g, z):
        return self.copy(6, g, self.parts.at[self.s, z + 1:4, self.y, :, g.first], self.zu.at[g.q, z:3, :, :g.wf], self.to_up)

    def c_down(self, g, z):
        return self.copy(7, g, self.parts.at[self.s, 0:z, self.y, :, g.first], self.zd.at[g.q, 0:z, :, :g.wf], self.to_down)

    def c_upc(self, g, z):
        return self.copy(8, g, self.parts.at[:, z + 1:4, :, :, g.last], self.zuc.at[g.g, :, z:3, :, :, :g.wl], self.to_up)

    def c_downc(self, g, z):
        return self.copy(9, g, self.parts.at[:, 0:z, :, :, g.last], self.zdc.at[g.g, :, 0:z, :, :, :g.wl], self.to_down)

    def add(self, at, cols, value):
        self.parts[(*at, cols)] = self.parts[(*at, cols)] + value

    def z_step(self, g, k, is_c):
        if is_c and not g.wl:
            return
        up, down = (self.c_upc, self.c_downc) if is_c else (self.c_up, self.c_down)
        rows = slice(None)

        def add(u, src, at):
            if is_c:
                def body(i, _):
                    a, b = i // 2, i % 2
                    self.add((a, u, b, rows), g.last, src[g.g, a, at, b, :, :g.wl])
                    return 0
                lax.fori_loop(0, 4, body, 0)
            else:
                self.add((self.s, u, self.y, rows), g.first, src[g.q, at, :, :g.wf])

        @pl.when(self.z == k - 1)
        def _():
            z = k - 1
            if z > 0:
                up(g, z - 1).wait_recv()
                for u in range(z + 1, 4):
                    add(u, self.zuc if is_c else self.zu, u - 1)
            if z < 3:
                up(g, z).start()

        @pl.when(self.z == 4 - k)
        def _():
            z = 4 - k
            if z < 3:
                down(g, z + 1).wait_recv()
                for u in range(0, z):
                    add(u, self.zdc if is_c else self.zd, u)
            if z > 0:
                down(g, z).start()

    def step1(self, g):
        self.c_xa(g).start()
        self.c_yb(g).start()
        self.z_step(g, 1, True)

    def step2(self, g):
        self.c_xa(g).wait_recv()

        def body(i, _):
            a, b = i // 2, i % 2
            self.add((self.s, a, b, HALF[0]), g.first, self.xa[g.f, a, b, :, :g.wf])
            return 0
        lax.fori_loop(0, 8, body, 0)
        self.c_ya(g).start()
        self.c_yb(g).wait_recv()

        def body(i, _):
            a, b = i // 4, i % 4
            self.add((a, b, self.y, HALF[1]), g.first, self.yb[g.f, a, b, :, :g.wf])
            return 0
        lax.fori_loop(0, 8, body, 0)
        self.c_xb(g).start()
        self.z_step(g, 2, True)

    def step3(self, g):
        self.c_ya(g).wait_recv()
        self.c_xb(g).wait_recv()

        def body(b, _):
            self.add((self.s, b, self.y, HALF[0]), g.first, self.ya[g.r, b, :, :g.wf])
            self.add((self.s, b, self.y, HALF[1]), g.first, self.xb[g.r, b, :, :g.wf])
            return 0
        lax.fori_loop(0, 4, body, 0)
        self.z_step(g, 1, False)
        self.z_step(g, 3, True)

    def step4(self, g):
        self.z_step(g, 2, False)
        if not g.wl:
            return
        self.z_step(g, 4, True)
        z = self.z
        rows = slice(None)

        @pl.when(z > 0)
        def _():
            def body(i, _):
                a, b = i // 2, i % 2
                self.add((a, z, b, rows), g.last, self.zuc[g.g, a, z - 1, b, :, :g.wl])
                return 0
            lax.fori_loop(0, 4, body, 0)

        @pl.when(z < 3)
        def _():
            def body(i, _):
                a, b = i // 2, i % 2
                self.add((a, z, b, rows), g.last, self.zdc[g.g, a, z, b, :, :g.wl])
                return 0
            lax.fori_loop(0, 4, body, 0)
        self.c_xc(g).start()

    def step5(self, g):
        self.z_step(g, 3, False)
        if not g.wl:
            return
        self.c_xc(g).wait_recv()
        for b in range(2):
            self.add((self.s, self.z, b, slice(None)), g.last, self.xc[g.r, b, :, :g.wl])
        self.c_yc(g).start()

    def step6(self, g):
        self.z_step(g, 4, False)
        z = self.z
        k = g.p % 2
        if g.p >= 2:
            self.c_out(Piece(g.p - 2)).wait()
        mine = self.parts[self.s, z, self.y, :, g.first].astype(jnp.float32)

        @pl.when(z == 0)
        def _():
            self.stage[k, :, :g.wf] = mine + self.zd[g.q, 0, :, :g.wf].astype(jnp.float32)

        @pl.when(z == 3)
        def _():
            self.stage[k, :, :g.wf] = mine + self.zu[g.q, 2, :, :g.wf].astype(jnp.float32)

        @pl.when((z > 0) & (z < 3))
        def _():
            self.stage[k, :, :g.wf] = ((mine + self.zu[g.q, z - 1, :, :g.wf].astype(jnp.float32))
                                       + self.zd[g.q, z, :, :g.wf].astype(jnp.float32))
        if g.wl:
            self.c_yc(g).wait_recv()
            self.stage[k, :, g.wf:g.wf + g.wl] = (self.parts[self.s, z, self.y, :, g.last].astype(jnp.float32)
                                                  + self.yc[g.r, :, :g.wl].astype(jnp.float32))
        self.c_out(g).start()

    def c_out(self, g):
        k = g.p % 2
        return pltpu.make_async_copy(self.stage.at[k, :, :g.wf + g.wl], self.out.at[:, g.all], self.out_sem.at[k])

    def tick(self, t):
        steps = (self.step2, self.step3, self.step4, self.step5, self.step6)
        for k, step in enumerate(steps):
            if 0 <= t - 1 - k < NS:
                step(Piece(t - 1 - k))

    def serve(self, point):
        for what, n in PLAN[point]:
            self.tick(n) if what == "round" else self.step1(Piece(n))

    def finish(self):
        self.c_out(Piece(NS - 2)).wait()
        self.c_out(Piece(NS - 1)).wait()
        for p in range(NS):
            g = Piece(p)
            self.c_xa(g).wait_send()
            self.c_yb(g).wait_send()
            self.c_ya(g).wait_send()
            self.c_xb(g).wait_send()
            if g.wl:
                self.c_xc(g).wait_send()
                self.c_yc(g).wait_send()
        for z in range(4):
            @pl.when(self.z == z)
            def _(z=z):
                for p in range(NS):
                    g = Piece(p)
                    if z < 3:
                        self.c_up(g, z).wait_send()
                        if g.wl:
                            self.c_upc(g, z).wait_send()
                    if z > 0:
                        self.c_down(g, z).wait_send()
                        if g.wl:
                            self.c_downc(g, z).wait_send()


P_SCRATCH = [pltpu.VMEM((2, 4, 2, 32, FLAT), jnp.bfloat16)]
RECV_SCRATCH = [
    pltpu.VMEM((N1, 4, 2, 16, MOST_FIRST), jnp.bfloat16),
    pltpu.VMEM((N1, 2, 4, 16, MOST_FIRST), jnp.bfloat16),
    pltpu.VMEM((NR, 4, 16, MOST_FIRST), jnp.bfloat16),
    pltpu.VMEM((NR, 4, 16, MOST_FIRST), jnp.bfloat16),
    pltpu.VMEM((NZ, 3, 32, MOST_FIRST), jnp.bfloat16),
    pltpu.VMEM((NZ, 3, 32, MOST_FIRST), jnp.bfloat16),
    pltpu.VMEM((NZ1, 2, 3, 2, 32, MOST_LAST), jnp.bfloat16),
    pltpu.VMEM((NZ1, 2, 3, 2, 32, MOST_LAST), jnp.bfloat16),
    pltpu.VMEM((NR, 2, 32, MOST_LAST), jnp.bfloat16),
    pltpu.VMEM((NR, 32, MOST_LAST), jnp.bfloat16),
]

def greet():
    s, t, z, y, c = place()
    bar = pltpu.get_barrier_semaphore()

    def tell(dev):
        pl.semaphore_signal(bar, inc=1, device_id=dev, device_id_type=MESH_ID)
    tell({"seq": 1 - s, "tm": t})
    tell({"seq": s, "tm": t + 2 - 4 * y})
    tell({"seq": s, "tm": t + 1 - 2 * c})

    @pl.when(z < 3)
    def _():
        tell({"seq": s, "tm": t + 4})

    @pl.when(z > 0)
    def _():
        tell({"seq": s, "tm": t - 4})
    far = jnp.where(c == 1, t + 1, t - 1)
    has_far = (far >= 0) & (far < 16)

    @pl.when(has_far)
    def _():
        tell({"seq": s, "tm": far})
    return bar, 3 + jnp.where(has_far, 1, 0) + jnp.where(z < 3, 1, 0) + jnp.where(z > 0, 1, 0)


D = 1024
FF = 4096
SEG = 256
HD = H * DH
HH = HD // 2
WIDE = H * E * DH
FFB = 512
NFF = FF // FFB
NG = 4
LOGIT = 64
OWN_SIB = 24
F32 = jnp.float32
BF = jnp.bfloat16


def dot(a, b):
    return jnp.dot(a, b, preferred_element_type=F32)


def dot_nt(a, b):
    return lax.dot_general(a, b, (((1,), (1,)), ((), ())), preferred_element_type=F32)


def dot_tn(a, b):
    return lax.dot_general(a, b, (((0,), (0,)), ((), ())), preferred_element_type=F32)


def halves(v):
    top = v.astype(BF)
    return top, (v - top.astype(F32)).astype(BF)


def unit_rows(v):
    centre = v - jnp.mean(v, axis=-1, keepdims=True)
    spread = jnp.mean(centre * centre, axis=-1, keepdims=True)
    inv = lax.rsqrt(spread + epsilon)
    return centre * inv, inv


def norm_back(unit, inv, cot):
    return inv * (cot - jnp.mean(cot, axis=-1, keepdims=True)
                  - unit * jnp.mean(cot * unit, axis=-1, keepdims=True))


def normal_cdf(v, bell):
    u = 1.0 / (1.0 + 0.23164189 * jnp.abs(v))
    poly = ((((0.5307027145 * u - 0.7265760135) * u + 0.7107068705) * u - 0.142248368) * u + 0.127414796) * u
    tail = poly * bell
    return jnp.where(v < 0.0, tail, 1.0 - tail)


def for_rows(step, body):
    def inner(i, _):
        body(pl.ds(pl.multiple_of(i * step, step), step))
        return 0
    lax.fori_loop(0, SEG // step, inner, 0)


def side_by_side(blocks):
    return jnp.concatenate(blocks, axis=1)


NAMES = (
    "x", "oc", "gains", "rt", "rf", "spread", "hot", "wq", "wk", "wr", "wrp", "wu", "wd", "exv", "exo",
    "xn", "hn", "mid", "lo", "nsc", "q", "k", "v", "sig", "att", "acc", "g_o", "g_p",
    "act", "uc", "bc", "kc", "vc", "kn", "vn", "ob", "gg", "ogc", "qc", "vg", "ac", "acc2", "up",
    "at", "full",
    "ld", "ld2", "lde", "kv_s", "kv_r", "sib_s", "sib_r", "st", "stage", "out_sem", "ssem", "rsem",
)


def layer_scratch():
    dma = pltpu.SemaphoreType.DMA
    v = pltpu.VMEM
    return [
        v((SEG, D), BF), v((SEG, D), BF), v((2, D), BF), v((2 * H, 2, SEG), jnp.int32), v((128, SEG), BF),
        v((128, 256), BF), v((SEG, 128), F32),
        v((HD, D), BF), v((HD, D), BF), v((2 * H * E, D), BF), v((128, D), BF),
        v((2, D, FFB), BF), v((2, FFB, D), BF), v((2, E, 256, HH), BF), v((2, E, 256, HH), BF),
        v((SEG, D), BF), v((SEG, D), BF), v((SEG, D), F32), v((SEG, D), F32), v((SEG, D), F32),
        v((2, SEG, HH), BF), v((2, 2 * SEG, HH), BF), v((2, 2 * SEG, HH), BF), v((SEG, 128), F32),
        v((2, SEG, HH), BF), v((2, 2 * SEG, HH), F32), v((2 * SEG, 2304), BF), v((2 * SEG, 3328), BF),
        v((NG, 2 * SEG, FFB), BF), v((NG, 2 * SEG, FFB), BF), v((SEG, D), BF),
        v((2, 2 * SEG, HH), BF), v((2, 2 * SEG, HH), BF), v((2, SEG, HH), BF), v((2, SEG, HH), BF), v((SEG, D), BF), v((SEG, 256), BF),
        v((SEG, 128), F32), v((2, SEG, HH), F32), v((2, SEG, 128), F32),
        v((2, SEG, HH), BF), v((2, 2 * SEG, HH), F32), v((SEG, FFB), F32),
        v((6, 16, 32, 2 * SEG), BF), v((2, 16, 2, 32, SEG), BF),
        dma((16,)), dma((4,)), dma((2, 2 * E)), dma((5,)), dma((5,)), dma((OWN_SIB,)), dma((OWN_SIB,)), dma((2,)),
        v((2, 32, MOST), F32), dma((2,)), dma((10, NS)), dma((10, NS)),
    ]


def layer_kernel(x_h, rt_h, len_s, gains_h, wq_h, wk_h, wv_h, wr_h, wo_h, wu_h, wd_h, oc_h,
                 spread_h, lo_h, ig_h, flat_h, *scratch):
    m = types.SimpleNamespace(**dict(zip(NAMES, scratch[:len(NAMES)])))
    recv = scratch[len(NAMES):]
    s, t, z, y, c = place()
    last_t = lax.axis_size("tm") - 1
    sib = {"seq": s, "tm": t + 1 - 2 * c}
    scale = DH ** -0.5
    own = slice(SEG, 2 * SEG)
    mem = slice(0, SEG)

    bar, peers = greet()

    def load(i, src, dst):
        cp = pltpu.make_async_copy(src, dst, m.ld.at[i])
        cp.start()
        return cp

    def sibling(i, src, dst):
        return pltpu.make_async_remote_copy(
            src_ref=src, dst_ref=dst, send_sem=m.sib_s.at[i], recv_sem=m.sib_r.at[i],
            device_id=sib, device_id_type=MESH_ID)

    def at_copy(i, slot):
        return sibling(i, m.full.at[slot, :, 1 - c], m.at.at[i, :, :, SEG:])

    def turn(i, slot, value):
        m.full[slot] = jnp.transpose(value).reshape(16, 2, 32, SEG)
        m.at[i, :, :, :SEG] = m.full[slot, :, c]
        at_copy(i, slot).start()

    def go_copy():
        return sibling(6, m.g_o.at[mem], m.g_o.at[own])

    def gp_copy():
        return sibling(7, m.g_p.at[mem], m.g_p.at[own])

    def ff_copies(j):
        return act_copy(j), uc_copy(j)

    def act_copy(j):
        g = rem(j, NG)
        return sibling(8 + 2 * j, m.act.at[g, mem], m.act.at[g, own])

    def uc_copy(j):
        g = rem(j, NG)
        return sibling(9 + 2 * j, m.uc.at[g, mem], m.uc.at[g, own])

    def ff_loads(j):
        return wu_load(j), wd_load(j)

    def wu_load(j):
        cols = pl.ds(pl.multiple_of(j * FFB, FFB), FFB)
        return pltpu.make_async_copy(wu_h.at[:, cols], m.wu.at[rem(j, 2)], m.ld2.at[rem(j, 2)])

    def wd_load(j):
        rows = pl.ds(pl.multiple_of(j * FFB, FFB), FFB)
        return pltpu.make_async_copy(wd_h.at[rows, :], m.wd.at[rem(j, 2)], m.ld2.at[2 + rem(j, 2)])

    def along(i, src, dst, by):
        return pltpu.make_async_remote_copy(
            src_ref=src, dst_ref=dst, send_sem=m.kv_s.at[i], recv_sem=m.kv_r.at[i],
            device_id={"seq": s, "tm": t + by}, device_id_type=MESH_ID)

    def k_copy():
        return along(0, m.k.at[:, own], m.k.at[:, mem], 1)

    def v_copy(half):
        return along(1 + half, m.v.at[half, own], m.v.at[half, mem], 1)

    def kc_copy():
        return along(3, m.kc.at[:, mem], m.kn, -1)

    def vc_copy():
        return along(4, m.vc.at[:, mem], m.vn, -1)

    def half_rows(half):
        return slice(half * HH, (half + 1) * HH)

    def head_only(v, h):
        lane = lax.broadcasted_iota(jnp.int32, v.shape, 1)
        lo = rem(h, 2) * DH
        return jnp.where((lane >= lo) & (lane < lo + DH), v, jnp.zeros_like(v))

    def gates_wide(table, half, e):
        return dot(m.gg[...], table[half, e])

    def make_table(table, first):
        row = lax.broadcasted_iota(jnp.int32, (256, HH), 0)
        lane = lax.broadcasted_iota(jnp.int32, (256, HH), 1)
        row = jnp.where(row >= 128, row - 128, row) - first - jnp.where(lane >= DH, E, 0)
        for half in range(2):
            for e in range(E):
                table[half, e] = jnp.where(row == 2 * E * half + e, 1.0, 0.0).astype(BF)

    def expert_loads(which, n, e, src, dst):
        return [pltpu.make_async_copy(src.at[pl.ds((h * E + e) * DH, DH)], dst.at[pl.ds(h * DH, DH)], m.lde.at[which, n])
                for h in range(H)]

    def ring(n):
        return expert_loads(0, n, n % E, wo_h if n < E else wv_h, m.wd.at[n % 2])

    def weights_of(h):
        half = h // 2
        scores = dot_nt(head_only(m.q[half], h), m.k[half]) * scale
        length = len_s[0, 0]
        row = lax.broadcasted_iota(jnp.int32, (SEG, 2 * SEG), 0)
        col = lax.broadcasted_iota(jnp.int32, (SEG, 2 * SEG), 1)
        allowed = ((col < SEG) & (col >= SEG - length)) | ((col >= SEG) & (col - SEG <= row))
        scores = jnp.where(allowed, scores, -1e30)
        e = jnp.exp(scores - jnp.max(scores, axis=-1, keepdims=True))
        return e / jnp.sum(e, axis=-1, keepdims=True)

    l_x = load(0, x_h, m.x)
    l_g = load(1, gains_h, m.gains)
    l_k = load(2, wk_h, m.wk)
    l_r = load(3, wr_h, m.wr)
    l_rt = load(4, rt_h, m.rt)
    l_sp = load(12, spread_h, m.spread)

    def forward(wv, wo, wide):
        l_v = [expert_loads(0, e, e, wv_h, wv.at[e]) for e in range(E)]
        for group in l_v:
            for cp in group:
                cp.start()
        make_table(m.exv, LOGIT)
        l_x.wait()
        l_g.wait()

        def norm1(rows):
            unit, _ = unit_rows(m.x[rows, :].astype(F32))
            m.xn[rows, :] = (unit * m.gains[0:1, :].astype(F32)).astype(BF)
        for_rows(64, norm1)
        l_k.wait()
        for half in range(2):
            m.k[half, own] = dot_nt(m.xn[...], m.wk[half_rows(half), :]).astype(BF)
        l_q = load(8, wq_h, m.wq)
        l_oc = load(9, oc_h, m.oc)
        pl.semaphore_wait(bar, peers)

        @pl.when(t < last_t)
        def _():
            k_copy().start()
        l_r.wait()
        m.wrp[...] = jnp.zeros((128, D), BF)
        m.wrp[LOGIT:LOGIT + 2 * H * E, :] = m.wr[...]
        sig = jax.nn.sigmoid(dot_nt(m.xn[...], m.wrp[...]))
        l_rt.wait()
        l_sp.wait()
        m.rf[...] = jnp.zeros((128, SEG), BF)
        for i in range(2):
            m.rf[16 * i:16 * i + 2 * H, :] = m.rt[:, i, :].astype(F32).astype(BF)
        named = dot_tn(m.rf[...], m.spread[...])
        expert = m.spread[127:128, :128].astype(F32)
        hit = (named[:, :128] == expert) | (named[:, 128:] == expert)
        m.hot[...] = jnp.where(hit, 1.0, 0.0)
        m.sig[...] = sig
        top, low = halves(sig * m.hot[...])
        m.gg[:, :128] = top
        m.gg[:, 128:] = low
        for half in range(2):
            total = jnp.zeros((SEG, HH), F32)
            for e in range(E):
                if half == 0:
                    for cp in l_v[e]:
                        cp.wait()
                total = total + dot_nt(m.xn[...], wv[e, half_rows(half)]) * gates_wide(m.exv, half, e)
            m.v[half, own] = total.astype(BF)
            if half == 0:
                l_wo = [expert_loads(1, e, e, wo_h, wo.at[pl.ds(e * HD, HD)]) for e in range(E)]
                for group in l_wo:
                    for cp in group:
                        cp.start()
                for j in range(2):
                    for cp in ff_loads(j):
                        cp.start()

            @pl.when(t < last_t)
            def _():
                v_copy(half).start()
        l_q.wait()
        for half in range(2):
            m.q[half] = dot_nt(m.xn[...], m.wq[half_rows(half), :]).astype(BF)
        l_oc.wait()
        turn(0, 0, m.oc[...])
        turn(3, 1, m.xn[...])
        make_table(m.exo, LOGIT + H * E)

        @pl.when(t > 0)
        def _():
            k_copy().wait_recv()

        @pl.when(t == 0)
        def _():
            m.k[:, mem] = jnp.zeros((2, SEG, HH), BF)
            m.v[:, mem] = jnp.zeros((2, SEG, HH), BF)
        for h in range(H):
            m.act[h, mem] = weights_of(h).astype(BF)
        for half in range(2):
            for e in range(E):
                wide[half, e] = gates_wide(m.exo, half, e)
        for cp in ff_loads(0):
            cp.wait()
        m.up[...] = dot_nt(m.oc[...], m.wd[0])
        m.g_o[mem, 2176:2304] = jnp.zeros((SEG, 128), BF)
        for half in range(2):
            @pl.when(t > 0)
            def _():
                v_copy(half).wait_recv()
            total = jnp.zeros((SEG, HH), F32)
            for h in (2 * half, 2 * half + 1):
                total = total + dot(m.act[h, mem], head_only(m.v[half], h))
            m.att[half] = total.astype(BF)
        att = [m.att[half].astype(F32) for half in range(2)]
        for e in range(0, E, 2):
            blocks = [(wide[half, i] * att[half]).astype(BF) for i in range(e, min(e + 2, E)) for half in range(2)]
            m.g_o[mem, e * HD:min(e + 2, E) * HD] = side_by_side(blocks)
        go_copy().start()
        for group in l_wo:
            for cp in group:
                cp.wait()
        m.mid[...] = m.x[...].astype(F32) + dot(m.g_o[mem, :WIDE], wo[...])

        def norm2(rows):
            unit, _ = unit_rows(m.mid[rows, :])
            m.hn[rows, :] = (unit * m.gains[1:2, :].astype(F32)).astype(BF)
        for_rows(64, norm2)
        at_copy(0, 0).wait_send()
        turn(1, 0, m.hn[...])

    pl.run_scoped(forward, pltpu.VMEM((E, HD, D), BF), pltpu.VMEM((WIDE, D), BF), pltpu.VMEM((2, E, SEG, HH), F32))

    def backward(parts):
        ex = Exchange(parts, recv, (m.ssem, m.rsem), m.stage, m.out_sem, flat_h)

        def product(i, g):
            return dot(m.at[i].reshape(512, 2 * SEG), g)

        def tiles(i, g, tile):
            store_tile(parts, tile, product(i, g))

        m.lo[...] = m.mid[...]
        m.nsc[...] = jnp.zeros((SEG, D), F32)
        at_copy(0, 0).wait_recv()
        at_copy(1, 0).wait_recv()

        def block(j, _):
            b = rem(j, 2)
            g = rem(j, NG)

            @pl.when(j > 0)
            def _():
                wu_load(j).wait()

            @pl.when(j >= NG)
            def _():
                for cp in ff_copies(j - NG):
                    cp.wait_send()
            pre = dot(m.hn[...], m.wu[b])
            bell = jnp.exp(-0.5 * pre * pre)
            cdf = normal_cdf(pre, bell)
            m.act[g, mem] = (pre * cdf).astype(BF)
            act_copy(j).start()
            pdf = bell * 0.3989422804014327
            m.uc[g, mem] = (m.up[...] * (cdf + pre * pdf)).astype(BF)
            uc_copy(j).start()

            @pl.when(j > 2)
            def _():
                act_grad(j - 1)
                up_grad(j - 1)
            m.lo[...] += dot(m.act[g, mem], m.wd[b])
            m.nsc[...] += dot_nt(m.uc[g, mem], m.wu[b])

            @pl.when(j + 2 < NFF)
            def _():
                for cp in ff_loads(j + 2):
                    cp.start()

            @pl.when(j == 0)
            def _():
                act_grad(0)
                ex.serve("d0")
                up_grad(0)
                ex.serve("u0")

            @pl.when(j + 1 < NFF)
            def _():
                wd_load(j + 1).wait()
                m.up[...] = dot_nt(m.oc[...], m.wd[rem(j + 1, 2)])

            @pl.when(j == 1)
            def _():
                act_grad(1)
                up_grad(1)
            for i in range(1, NFF):
                if PLAN[f"j{i}"]:
                    pl.when(j == i)(lambda i=i: ex.serve(f"j{i}"))
            return 0

        def act_grad(j):
            act_copy(j).wait_recv()
            tiles(0, m.act[rem(j, NG)], 8 * j)

        def up_grad(j):
            uc_copy(j).wait_recv()
            tiles(1, m.uc[rem(j, NG)], 8 * j + 4)
        lax.fori_loop(0, NFF, block, 0)
        for n in range(2):
            for cp in ring(n):
                cp.start()
        act_grad(NFF - 1)
        up_grad(NFF - 1)
        ex.serve("dw7")
        for j in range(NFF - NG, NFF):
            for cp in ff_copies(j):
                cp.wait_send()
        m.ob[...] = m.lo[...].astype(BF)
        l_lo = pltpu.make_async_copy(m.ob, lo_h, m.st.at[0])
        l_lo.start()

        def norm2_back(rows):
            unit, inv = unit_rows(m.mid[rows, :])
            cot = m.nsc[rows, :]
            mcot = m.oc[rows, :].astype(F32) + norm_back(unit, inv, cot * m.gains[1:2, :].astype(F32))
            m.lo[rows, :] = mcot
            m.bc[rows, :] = mcot.astype(BF)
            m.hn[rows, :] = (cot * unit).astype(BF)
        for_rows(32, norm2_back)
        at_copy(3, 1).wait_send()
        turn(2, 1, m.bc[...])
        at_copy(1, 0).wait_send()
        turn(5, 0, m.hn[...])
        ex.serve("ln2b")

        def ring_next(n):
            if n + 2 < 2 * E:
                for cp in ring(n + 2):
                    cp.start()

        att = [m.att[half].astype(F32) for half in range(2)]
        seen = jnp.zeros((SEG, 128), F32)
        total = [jnp.zeros((SEG, HH), F32)] * 2
        for e in range(E):
            for cp in ring(e):
                cp.wait()
            cots = [dot_nt(m.bc[...], m.wd[e % 2, half_rows(half)]) for half in range(2)]
            ring_next(e)
            for half, cot in enumerate(cots):
                seen = seen + dot_nt((cot * att[half]).astype(BF), m.exo[half, e, :128])
                total[half] = total[half] + cot * gates_wide(m.exo, half, e)
            ex.serve(f"tho{e}")
        m.ogc[...] = seen
        for half in range(2):
            m.ac[half] = total[half].astype(BF)

        m.acc[...] = jnp.zeros((2, 2 * SEG, HH), F32)
        m.acc2[...] = jnp.zeros((2, 2 * SEG, HH), F32)
        m.qc[...] = jnp.zeros((2, SEG, HH), F32)

        def scores_back(h):
            half = h // 2
            probs = weights_of(h)
            cot = head_only(m.ac[half], h)
            m.acc2[half] += dot_tn(probs.astype(BF), cot)
            pc = dot_nt(cot, m.v[half])
            sc = (probs * (pc - jnp.sum(probs * pc, axis=-1, keepdims=True))).astype(BF)
            m.qc[half] += dot(sc, head_only(m.k[half], h)) * scale
            m.acc[half] += dot_tn(sc, head_only(m.q[half], h)) * scale
        for i in range(2):
            scores_back(2 * i)
            scores_back(2 * i + 1)
            ex.serve(f"sb{i}")
        m.vc[...] = m.acc2[...].astype(BF)
        m.kc[...] = m.acc[...].astype(BF)

        @pl.when(t > 0)
        def _():
            vc_copy().start()
            kc_copy().start()
        go_copy().wait_recv()
        at_copy(2, 1).wait_recv()

        for i in range(3):
            tiles(2, m.g_o[:, 6 * TILE * i:6 * TILE * (i + 1)], 64 + 6 * i)
            ex.serve(f"dwo{i}")
        m.g_p[mem, HD:512] = jnp.zeros((SEG, 512 - HD), BF)
        m.g_p[mem, 512 + HD:1024] = jnp.zeros((SEG, 512 - HD), BF)
        m.g_p[mem, :HD] = side_by_side([m.qc[half].astype(BF) for half in range(2)])

        @pl.when(t < last_t)
        def _():
            vc_copy().wait_recv()
            kc_copy().wait_recv()

        @pl.when(t == last_t)
        def _():
            m.kn[...] = jnp.zeros((2, SEG, HH), BF)
            m.vn[...] = jnp.zeros((2, SEG, HH), BF)
        m.g_p[mem, 512:512 + HD] = side_by_side(
            [(m.kc[half, own].astype(F32) + m.kn[half].astype(F32)).astype(BF) for half in range(2)])
        l_lo.wait()

        own_cot, next_cot = m.mid, m.nsc

        own_cot[...] = (dot(m.g_p[mem, :HD], m.wq[...])
                        + sum(dot(m.kc[half, own], m.wk[half_rows(half), :]) for half in range(2)))
        next_cot[...] = sum(dot(m.kn[half], m.wk[half_rows(half), :]) for half in range(2))
        m.vg[...] = jnp.zeros((2, SEG, 128), F32)
        blocks = []
        for e in range(E):
            for cp in ring(E + e):
                cp.wait()
            wv = m.wd.at[(E + e) % 2]
            pairs = []
            for half in range(2):
                proj = dot_nt(m.xn[...], wv[half_rows(half)])
                gate = gates_wide(m.exv, half, e)
                pair = []
                for i, v in enumerate((m.vc[half, own], m.vn[half])):
                    v = v.astype(F32)
                    m.vg[i] += dot_nt((v * proj).astype(BF), m.exv[half, e, :128])
                    pair.append((gate * v).astype(BF))
                blocks.append((pair[0].astype(F32) + pair[1].astype(F32)).astype(BF))
                pairs.append(pair)
            for i, acc in enumerate((own_cot, next_cot)):
                acc[...] += dot(side_by_side([pair[i] for pair in pairs]), wv[:HD])
            ring_next(E + e)
            ex.serve(f"tv{e}")
            if e % 2 == 1 or e == E - 1:
                first = e - 1 if e % 2 == 1 else e
                m.g_p[mem, 1024 + first * HD:1024 + (e + 1) * HD] = side_by_side(blocks[2 * first:])
        slope = m.sig[...] * (1.0 - m.sig[...]) * m.hot[...]
        lo_cot = ((m.vg[0] + m.ogc[...]) * slope).astype(BF)
        ln_cot = (m.vg[1] * slope).astype(BF)
        own_cot[...] += dot(lo_cot, m.wrp[...])
        next_cot[...] += dot(ln_cot, m.wrp[...])
        both = (lo_cot.astype(F32) + ln_cot.astype(F32)).astype(BF)
        lane = lax.broadcasted_iota(jnp.int32, (SEG, 128), 1)
        m.g_p[mem, 3200:3328] = jnp.where(lane < LOGIT, m.g_p[mem, 3200:3328], both)
        gp_copy().start()

        def norm1_back(rows):
            unit, inv = unit_rows(m.x[rows, :].astype(F32))
            cot = own_cot[rows, :]
            m.lo[rows, :] += norm_back(unit, inv, cot * m.gains[0:1, :].astype(F32))
            m.hn[rows, :] = ((cot + next_cot[rows, :]) * unit).astype(BF)
        for_rows(32, norm1_back)
        l_ig = pltpu.make_async_copy(m.lo, ig_h, m.st.at[1])
        l_ig.start()
        at_copy(2, 1).wait_send()
        turn(4, 1, m.hn[...])
        ex.serve("ln1b")
        gp_copy().wait_recv()
        at_copy(3, 1).wait_recv()

        for i in range(6):
            tiles(3, m.g_p[:, 4 * TILE * i:4 * TILE * (i + 1)], 82 + 4 * i)
            if i in (1, 3):
                ex.serve(f"dwp{i // 2}")
        last = product(3, m.g_p[:, 3072:3328])
        store_tile(parts, 106, last[:, :TILE])
        last = last[:, TILE:]
        lane = lax.broadcasted_iota(jnp.int32, (2 * SEG, TILE), 1)
        at_copy(5, 0).wait_recv()
        at_copy(4, 1).wait_recv()
        for i, at in ((4, 104), (5, 105)):
            last += product(i, jnp.where(lane == at, 1.0, 0.0).astype(BF))
        store_tile(parts, 107, last)

        ex.serve("dwp2")
        ex.serve("rest")
        ex.finish()
        l_ig.wait()

    pl.run_scoped(backward, *P_SCRATCH)
    at_copy(5, 0).wait_send()
    at_copy(4, 1).wait_send()
    go_copy().wait_send()
    gp_copy().wait_send()

    @pl.when(t < last_t)
    def _():
        k_copy().wait_send()
        v_copy(0).wait_send()
        v_copy(1).wait_send()

    @pl.when(t > 0)
    def _():
        kc_copy().wait_send()
        vc_copy().wait_send()


def tables():
    lane = np.arange(128) - LOGIT
    inside = (lane >= 0) & (lane < 2 * H * E)
    pick = (np.arange(2 * H)[:, None] == lane[None, :] // E) & inside
    spread = np.zeros((128, 256), np.float32)
    spread[:2 * H, :128] = pick
    spread[16:16 + 2 * H, 128:] = pick
    spread[127, :128] = np.where(inside, lane % E, -1)
    return spread.astype(ml_dtypes.bfloat16)


def fused_device(layer_input, routes, memory_lengths, norm_gains, w_query, w_key, w_value,
                 w_router, w_output, w_up, w_down, output_cot):
    anywhere = pl.BlockSpec(memory_space=pl.ANY)
    specs = [anywhere] * 13
    specs[2] = pl.BlockSpec(memory_space=pltpu.SMEM)
    out, grad, flat = pl.pallas_call(
        layer_kernel,
        out_shape=(jax.ShapeDtypeStruct((SEG, D), BF), jax.ShapeDtypeStruct((SEG, D), F32),
                   jax.ShapeDtypeStruct((32, FLAT), F32)),
        in_specs=specs,
        out_specs=(anywhere,) * 3,
        scratch_shapes=layer_scratch() + RECV_SCRATCH,
        compiler_params=pltpu.CompilerParams(
            collective_id=0, has_side_effects=True, vmem_limit_bytes=VMEM_LIMIT),
        name="layer",
    )(layer_input[0], jnp.transpose(routes[0], (1, 2, 0)), memory_lengths, norm_gains, w_query.T, w_key.T, w_value.T, w_router.T,
      w_output, w_up, w_down, output_cot[0], tables())
    shapes = ((SEG, D), BF), ((SEG, D), F32), ((2, 32), F32), ((32, HD), F32), ((32, HD), F32), \
        ((32, WIDE), F32), ((32, 2 * H * E), F32), ((32, WIDE), F32), ((32, FF), F32), ((32, FF), F32)
    vm = pl.BlockSpec(memory_space=pltpu.VMEM)
    res = pl.pallas_call(
        split_kernel,
        out_shape=tuple(jax.ShapeDtypeStruct(*v) for v in shapes),
        in_specs=(anywhere, anywhere, anywhere),
        out_specs=(vm,) * 10,
        scratch_shapes=[pltpu.VMEM((32, FLAT), F32), pltpu.SemaphoreType.DMA((3,))],
        compiler_params=pltpu.CompilerParams(vmem_limit_bytes=VMEM_LIMIT),
        name="split",
    )(out, grad, flat)
    return (res[0][None], res[1][None], *res[2:7], res[7].T, res[8], res[9].T)


def split_kernel(out_h, grad_h, flat_h, lo, ig, gains, dq, dk, dv, dr, do, du, dd, flat, sem):
    copies = [pltpu.make_async_copy(flat_h, flat, sem.at[2]), pltpu.make_async_copy(out_h, lo, sem.at[0]),
              pltpu.make_async_copy(grad_h, ig, sem.at[1])]
    for cp in copies:
        cp.start()
    copies.pop(0).wait()
    for j in range(NFF):
        dd[:, j * FFB:(j + 1) * FFB] = flat[:, 2 * j * FFB:(2 * j + 1) * FFB]
        du[:, j * FFB:(j + 1) * FFB] = flat[:, (2 * j + 1) * FFB:(2 * j + 2) * FFB]
    base = 82 * TILE
    dq[...] = flat[:, base:base + HD]
    dk[...] = flat[:, base + 512:base + 512 + HD]
    for h in range(H):
        for e in range(E):
            to = slice((h * E + e) * DH, (h * E + e + 1) * DH)
            at = e * HD + h * DH
            do[:, to] = flat[:, 2 * FF + at:2 * FF + at + DH]
            dv[:, to] = flat[:, base + 1024 + at:base + 1024 + at + DH]
    tail = flat[:, 107 * TILE:108 * TILE]
    dr[...] = tail[:, LOGIT:LOGIT + 2 * H * E]
    gains[...] = jnp.transpose(tail)[104:106, :]
    for cp in copies:
        cp.wait()


def solution(mesh):
    placed = (
        P("seq", "tm", None),
        P("seq", "tm", None, None),
        P("seq", "tm"),
        P(),
        P(),
        P(),
        P(),
        P(),
        P(),
        P(),
        P(),
        P("seq", "tm", None),
    )
    fused = mesh.shape["seq"] == 2 and mesh.shape["tm"] == 16
    return jax.shard_map(
        fused_device if fused else per_device,
        mesh=mesh,
        in_specs=placed,
        out_specs=(
            P("seq", "tm", None),
            P("seq", "tm", None),
            P(None, ("seq", "tm")),
            P(("seq", "tm"), None),
            P(("seq", "tm"), None),
            P(("seq", "tm"), None),
            P(("seq", "tm"), None),
            P(None, ("seq", "tm")),
            P(("seq", "tm"), None),
            P(None, ("seq", "tm")),
        ),
        check_vma=False,
    )
```
